256 devices in a mesh: ty: 2 (over core), tx: 4 (over z_lo), pos: 32 (over y, z_hi, x).
Axes of the slice: x: 4, y: 4, z: 8 (z_hi: 2, z_lo: 4; z = z_hi * 4 + z_lo), core: 2. Of those that a mesh axis runs over, the one named last changes fastest.
Arguments:
- object_field: float32 [2, 2, 512, 1024], P(None, None, ('ty', 'pos'), 'tx'), may hold values from -6 to 6
- momentum: float32 [2, 2, 512, 1024], P(None, None, ('ty', 'pos'), 'tx'), may hold values from -12 to 12
- measured: float32 [2, 4, 32, 256, 256], P('ty', 'tx', 'pos'), may hold values from 0 to 2
- illumination: float32 [2, 256, 256], replicated, may hold values from -6 to 6
- slab_phase: float32 [256, 256], replicated, may hold values from -3.140625 to 3.140625
- offsets: int32 [2, 4, 32, 2], P('ty', 'tx'), may hold values from 0 to 128, as said below
- entry_counts: int32 [2, 4], P('ty', 'tx'), may hold values from 8 to 16, as said below
Outputs:
- new_object: float32 [2, 2, 512, 1024], P(None, None, ('ty', 'pos'), 'tx')
- new_momentum: float32 [2, 2, 512, 1024], P(None, None, ('ty', 'pos'), 'tx')
- amplitudes: float32 [2, 4, 32, 256, 256], P('ty', 'tx', 'pos')
The draws below stay inside these ranges and needn't reach their ends.
Inputs may be any that keep to these rules, and one draw needn't show every extreme that they name: offsets[a, b, k] is the corner of a window of 256 x 256 cells, counted from the corner of tile (a, b) widened by 64 cells on every side. Tile (a, b) uses the first entry_counts[a, b] slots of its list; some tile uses exactly 16 slots in every draw.
All inputs are finite; a program needn't handle non-finite values.
Results may differ from the reference program's by a relative error of at most 0.0003.
Values sent between devices are 32-bit elements; how exact they have to be, the bound alone decides.
A program may use at most 64 MiB of HBM per device.

```python
import math
import jax
import jax.numpy as jnp
from jax import lax

W = 256
TILE = 256
MARGIN = 64
LIST = 32
TROWS = 2
TCOLS = 4
NYO = 512
NXO = 1024


def draw_offsets(key, part):
    return jax.random.randint(key, (TROWS, TCOLS, LIST, 2), 0, TILE + 2 * MARGIN - W + 1, dtype=jnp.int32)


def draw_entry_counts(key, part):
    tiles = TROWS * TCOLS
    drawn = jax.random.randint(jax.random.fold_in(key, 11), (tiles,), max(1, LIST // 4), LIST // 2 + 1, dtype=jnp.int32)
    chosen = jax.random.randint(jax.random.fold_in(key, 12), (), 0, tiles, dtype=jnp.int32)
    flat_index = jnp.arange(tiles, dtype=jnp.int32)
    return jnp.where(flat_index == chosen, LIST // 2, drawn).reshape(TROWS, TCOLS).astype(jnp.int32)


def levels(own_key, extent, shards, smallest, largest):
    gain, own = 1.0, jax.random.fold_in(own_key, 6)
    for dim, shards_of in shards:
        steps = jnp.exp(jax.random.uniform(jax.random.fold_in(own, dim), (shards_of,), jnp.float32, smallest / len(shards), largest / len(shards)))
        gain = gain * jnp.repeat(steps, extent[dim] // shards_of).reshape([-1 if axis == dim else 1 for axis in range(len(extent))])
    return gain


def bell_draw(own_key, extent, spread, limit, pieces=(), held_as=jnp.bfloat16):
    factor_of = levels(own_key, extent, pieces, -0.22, 0.18) if pieces else 1.0
    values = jax.random.normal(own_key, extent, jnp.float32) * spread * factor_of
    return jnp.minimum(jnp.maximum(values, -limit), limit).astype(held_as)


def setup_inputs(seed: int = 0) -> dict:
    key_of = jax.random.split(jax.random.key(seed), 8)
    return {
        "object_field": bell_draw(key_of[0], (2, 2, NYO, NXO), 1.0, 6.0, ((2, 64), (3, 4)), jnp.float32),
        "momentum": bell_draw(key_of[1], (2, 2, NYO, NXO), 2.0, 12.0, ((2, 64), (3, 4)), jnp.float32),
        "measured": jnp.clip(2.0 * jax.random.uniform(key_of[2], (TROWS, TCOLS, LIST, W, W), jnp.float32) ** levels(key_of[2], (TROWS, TCOLS, LIST, W, W), ((0, 2), (1, 4), (2, 32)), -0.2, 0.2), 0.0, 2.0),
        "illumination": bell_draw(key_of[3], (2, W, W), 1.0, 6.0, (), jnp.float32),
        "slab_phase": jnp.clip(jax.random.uniform(key_of[4], (W, W), jnp.float32, -3.140625, 3.140625), -3.140625, 3.140625),
        "offsets": draw_offsets(jax.random.fold_in(key_of[7], 71), 0),
        "entry_counts": draw_entry_counts(jax.random.fold_in(key_of[7], 71), 0),
    }


HIGHEST = lax.Precision.HIGHEST
magnitude_floor = 0.5
momentum_rate = 0.9
step_length = 0.05

def tables(length):
    indices = jnp.arange(length, dtype=jnp.int32)
    product = indices[:, None] * indices[None, :] % length
    angles = product.astype(jnp.float32) * (2.0 * math.pi / length)
    factor = 1.0 / math.sqrt(length)
    return (jnp.cos(angles) * factor, jnp.sin(angles) * factor)

def matmul(left, right):
    return jnp.dot(left, right, precision=HIGHEST)

def transform(real_part, imag_part, cosine, sine_table, inverse):
    factor = 1.0 if inverse else -1.0
    right_real = matmul(real_part, cosine) - factor * matmul(imag_part, sine_table)
    right_imag = matmul(imag_part, cosine) + factor * matmul(real_part, sine_table)
    left_real = matmul(cosine, right_real) - factor * matmul(sine_table, right_imag)
    left_imag = matmul(cosine, right_imag) + factor * matmul(sine_table, right_real)
    return (left_real, left_imag)

def complex_product(first_real, first_imag, second_real, second_imag):
    return (first_real * second_real - first_imag * second_imag, first_real * second_imag + first_imag * second_real)

def forward_window(window, illumination, slab_real, slab_imag, cosine, sine_table):
    entering = complex_product(illumination[0], illumination[1], window[0], window[1])
    spectrum = transform(entering[0], entering[1], cosine, sine_table, False)
    spectrum = complex_product(spectrum[0], spectrum[1], slab_real, slab_imag)
    between = transform(spectrum[0], spectrum[1], cosine, sine_table, True)
    leaving = complex_product(between[0], between[1], window[2], window[3])
    farfield = transform(leaving[0], leaving[1], cosine, sine_table, False)
    return (between, farfield)

def window_gradient(window, measured_window, illumination, slab_real, slab_imag, cosine, sine_table):
    between, farfield = forward_window(window, illumination, slab_real, slab_imag, cosine, sine_table)
    magnitude = jnp.sqrt(farfield[0] * farfield[0] + farfield[1] * farfield[1])
    keeping = 1.0 - measured_window / jnp.maximum(magnitude, magnitude_floor)
    backward = transform(farfield[0] * keeping, farfield[1] * keeping, cosine, sine_table, True)
    grad_second = complex_product(between[0], -between[1], backward[0], backward[1])
    toward = complex_product(window[2], -window[3], backward[0], backward[1])
    spectrum = transform(toward[0], toward[1], cosine, sine_table, False)
    spectrum = complex_product(spectrum[0], spectrum[1], slab_real, -slab_imag)
    incoming = transform(spectrum[0], spectrum[1], cosine, sine_table, True)
    grad_first = complex_product(illumination[0], -illumination[1], incoming[0], incoming[1])
    return jnp.stack([grad_first[0], grad_first[1], grad_second[0], grad_second[1]])

def reference(object_field, momentum, measured, illumination, slab_phase, offsets, entry_counts):
    cosine, sine_table = tables(W)
    slab_real = jnp.cos(slab_phase)
    slab_imag = jnp.sin(slab_phase)
    layers = object_field.reshape(4, NYO, NXO)
    widths = ((0, 0), (MARGIN, MARGIN), (MARGIN, MARGIN))
    padded = jnp.pad(layers, widths)
    total = TROWS * TCOLS * LIST
    zero = jnp.zeros((), jnp.int32)

    def locate(entry):
        tile_index = entry // LIST
        within = entry % LIST
        tile_row = tile_index // TCOLS
        tile_col = tile_index % TCOLS
        place = offsets[tile_row, tile_col, within]
        row_start = (tile_row * TILE + place[0]).astype(jnp.int32)
        col_start = (tile_col * TILE + place[1]).astype(jnp.int32)
        live = (within < entry_counts[tile_row, tile_col]).astype(jnp.float32)
        return (tile_row, tile_col, within, row_start, col_start, live)

    def accumulate(gradient, entry):
        tile_row, tile_col, within, row_start, col_start, live = locate(entry)
        window = lax.dynamic_slice(padded, (zero, row_start, col_start), (4, W, W))
        term = window_gradient(window, measured[tile_row, tile_col, within], illumination, slab_real, slab_imag, cosine, sine_table) * live
        current = lax.dynamic_slice(gradient, (zero, row_start, col_start), (4, W, W))
        return (lax.dynamic_update_slice(gradient, current + term, (zero, row_start, col_start)), live)
    entries = jnp.arange(total, dtype=jnp.int32)
    gradient = lax.scan(accumulate, jnp.zeros(padded.shape, jnp.float32), entries)[0]
    interior = gradient[:, MARGIN:MARGIN + NYO, MARGIN:MARGIN + NXO]
    velocity = momentum_rate * momentum.reshape(4, NYO, NXO) + interior
    updated = layers - step_length * velocity
    refreshed = jnp.pad(updated, widths)

    def predict(entry):
        tile_row, tile_col, within, row_start, col_start, live = locate(entry)
        window = lax.dynamic_slice(refreshed, (zero, row_start, col_start), (4, W, W))
        farfield = forward_window(window, illumination, slab_real, slab_imag, cosine, sine_table)[1]
        return jnp.sqrt(farfield[0] * farfield[0] + farfield[1] * farfield[1]) * live
    amplitudes = lax.map(predict, entries).reshape(TROWS, TCOLS, LIST, W, W)
    return (updated.reshape(2, 2, NYO, NXO), velocity.reshape(2, 2, NYO, NXO), amplitudes)
```

```python
import functools
import math

import jax
import jax.numpy as jnp
import numpy as np
from jax import lax
from jax.experimental import pallas as pl
from jax.experimental.pallas import tpu as pltpu
from jax.sharding import PartitionSpec as P

f32 = jnp.float32
bf16 = jnp.bfloat16
MESH = pl.DeviceIdType.MESH
magnitude_floor = 0.5
momentum_rate = 0.9
step_length = 0.05
W = 256
MARGIN = 64
ROLES = [(s, h, k) for s in range(2) for h in range(2) for k in range(3)]
VMEM_LIMIT = 48 * 1024 * 1024


def tables(length):
    indices = np.arange(length)
    angles = (indices[:, None] * indices[None, :] % length) * (2.0 * math.pi / length)
    c = np.cos(angles) / math.sqrt(length)
    s = np.sin(angles) / math.sqrt(length)

    def halves(value):
        value = value.astype(np.float32)
        high = value.astype(jnp.bfloat16)
        low = (value - high.astype(np.float32)).astype(jnp.bfloat16)
        return np.stack([high, low])

    right = halves(np.concatenate([c, s], axis=0))
    forward = halves(np.block([[c, s], [-s, c]]))
    inverse = halves(np.block([[c, -s], [s, c]]))
    return right, np.stack([forward, inverse])


def coordinates():
    ty = lax.axis_index("ty")
    tx = lax.axis_index("tx")
    pos = lax.axis_index("pos")
    return ty, tx, pos, pos // 8, (pos // 4) % 2, pos % 4


def peer(ty, tx, pos):
    return {"ty": ty, "tx": tx, "pos": pos}


def position(y, zh, x):
    return y * 8 + zh * 4 + x


def close_peer(role, outward):
    s, h, k = role
    ty, tx, pos, y, zh, x = coordinates()
    step = (0, 3, 1)[k] if outward else (0, 1, 3)[k]
    other_ty = 1 - ty if s else ty
    other_zh = 1 - zh if h else zh
    return other_ty, (tx + step) % 4, other_zh, position(y, other_zh, x)


def enter(both_ways):
    ty, tx, pos, y, zh, x = coordinates()
    barrier = pltpu.get_barrier_semaphore()
    for role in ROLES:
        if role != (0, 0, 0):
            other_ty, other_tx, _, other_pos = close_peer(role, True)
            pl.semaphore_signal(barrier, inc=1, device_id=peer(other_ty, other_tx, other_pos), device_id_type=MESH)
    me = y * 4 + x
    small = (y % 2) * 4 + x

    def greet(start, count, modulus):
        def body(j, carry):
            t = (start + j) % modulus
            pl.semaphore_signal(
                barrier, inc=1, device_id=peer(ty, tx, position(t // 4, zh, t % 4)), device_id_type=MESH
            )
            return carry

        lax.fori_loop(0, count, body, 0)

    @pl.when(y < 2)
    def _():
        greet(me + 1, 15, 16)
        pl.semaphore_wait(barrier, 11 + (15 if both_ways else 7))

    @pl.when(y >= 2)
    def _():
        if both_ways:
            greet(small, 8, 8)
        pl.semaphore_wait(barrier, 11 + 8)


def gather_close(src, held, send_sem, recv_sem):
    ty, tx, pos, y, zh, x = coordinates()
    copies = []
    for index, role in enumerate(ROLES):
        if role == (0, 0, 0):
            continue
        k = role[2]
        other_ty, other_tx, _, other_pos = close_peer(role, True)
        if k == 0:
            source, target = src, held.at[ty, 0, :, zh]
        else:
            lanes = pl.ds(128 * (k - 1), 128)
            source, target = src.at[:, :, lanes], held.at[ty, 1, :, zh, :, lanes]
        copy = pltpu.make_async_remote_copy(
            src_ref=source,
            dst_ref=target,
            send_sem=send_sem.at[index],
            recv_sem=recv_sem.at[index],
            device_id=peer(other_ty, other_tx, other_pos),
            device_id_type=MESH,
        )
        copy.start()
        copies.append(copy)
    held[ty, 0, :, zh] = src[...]
    return copies


def row_swap(row_start):
    ty, tx, pos, y, zh, x = coordinates()
    shape = (2, 8, 256)
    row = (
        y * 64
        + x * 8
        + lax.broadcasted_iota(jnp.int32, shape, 0) * 32
        + lax.broadcasted_iota(jnp.int32, shape, 1)
    )
    return ((row < MARGIN) & (row_start > row + MARGIN)) | ((row >= 192) & (row > row_start + 191))


def column_swap(column_start):
    column = lax.broadcasted_iota(jnp.int32, (2, 8, 256), 2)
    return ((column < MARGIN) & (column_start > column + MARGIN)) | (
        (column >= 192) & (column > column_start + 191)
    )


def edge_columns():
    tx = lax.axis_index("tx")
    column = lax.broadcasted_iota(jnp.int32, (2, 8, 256), 2)
    missing = ((column < 128) & (tx == 3)) | ((column >= 128) & (tx == 0))
    return jnp.where(missing, 0.0, 1.0)


def edge_rows():
    ty, tx, pos, y, zh, x = coordinates()
    present = ((ty == 0) & (y == 0)) | ((ty == 1) & (y == 3))
    return jnp.where(present, 1.0, 0.0)


def gather_far(offsets, held, blocks, window, send_sem, recv_sem):
    ty, tx, pos, y, zh, x = coordinates()
    base = (y % 2) * 4 + x
    me = y * 4 + x
    columns_real = edge_columns()
    rows_real = edge_rows()

    def target_of(j):
        t = (base + j) % 8
        return position(t // 4, zh, t % 4)

    def copy_to(j):
        return pltpu.make_async_remote_copy(
            src_ref=blocks.at[j],
            dst_ref=window.at[:, pl.ds(2 * y, 2), x],
            send_sem=send_sem.at[j],
            recv_sem=recv_sem.at[me],
            device_id=peer(ty, tx, target_of(j)),
            device_id_type=MESH,
        )

    for j in range(8):
        target = target_of(j)
        swap_rows = row_swap(offsets[target, 0])
        swap_columns = column_swap(offsets[target, 1])
        for layer in range(4):
            own = jnp.where(swap_columns, held[ty, 1, layer] * columns_real, held[ty, 0, layer])
            sibling = jnp.where(swap_columns, held[1 - ty, 1, layer] * columns_real, held[1 - ty, 0, layer])
            blocks[j, layer] = jnp.where(swap_rows, sibling * rows_real, own)
        if j == 0:

            @pl.when(y >= 2)
            def _():
                copy_to(0).start()

            @pl.when(y < 2)
            def _():
                window[:, pl.ds(2 * y, 2), x] = blocks[0]

        else:
            copy_to(j).start()

    @pl.when(y < 2)
    def _():
        def arrive(j, carry):
            s = (me + j) % 16
            pltpu.make_async_remote_copy(
                src_ref=blocks.at[0],
                dst_ref=window.at[:, pl.ds(2 * (s // 4), 2), s % 4],
                send_sem=send_sem.at[0],
                recv_sem=recv_sem.at[s],
                device_id=peer(ty, tx, position(s // 4, zh, s % 4)),
                device_id_type=MESH,
            ).wait_recv()
            return carry

        lax.fori_loop(1, 16, arrive, 0)

    @pl.when(y >= 2)
    def _():
        copy_to(0).wait_send()

    for j in range(1, 8):
        copy_to(j).wait_send()


def gather_kernel(offsets, rows, window, held, blocks, send_close, recv_close, send_far, recv_far):
    enter(False)
    for copy in gather_close(rows, held, send_close, recv_close):
        copy.wait()
    gather_far(offsets, held, blocks, window, send_far, recv_far)


def return_kernel(
    offsets,
    rows,
    momentum,
    gradient,
    new_rows,
    new_momentum,
    window,
    arrived,
    sums,
    parts_own,
    parts_side,
    held,
    blocks,
    send_return,
    recv_return,
    send_sum,
    recv_sum,
    send_close,
    recv_close,
    send_far,
    recv_far,
):
    ty, tx, pos, y, zh, x = coordinates()
    enter(True)
    me = y * 4 + x
    base = (y % 2) * 4 + x

    def copy_to(j):
        t = (me + j) % 16
        return pltpu.make_async_remote_copy(
            src_ref=gradient.at[:, pl.ds(2 * (t // 4), 2), t % 4],
            dst_ref=arrived.at[base],
            send_sem=send_return.at[j],
            recv_sem=recv_return.at[base],
            device_id=peer(ty, tx, position(t // 4, zh, t % 4)),
            device_id_type=MESH,
        )

    def copy_from(s):
        return pltpu.make_async_remote_copy(
            src_ref=gradient.at[:, pl.ds(0, 2), 0],
            dst_ref=arrived.at[s],
            send_sem=send_return.at[0],
            recv_sem=recv_return.at[s],
            device_id=peer(ty, tx, position(s // 4, zh, s % 4)),
            device_id_type=MESH,
        )

    @pl.when(y < 2)
    def _():
        def leave(j, carry):
            copy_to(j).start()
            return carry

        lax.fori_loop(1, 16, leave, 0)
        arrived[base] = gradient[:, pl.ds(2 * y, 2), x]

    @pl.when(y >= 2)
    def _():
        copy_from(base).wait_recv()

    for j in range(1, 8):
        copy_from((base + j) % 8).wait_recv()

    columns_real = edge_columns()
    rows_real = edge_rows()
    swaps = []
    for j in range(8):
        target = position(j // 4, zh, j % 4)
        swaps.append((row_swap(offsets[target, 0]), column_swap(offsets[target, 1])))
    for layer in range(4):
        own = jnp.zeros((2, 8, 256), f32)
        own_side, sibling, sibling_side = own, own, own
        for j in range(8):
            swap_rows, swap_columns = swaps[j]
            block = arrived[j, layer]
            mine = jnp.where(swap_rows, 0.0, block)
            theirs = jnp.where(swap_rows, block, 0.0)
            own = own + jnp.where(swap_columns, 0.0, mine)
            own_side = own_side + jnp.where(swap_columns, mine, 0.0)
            sibling = sibling + jnp.where(swap_columns, 0.0, theirs)
            sibling_side = sibling_side + jnp.where(swap_columns, theirs, 0.0)
        sums[ty, 0, layer] = own
        sums[ty, 1, layer] = own_side * columns_real
        sums[1 - ty, 0, layer] = sibling * rows_real
        sums[1 - ty, 1, layer] = sibling_side * columns_real * rows_real

    copies = []
    for index, role in enumerate(ROLES):
        if role == (0, 0, 0):
            continue
        s, h, k = role
        other_ty, other_tx, other_zh, other_pos = close_peer(role, False)
        if k == 0:
            source, target = sums.at[other_ty, 0, :, other_zh], parts_own.at[2 * s + h]
        else:
            lanes = pl.ds(128 * (k - 1), 128)
            source = sums.at[other_ty, 1, :, other_zh, :, lanes]
            target = parts_side.at[2 * s + h, :, :, lanes]
        copy = pltpu.make_async_remote_copy(
            src_ref=source,
            dst_ref=target,
            send_sem=send_sum.at[index],
            recv_sem=recv_sum.at[index],
            device_id=peer(other_ty, other_tx, other_pos),
            device_id_type=MESH,
        )
        copy.start()
        copies.append(copy)
    for copy in copies:
        copy.wait()
    total = sums[ty, 0, :, zh]
    for part in range(4):
        if part:
            total = total + parts_own[part]
        total = total + parts_side[part]
    velocity = momentum_rate * momentum[...] + total
    new_momentum[...] = velocity
    new_rows[...] = rows[...] - step_length * velocity
    for copy in gather_close(new_rows, held, send_close, recv_close):
        copy.wait()
    gather_far(offsets, held, blocks, window, send_far, recv_far)

    @pl.when(y < 2)
    def _():
        def left(j, carry):
            copy_to(j).wait_send()
            return carry

        lax.fori_loop(1, 16, left, 0)


def split(value):
    high = value.astype(bf16)
    return high, (value - high.astype(f32)).astype(bf16)


def product(left, right):
    return jnp.dot(left, right, preferred_element_type=f32)


def transform(real_part, imag_part, right, left, inverse):
    def stacked(r, i):
        if inverse:
            return jnp.concatenate([jnp.concatenate([r, -i], 1), jnp.concatenate([i, r], 1)], 0)
        return jnp.concatenate([jnp.concatenate([r, i], 1), jnp.concatenate([i, -r], 1)], 0)

    real_high, real_low = split(real_part)
    imag_high, imag_low = split(imag_part)
    high = stacked(real_high, imag_high)
    low = stacked(real_low, imag_low)
    middle = product(high, right[0]) + product(low, right[0]) + product(high, right[1])
    high, low = split(middle)
    which = 1 if inverse else 0
    result = product(left[which, 0], high) + product(left[which, 0], low) + product(left[which, 1], high)
    return result[:W], result[W:]


def complex_product(first_real, first_imag, second_real, second_imag):
    return (
        first_real * second_real - first_imag * second_imag,
        first_real * second_imag + first_imag * second_real,
    )


def shifted_probe(offsets, illumination):
    pos = lax.axis_index("pos")
    down = (offsets[pos, 0] + 192) % 256
    across = (offsets[pos, 1] + 192) % 256
    return [pltpu.roll(pltpu.roll(illumination[part], down, 0), across, 1) for part in range(2)]


def forward(window, probe, slab, right, left):
    entering = complex_product(probe[0], probe[1], window[0], window[1])
    spectrum = transform(entering[0], entering[1], right, left, False)
    spectrum = complex_product(spectrum[0], spectrum[1], slab[0], slab[1])
    between = transform(spectrum[0], spectrum[1], right, left, True)
    leaving = complex_product(between[0], between[1], window[2], window[3])
    return between, transform(leaving[0], leaving[1], right, left, False)


def gradient_kernel(offsets, counts, window, measured, illumination, slab, right, left, gradient):
    pos = lax.axis_index("pos")
    live = pos < counts[0, 0]

    @pl.when(jnp.logical_not(live))
    def _():
        gradient[...] = jnp.zeros_like(gradient)

    @pl.when(live)
    def _():
        probe = shifted_probe(offsets, illumination)
        between, farfield = forward(window, probe, slab, right, left)
        magnitude = jnp.sqrt(farfield[0] * farfield[0] + farfield[1] * farfield[1])
        keeping = 1.0 - measured[...] / jnp.maximum(magnitude, magnitude_floor)
        backward = transform(farfield[0] * keeping, farfield[1] * keeping, right, left, True)
        grad_second = complex_product(between[0], -between[1], backward[0], backward[1])
        gradient[2] = grad_second[0]
        gradient[3] = grad_second[1]
        toward = complex_product(window[2], -window[3], backward[0], backward[1])
        spectrum = transform(toward[0], toward[1], right, left, False)
        spectrum = complex_product(spectrum[0], spectrum[1], slab[0], -slab[1])
        incoming = transform(spectrum[0], spectrum[1], right, left, True)
        grad_first = complex_product(probe[0], -probe[1], incoming[0], incoming[1])
        gradient[0] = grad_first[0]
        gradient[1] = grad_first[1]


def predict_kernel(offsets, counts, window, illumination, slab, right, left, amplitude):
    pos = lax.axis_index("pos")
    live = pos < counts[0, 0]

    @pl.when(jnp.logical_not(live))
    def _():
        amplitude[...] = jnp.zeros_like(amplitude)

    @pl.when(live)
    def _():
        probe = shifted_probe(offsets, illumination)
        farfield = forward(window, probe, slab, right, left)[1]
        amplitude[...] = jnp.sqrt(farfield[0] * farfield[0] + farfield[1] * farfield[1])


def specs(count, scalars):
    return [pl.BlockSpec(memory_space=pltpu.SMEM)] * scalars + [pl.BlockSpec(memory_space=pltpu.VMEM)] * count


def shards(object_field, momentum, measured, illumination, slab_phase, offsets, entry_counts):
    rows = object_field.reshape(4, 8, W)
    momentum = momentum.reshape(4, 8, W)
    places = offsets[0, 0]
    right, left = (jnp.asarray(t) for t in tables(W))
    slab = jnp.stack([jnp.cos(slab_phase), jnp.sin(slab_phase)])
    dma = pltpu.SemaphoreType.DMA
    close = len(ROLES)
    window_shape = (4, 8, 4, 8, W)
    block_shape = (4, 2, 8, W)
    remote = functools.partial(
        pltpu.CompilerParams, has_side_effects=True, vmem_limit_bytes=VMEM_LIMIT
    )
    window = pl.pallas_call(
        gather_kernel,
        out_shape=jax.ShapeDtypeStruct(window_shape, f32),
        in_specs=specs(1, 1),
        out_specs=pl.BlockSpec(memory_space=pltpu.VMEM),
        scratch_shapes=[
            pltpu.VMEM((2, 2, *block_shape), f32),
            pltpu.VMEM((8, *block_shape), f32),
            dma((close,)),
            dma((close,)),
            dma((8,)),
            dma((16,)),
        ],
        compiler_params=remote(collective_id=0),
        name="gather_windows",
    )(places, rows)
    local = pltpu.CompilerParams(vmem_limit_bytes=VMEM_LIMIT)
    gradient = pl.pallas_call(
        gradient_kernel,
        out_shape=jax.ShapeDtypeStruct((4, W, W), f32),
        in_specs=specs(6, 2),
        out_specs=pl.BlockSpec(memory_space=pltpu.VMEM),
        compiler_params=local,
        name="window_gradient",
    )(places, entry_counts, window.reshape(4, W, W), measured[0, 0, 0], illumination, slab, right, left)
    new_rows, new_momentum, window = pl.pallas_call(
        return_kernel,
        out_shape=(
            jax.ShapeDtypeStruct((4, 8, W), f32),
            jax.ShapeDtypeStruct((4, 8, W), f32),
            jax.ShapeDtypeStruct(window_shape, f32),
        ),
        in_specs=specs(3, 1),
        out_specs=specs(3, 0),
        scratch_shapes=[
            pltpu.VMEM((8, *block_shape), f32),
            pltpu.VMEM((2, 2, *block_shape), f32),
            pltpu.VMEM((4, 4, 8, W), f32),
            pltpu.VMEM((4, 4, 8, W), f32),
            pltpu.VMEM((2, 2, *block_shape), f32),
            pltpu.VMEM((8, *block_shape), f32),
            dma((16,)),
            dma((8,)),
            dma((close,)),
            dma((close,)),
            dma((close,)),
            dma((close,)),
            dma((8,)),
            dma((16,)),
        ],
        compiler_params=remote(collective_id=1),
        name="return_gradients",
    )(places, rows, momentum, gradient.reshape(window_shape))
    amplitude = pl.pallas_call(
        predict_kernel,
        out_shape=jax.ShapeDtypeStruct((W, W), f32),
        in_specs=specs(5, 2),
        out_specs=pl.BlockSpec(memory_space=pltpu.VMEM),
        compiler_params=local,
        name="predict",
    )(places, entry_counts, window.reshape(4, W, W), illumination, slab, right, left)
    return (
        new_rows.reshape(2, 2, 8, W),
        new_momentum.reshape(2, 2, 8, W),
        amplitude[None, None, None],
    )


def solution(mesh):
    rows = P(None, None, ("ty", "pos"), "tx")
    slots = P("ty", "tx", "pos", None, None)
    return jax.shard_map(
        shards,
        mesh=mesh,
        in_specs=(rows, rows, slots, P(), P(), P("ty", "tx", None, None), P("ty", "tx")),
        out_specs=(rows, rows, slots),
        check_vma=False,
    )
```

```python
import functools
import math

import jax
import jax.numpy as jnp
import numpy as np
from jax import lax
from jax.experimental import pallas as pl
from jax.experimental.pallas import tpu as pltpu
from jax.sharding import PartitionSpec as P

f32 = jnp.float32
bf16 = jnp.bfloat16
MESH = pl.DeviceIdType.MESH
magnitude_floor = 0.5
momentum_rate = 0.9
step_length = 0.05
W = 256
MARGIN = 64
ROLES = [(s, h, k) for s in range(2) for h in range(2) for k in range(3) if (s, h, k) != (0, 0, 0)]
VMEM_LIMIT = 48 * 1024 * 1024


def tables(length):
    indices = np.arange(length)
    angles = (indices[:, None] * indices[None, :] % length) * (2.0 * math.pi / length)
    c = np.cos(angles) / math.sqrt(length)
    s = np.sin(angles) / math.sqrt(length)

    def halves(value):
        value = value.astype(np.float32)
        high = value.astype(jnp.bfloat16)
        low = (value - high.astype(np.float32)).astype(jnp.bfloat16)
        return np.stack([high, low])

    right = halves(np.concatenate([c, s], axis=0))
    forward = halves(np.block([[c, s], [-s, c]]))
    inverse = halves(np.block([[c, -s], [s, c]]))
    return right, np.stack([forward, inverse])


def coordinates():
    ty = lax.axis_index("ty")
    tx = lax.axis_index("tx")
    pos = lax.axis_index("pos")
    return ty, tx, pos, pos // 8, (pos // 4) % 2, pos % 4


def peer(ty, tx, pos):
    return {"ty": ty, "tx": tx, "pos": pos}


def position(y, zh, x):
    return y * 8 + zh * 4 + x


def close_peer(role, outward):
    s, h, k = role
    ty, tx, pos, y, zh, x = coordinates()
    step = (0, 3, 1)[k] if outward else (0, 1, 3)[k]
    other_ty = 1 - ty if s else ty
    other_zh = 1 - zh if h else zh
    return other_ty, (tx + step) % 4, other_zh, position(y, other_zh, x)


def has_role(role, y_pair, tx_lower, tx_upper):
    s, h, k = role
    terms = ([y_pair] if s else []) + [[], [tx_lower], [tx_upper]][k]
    return functools.reduce(jnp.logical_and, terms) if terms else None


def when(condition, body):
    if condition is None:
        body()
    else:
        pl.when(condition)(body)


def enter():
    ty, tx, pos, y, zh, x = coordinates()
    barrier = pltpu.get_barrier_semaphore()
    outer = (y == 0) | (y == 3)
    for role in ROLES:
        other_ty, other_tx, _, other_pos = close_peer(role, True)

        def signal(other_ty=other_ty, other_tx=other_tx, other_pos=other_pos):
            pl.semaphore_signal(barrier, inc=1, device_id=peer(other_ty, other_tx, other_pos), device_id_type=MESH)

        when(has_role(role, outer, tx > 0, tx < 3), signal)
    near = jnp.where((tx == 0) | (tx == 3), 4, 6) * jnp.where(outer, 2, 1) - 1
    me = y * 4 + x
    small = (y % 2) * 4 + x

    def greet(start, count, modulus):
        def body(j, carry):
            t = (start + j) % modulus
            pl.semaphore_signal(
                barrier, inc=1, device_id=peer(ty, tx, position(t // 4, zh, t % 4)), device_id_type=MESH
            )
            return carry

        lax.fori_loop(0, count, body, 0)

    @pl.when(y < 2)
    def _():
        greet(me + 1, 15, 16)
        pl.semaphore_wait(barrier, near + 15)

    @pl.when(y >= 2)
    def _():
        greet(small, 8, 8)
        pl.semaphore_wait(barrier, near + 8)


def sibling_facts():
    ty, tx, pos, y, zh, x = coordinates()
    takes = ((ty == 0) & (y == 0)) | ((ty == 1) & (y == 3))
    gives = ((ty == 1) & (y == 0)) | ((ty == 0) & (y == 3))
    return takes, gives


def close_copy(index, role, piece, src, held, send_sem, recv_sem):
    ty, tx, pos, y, zh, x = coordinates()
    k = role[2]
    layers = pl.ds(2 * piece, 2)
    other_ty, other_tx, _, other_pos = close_peer(role, True)
    if k == 0:
        source, target = src.at[layers], held.at[ty, 0, layers, zh]
    else:
        lanes = pl.ds(128 * (k - 1), 128)
        source, target = src.at[layers, :, lanes], held.at[ty, 1, layers, zh, :, lanes]
    return pltpu.make_async_remote_copy(
        src_ref=source,
        dst_ref=target,
        send_sem=send_sem.at[piece, index],
        recv_sem=recv_sem.at[piece, index],
        device_id=peer(other_ty, other_tx, other_pos),
        device_id_type=MESH,
    )


def close_start(piece, src, held, send_sem, recv_sem):
    ty, tx, pos, y, zh, x = coordinates()
    takes, gives = sibling_facts()
    for index, role in enumerate(ROLES):
        copy = close_copy(index, role, piece, src, held, send_sem, recv_sem)
        when(has_role(role, gives, tx > 0, tx < 3), copy.start)
    for layer in (2 * piece, 2 * piece + 1):
        held[ty, 0, layer, zh] = src[layer]


def close_wait(piece, src, held, send_sem, recv_sem):
    ty, tx, pos, y, zh, x = coordinates()
    takes, gives = sibling_facts()
    for index, role in enumerate(ROLES):
        copy = close_copy(index, role, piece, src, held, send_sem, recv_sem)
        when(has_role(role, takes, tx < 3, tx > 0), copy.wait_recv)


def close_drain(piece, src, held, send_sem, recv_sem):
    ty, tx, pos, y, zh, x = coordinates()
    takes, gives = sibling_facts()
    for index, role in enumerate(ROLES):
        copy = close_copy(index, role, piece, src, held, send_sem, recv_sem)
        when(has_role(role, gives, tx > 0, tx < 3), copy.wait_send)


def clear_missing(held):
    ty, tx, pos, y, zh, x = coordinates()
    takes, gives = sibling_facts()
    nothing = jnp.zeros((4, 2, 8, 128), f32)

    @pl.when(jnp.logical_not(takes))
    def _():
        for kind in range(2):
            held[1 - ty, kind] = jnp.zeros((4, 2, 8, W), f32)

    @pl.when(tx == 3)
    def _():
        for core in range(2):
            held[core, 1, :, :, :, 0:128] = nothing

    @pl.when(tx == 0)
    def _():
        for core in range(2):
            held[core, 1, :, :, :, 128:256] = nothing


def row_swap(row_start):
    ty, tx, pos, y, zh, x = coordinates()
    shape = (2, 8, W)
    row = (
        y * 64
        + x * 8
        + lax.broadcasted_iota(jnp.int32, shape, 0) * 32
        + lax.broadcasted_iota(jnp.int32, shape, 1)
    )
    return ((row < MARGIN) & (row_start > row + MARGIN)) | ((row >= 192) & (row > row_start + 191))


def column_swap(column_start):
    column = lax.broadcasted_iota(jnp.int32, (2, 8, W), 2)
    return ((column < MARGIN) & (column_start > column + MARGIN)) | (
        (column >= 192) & (column > column_start + 191)
    )


def far_copy(j, piece, blocks, window, send_sem, recv_sem):
    ty, tx, pos, y, zh, x = coordinates()
    t = ((y % 2) * 4 + x + j) % 8
    return pltpu.make_async_remote_copy(
        src_ref=blocks.at[piece, j],
        dst_ref=window.at[pl.ds(2 * piece, 2), pl.ds(2 * y, 2), x],
        send_sem=send_sem.at[piece, j],
        recv_sem=recv_sem.at[piece, y * 4 + x],
        device_id=peer(ty, tx, position(t // 4, zh, t % 4)),
        device_id_type=MESH,
    )


def far_start(piece, offsets, held, blocks, window, send_sem, recv_sem):
    ty, tx, pos, y, zh, x = coordinates()
    for j in range(8):
        t = ((y % 2) * 4 + x + j) % 8
        target = position(t // 4, zh, t % 4)
        swap_rows = row_swap(offsets[target, 0])
        swap_columns = column_swap(offsets[target, 1])
        for part in range(2):
            layer = 2 * piece + part
            own = jnp.where(swap_columns, held[ty, 1, layer], held[ty, 0, layer])
            sibling = jnp.where(swap_columns, held[1 - ty, 1, layer], held[1 - ty, 0, layer])
            blocks[piece, j, part] = jnp.where(swap_rows, sibling, own)
        if j == 0:

            @pl.when(y >= 2)
            def _():
                far_copy(0, piece, blocks, window, send_sem, recv_sem).start()

            @pl.when(y < 2)
            def _():
                for part in range(2):
                    window[2 * piece + part, pl.ds(2 * y, 2), x] = blocks[piece, 0, part]

        else:
            far_copy(j, piece, blocks, window, send_sem, recv_sem).start()


def far_wait(piece, blocks, window, send_sem, recv_sem):
    ty, tx, pos, y, zh, x = coordinates()

    def arrive(j, carry):
        s = (y * 4 + x + j) % 16
        pltpu.make_async_remote_copy(
            src_ref=blocks.at[piece, 0],
            dst_ref=window.at[pl.ds(2 * piece, 2), pl.ds(2 * (s // 4), 2), s % 4],
            send_sem=send_sem.at[piece, 0],
            recv_sem=recv_sem.at[piece, s],
            device_id=peer(ty, tx, position(s // 4, zh, s % 4)),
            device_id_type=MESH,
        ).wait_recv()
        return carry

    lax.fori_loop(1, 16, arrive, 0)


def far_drain(piece, blocks, window, send_sem, recv_sem):
    ty, tx, pos, y, zh, x = coordinates()

    @pl.when(y >= 2)
    def _():
        far_copy(0, piece, blocks, window, send_sem, recv_sem).wait_send()

    for j in range(1, 8):
        far_copy(j, piece, blocks, window, send_sem, recv_sem).wait_send()


def return_copy(j, piece, gradient, arrived, send_sem, recv_sem):
    ty, tx, pos, y, zh, x = coordinates()
    t = (y * 4 + x + j) % 16
    return pltpu.make_async_remote_copy(
        src_ref=gradient.at[pl.ds(2 * piece, 2), pl.ds(2 * (t // 4), 2), t % 4],
        dst_ref=arrived.at[piece, (y % 2) * 4 + x],
        send_sem=send_sem.at[piece, j],
        recv_sem=recv_sem.at[piece, (y % 2) * 4 + x],
        device_id=peer(ty, tx, position(t // 4, zh, t % 4)),
        device_id_type=MESH,
    )


def return_start(piece, gradient, arrived, send_sem, recv_sem):
    ty, tx, pos, y, zh, x = coordinates()

    def leave(j, carry):
        return_copy(j, piece, gradient, arrived, send_sem, recv_sem).start()
        return carry

    lax.fori_loop(1, 16, leave, 0)
    for part in range(2):
        arrived[piece, (y % 2) * 4 + x, part] = gradient[2 * piece + part, pl.ds(2 * y, 2), x]


def return_wait(piece, gradient, arrived, send_sem, recv_sem):
    ty, tx, pos, y, zh, x = coordinates()
    base = (y % 2) * 4 + x

    def wait_for(s):
        pltpu.make_async_remote_copy(
            src_ref=gradient.at[pl.ds(2 * piece, 2), pl.ds(0, 2), 0],
            dst_ref=arrived.at[piece, s],
            send_sem=send_sem.at[piece, 0],
            recv_sem=recv_sem.at[piece, s],
            device_id=peer(ty, tx, position(s // 4, zh, s % 4)),
            device_id_type=MESH,
        ).wait_recv()

    @pl.when(y >= 2)
    def _():
        wait_for(base)

    for j in range(1, 8):
        wait_for((base + j) % 8)


def return_drain(piece, gradient, arrived, send_sem, recv_sem):
    def left(j, carry):
        return_copy(j, piece, gradient, arrived, send_sem, recv_sem).wait_send()
        return carry

    lax.fori_loop(1, 16, left, 0)


def add_returned(piece, offsets, arrived, sums):
    ty, tx, pos, y, zh, x = coordinates()
    swaps = []
    for j in range(8):
        target = position(j // 4, zh, j % 4)
        swaps.append((row_swap(offsets[target, 0]), column_swap(offsets[target, 1])))
    for part in range(2):
        layer = 2 * piece + part
        own = jnp.zeros((2, 8, W), f32)
        own_side, sibling, sibling_side = own, own, own
        for j in range(8):
            swap_rows, swap_columns = swaps[j]
            block = arrived[piece, j, part]
            mine = jnp.where(swap_rows, 0.0, block)
            theirs = jnp.where(swap_rows, block, 0.0)
            own = own + jnp.where(swap_columns, 0.0, mine)
            own_side = own_side + jnp.where(swap_columns, mine, 0.0)
            sibling = sibling + jnp.where(swap_columns, 0.0, theirs)
            sibling_side = sibling_side + jnp.where(swap_columns, theirs, 0.0)
        sums[ty, 0, layer] = own
        sums[ty, 1, layer] = own_side
        sums[1 - ty, 0, layer] = sibling
        sums[1 - ty, 1, layer] = sibling_side


def sum_copy(index, role, piece, sums, parts_own, parts_side, send_sem, recv_sem):
    s, h, k = role
    layers = pl.ds(2 * piece, 2)
    other_ty, other_tx, other_zh, other_pos = close_peer(role, False)
    if k == 0:
        source, target = sums.at[other_ty, 0, layers, other_zh], parts_own.at[2 * s + h, layers]
    else:
        lanes = pl.ds(128 * (k - 1), 128)
        source = sums.at[other_ty, 1, layers, other_zh, :, lanes]
        target = parts_side.at[2 * s + h, layers, :, lanes]
    return pltpu.make_async_remote_copy(
        src_ref=source,
        dst_ref=target,
        send_sem=send_sem.at[piece, index],
        recv_sem=recv_sem.at[piece, index],
        device_id=peer(other_ty, other_tx, other_pos),
        device_id_type=MESH,
    )


def sum_each(piece, action, *refs):
    ty, tx, pos, y, zh, x = coordinates()
    takes, gives = sibling_facts()
    for index, role in enumerate(ROLES):
        copy = sum_copy(index, role, piece, *refs)
        if action == "recv":
            when(has_role(role, gives, tx > 0, tx < 3), copy.wait_recv)
        else:
            act = copy.start if action == "start" else copy.wait_send
            when(has_role(role, takes, tx < 3, tx > 0), act)


def clear_parts(parts_own, parts_side):
    ty, tx, pos, y, zh, x = coordinates()
    takes, gives = sibling_facts()
    nothing = jnp.zeros((4, 8, 128), f32)

    @pl.when(jnp.logical_not(gives))
    def _():
        for part in (2, 3):
            parts_own[part] = jnp.zeros((4, 8, W), f32)
            parts_side[part] = jnp.zeros((4, 8, W), f32)

    @pl.when(tx == 0)
    def _():
        for part in range(4):
            parts_side[part, :, :, 0:128] = nothing

    @pl.when(tx == 3)
    def _():
        for part in range(4):
            parts_side[part, :, :, 128:256] = nothing


def split(value):
    high = value.astype(bf16)
    return high, (value - high.astype(f32)).astype(bf16)


def product(left, right):
    return jnp.dot(left, right, preferred_element_type=f32)


def transform(real_part, imag_part, right, left, inverse):
    def stacked(r, i):
        if inverse:
            return jnp.concatenate([jnp.concatenate([r, -i], 1), jnp.concatenate([i, r], 1)], 0)
        return jnp.concatenate([jnp.concatenate([r, i], 1), jnp.concatenate([i, -r], 1)], 0)

    real_high, real_low = split(real_part)
    imag_high, imag_low = split(imag_part)
    high = stacked(real_high, imag_high)
    low = stacked(real_low, imag_low)
    middle = product(high, right[0]) + product(low, right[0]) + product(high, right[1])
    high, low = split(middle)
    which = 1 if inverse else 0
    result = product(left[which, 0], high) + product(left[which, 0], low) + product(left[which, 1], high)
    return result[:W], result[W:]


def complex_product(first_real, first_imag, second_real, second_imag):
    return (
        first_real * second_real - first_imag * second_imag,
        first_real * second_imag + first_imag * second_real,
    )


def shifted_probe(offsets, illumination):
    pos = lax.axis_index("pos")
    down = (offsets[pos, 0] + 192) % 256
    across = (offsets[pos, 1] + 192) % 256
    return [pltpu.roll(pltpu.roll(illumination[part], down, 0), across, 1) for part in range(2)]


def layer_of(window, layer):
    return window[layer].reshape(W, W)


def between_field(window, probe, slab, right, left):
    entering = complex_product(probe[0], probe[1], layer_of(window, 0), layer_of(window, 1))
    spectrum = transform(entering[0], entering[1], right, left, False)
    spectrum = complex_product(spectrum[0], spectrum[1], slab[0], slab[1])
    return transform(spectrum[0], spectrum[1], right, left, True)


def farfield_of(between, window, right, left):
    leaving = complex_product(between[0], between[1], layer_of(window, 2), layer_of(window, 3))
    return transform(leaving[0], leaving[1], right, left, False)


def kernel(
    offsets,
    counts,
    rows,
    momentum,
    measured_hbm,
    illumination_hbm,
    phase_hbm,
    right_hbm,
    left_hbm,
    new_rows,
    new_momentum,
    amplitude,
    measured,
    illumination,
    phase,
    right,
    left,
    probe,
    slab,
    between_kept,
    held_first,
    held_second,
    blocks_first,
    blocks_second,
    window_first,
    window_second,
    gradient,
    arrived,
    sums,
    parts_own,
    parts_side,
    local_sem,
    close_send_first,
    close_recv_first,
    close_send_second,
    close_recv_second,
    far_send_first,
    far_recv_first,
    far_send_second,
    far_recv_second,
    return_send,
    return_recv,
    sum_send,
    sum_recv,
):
    ty, tx, pos, y, zh, x = coordinates()
    loads = [
        pltpu.make_async_copy(source, target, local_sem.at[n])
        for n, (source, target) in enumerate(
            (
                (phase_hbm, phase),
                (illumination_hbm, illumination),
                (right_hbm, right),
                (left_hbm, left),
                (measured_hbm, measured),
            )
        )
    ]

    @pl.when(y < 2)
    def _():
        for load in loads:
            load.start()

    clear_missing(held_first)
    clear_missing(held_second)
    clear_parts(parts_own, parts_side)
    enter()
    close_first = (rows, held_first, close_send_first, close_recv_first)
    close_second = (new_rows, held_second, close_send_second, close_recv_second)
    far_first = (blocks_first, window_first, far_send_first, far_recv_first)
    far_second = (blocks_second, window_second, far_send_second, far_recv_second)
    returned = (gradient, arrived, return_send, return_recv)
    summed = (sums, parts_own, parts_side, sum_send, sum_recv)
    for piece in (0, 1):
        close_start(piece, *close_first)
    for piece in (0, 1):
        close_wait(piece, *close_first)
        far_start(piece, offsets, held_first, *far_first)
    live = jnp.where(pos < counts[0, 0], 1.0, 0.0)

    @pl.when(y < 2)
    def _():
        for load in loads:
            load.wait()
        slab[0] = jnp.cos(phase[...])
        slab[1] = jnp.sin(phase[...])
        shifted = shifted_probe(offsets, illumination)
        probe[0] = shifted[0]
        probe[1] = shifted[1]
        far_wait(0, *far_first)
        between = between_field(window_first, probe, slab, right, left)
        between_kept[0] = between[0]
        between_kept[1] = between[1]
        far_wait(1, *far_first)
        farfield = farfield_of(between, window_first, right, left)
        magnitude = jnp.sqrt(farfield[0] * farfield[0] + farfield[1] * farfield[1])
        keeping = (1.0 - measured[...] / jnp.maximum(magnitude, magnitude_floor)) * live
        backward = transform(farfield[0] * keeping, farfield[1] * keeping, right, left, True)
        grad_second = complex_product(between_kept[0], -between_kept[1], backward[0], backward[1])
        gradient[2] = grad_second[0].reshape(8, 4, 8, W)
        gradient[3] = grad_second[1].reshape(8, 4, 8, W)
        return_start(1, *returned)
        toward = complex_product(layer_of(window_first, 2), -layer_of(window_first, 3), backward[0], backward[1])
        spectrum = transform(toward[0], toward[1], right, left, False)
        spectrum = complex_product(spectrum[0], spectrum[1], slab[0], -slab[1])
        incoming = transform(spectrum[0], spectrum[1], right, left, True)
        grad_first = complex_product(probe[0], -probe[1], incoming[0], incoming[1])
        gradient[0] = grad_first[0].reshape(8, 4, 8, W)
        gradient[1] = grad_first[1].reshape(8, 4, 8, W)
        return_start(0, *returned)

    for piece in (1, 0):
        return_wait(piece, *returned)
        add_returned(piece, offsets, arrived, sums)
        sum_each(piece, "start", *summed)
        sum_each(piece, "recv", *summed)
        for layer in (2 * piece, 2 * piece + 1):
            total = sums[ty, 0, layer, zh]
            for part in range(4):
                if part:
                    total = total + parts_own[part, layer]
                total = total + parts_side[part, layer]
            velocity = momentum_rate * momentum[layer] + total
            new_momentum[layer] = velocity
            new_rows[layer] = rows[layer] - step_length * velocity
        close_start(piece, *close_second)
        close_wait(piece, *close_second)
        far_start(piece, offsets, held_second, *far_second)

    @pl.when(y < 2)
    def _():
        far_wait(0, *far_second)
        between = between_field(window_second, probe, slab, right, left)
        far_wait(1, *far_second)
        farfield = farfield_of(between, window_second, right, left)
        amplitude[...] = jnp.sqrt(farfield[0] * farfield[0] + farfield[1] * farfield[1]) * live

    @pl.when(y >= 2)
    def _():
        amplitude[...] = jnp.zeros_like(amplitude)

    for piece in (0, 1):
        close_drain(piece, *close_first)
        close_drain(piece, *close_second)
        far_drain(piece, *far_first)
        far_drain(piece, *far_second)
        sum_each(piece, "sent", *summed)

    @pl.when(y < 2)
    def _():
        for piece in (0, 1):
            return_drain(piece, *returned)


def shards(object_field, momentum, measured, illumination, slab_phase, offsets, entry_counts):
    rows = object_field.reshape(4, 8, W)
    right, left = (jnp.asarray(t) for t in tables(W))
    dma = pltpu.SemaphoreType.DMA
    close = len(ROLES)
    window_shape = (4, 8, 4, 8, W)
    held_shape = (2, 2, 4, 2, 8, W)
    blocks_shape = (2, 8, 2, 2, 8, W)
    field = (2, W, W)
    vmem = pl.BlockSpec(memory_space=pltpu.VMEM)
    smem = pl.BlockSpec(memory_space=pltpu.SMEM)
    remain = pl.BlockSpec(memory_space=pl.ANY)
    new_rows, new_momentum, amplitude = pl.pallas_call(
        kernel,
        out_shape=(
            jax.ShapeDtypeStruct((4, 8, W), f32),
            jax.ShapeDtypeStruct((4, 8, W), f32),
            jax.ShapeDtypeStruct((W, W), f32),
        ),
        in_specs=[smem, smem, vmem, vmem, remain, remain, remain, remain, remain],
        out_specs=[vmem, vmem, vmem],
        scratch_shapes=[
            pltpu.VMEM((W, W), f32),
            pltpu.VMEM(field, f32),
            pltpu.VMEM((W, W), f32),
            pltpu.VMEM(right.shape, bf16),
            pltpu.VMEM(left.shape, bf16),
            pltpu.VMEM(field, f32),
            pltpu.VMEM(field, f32),
            pltpu.VMEM(field, f32),
            pltpu.VMEM(held_shape, f32),
            pltpu.VMEM(held_shape, f32),
            pltpu.VMEM(blocks_shape, f32),
            pltpu.VMEM(blocks_shape, f32),
            pltpu.VMEM(window_shape, f32),
            pltpu.VMEM(window_shape, f32),
            pltpu.VMEM(window_shape, f32),
            pltpu.VMEM(blocks_shape, f32),
            pltpu.VMEM(held_shape, f32),
            pltpu.VMEM((4, 4, 8, W), f32),
            pltpu.VMEM((4, 4, 8, W), f32),
            dma((5,)),
            dma((2, close)),
            dma((2, close)),
            dma((2, close)),
            dma((2, close)),
            dma((2, 8)),
            dma((2, 16)),
            dma((2, 8)),
            dma((2, 16)),
            dma((2, 16)),
            dma((2, 8)),
            dma((2, close)),
            dma((2, close)),
        ],
        compiler_params=pltpu.CompilerParams(
            has_side_effects=True, vmem_limit_bytes=VMEM_LIMIT, collective_id=0
        ),
        name="iterate",
    )(
        offsets[0, 0],
        entry_counts,
        rows,
        momentum.reshape(4, 8, W),
        measured[0, 0, 0],
        illumination,
        slab_phase,
        right,
        left,
    )
    return (
        new_rows.reshape(2, 2, 8, W),
        new_momentum.reshape(2, 2, 8, W),
        amplitude[None, None, None],
    )


def solution(mesh):
    rows = P(None, None, ("ty", "pos"), "tx")
    slots = P("ty", "tx", "pos", None, None)
    return jax.shard_map(
        shards,
        mesh=mesh,
        in_specs=(rows, rows, slots, P(), P(), P("ty", "tx", None, None), P("ty", "tx")),
        out_specs=(rows, rows, slots),
        check_vma=False,
    )
```

```python
import functools
import math

import jax
import jax.numpy as jnp
import numpy as np
from jax import lax
from jax.experimental import pallas as pl
from jax.experimental.pallas import tpu as pltpu
from jax.sharding import PartitionSpec as P

f32 = jnp.float32
bf16 = jnp.bfloat16
MESH = pl.DeviceIdType.MESH
magnitude_floor = 0.5
momentum_rate = 0.9
step_length = 0.05
W = 256
MARGIN = 64
ROLES = [(s, h, k) for s in range(2) for h in range(2) for k in range(3) if (s, h, k) != (0, 0, 0)]
VMEM_LIMIT = 60 * 1024 * 1024


def tables(length):
    half = length // 2
    place = np.arange(half)

    def halves(value):
        value = value.astype(np.float32)
        high = value.astype(jnp.bfloat16)
        low = (value - high.astype(np.float32)).astype(jnp.bfloat16)
        return np.stack([high, low])

    right = []
    for direction in (-1.0, 1.0):
        for odd in (0, 1):
            turns = (place[:, None] * (2 * place[None, :] + odd)) % length
            if direction > 0:
                turns = turns.T
            angles = turns * (direction * 2.0 * math.pi / length)
            c = np.cos(angles) / math.sqrt(length)
            s = np.sin(angles) / math.sqrt(length)
            right.append(halves(np.block([[c, s], [-s, c]])))
    right = np.stack(right).reshape(2, 2, 2, length, length)
    left = right.swapaxes(3, 4)
    order = np.zeros((length, length))
    order[np.arange(length), np.concatenate([2 * place, 2 * place + 1])] = 1.0
    return right, np.ascontiguousarray(left), np.stack([order, order.T]).astype(jnp.bfloat16)


def coordinates():
    ty = lax.axis_index("ty")
    tx = lax.axis_index("tx")
    pos = lax.axis_index("pos")
    return ty, tx, pos, pos // 8, (pos // 4) % 2, pos % 4


def peer(ty, tx, pos):
    return {"ty": ty, "tx": tx, "pos": pos}


def position(y, zh, x):
    return y * 8 + zh * 4 + x


def close_peer(role, outward):
    s, h, k = role
    ty, tx, pos, y, zh, x = coordinates()
    step = (0, 3, 1)[k] if outward else (0, 1, 3)[k]
    other_ty = 1 - ty if s else ty
    other_zh = 1 - zh if h else zh
    return other_ty, (tx + step) % 4, other_zh, position(y, other_zh, x)


def has_role(role, y_pair, tx_lower, tx_upper):
    s, h, k = role
    terms = ([y_pair] if s else []) + [[], [tx_lower], [tx_upper]][k]
    return functools.reduce(jnp.logical_and, terms) if terms else None


def when(condition, body):
    if condition is None:
        body()
    else:
        pl.when(condition)(body)


def enter():
    ty, tx, pos, y, zh, x = coordinates()
    barrier = pltpu.get_barrier_semaphore()
    outer = (y == 0) | (y == 3)
    for role in ROLES:
        other_ty, other_tx, _, other_pos = close_peer(role, True)

        def signal(other_ty=other_ty, other_tx=other_tx, other_pos=other_pos):
            pl.semaphore_signal(barrier, inc=1, device_id=peer(other_ty, other_tx, other_pos), device_id_type=MESH)

        when(has_role(role, outer, tx > 0, tx < 3), signal)
    near = jnp.where((tx == 0) | (tx == 3), 4, 6) * jnp.where(outer, 2, 1) - 1
    me = y * 4 + x
    small = (y % 2) * 4 + x

    def greet(start, count, modulus):
        def body(j, carry):
            t = (start + j) % modulus
            pl.semaphore_signal(
                barrier, inc=1, device_id=peer(ty, tx, position(t // 4, zh, t % 4)), device_id_type=MESH
            )
            return carry

        lax.fori_loop(0, count, body, 0)

    @pl.when((y < 2) | (ty == 1))
    def _():
        greet(me + 1, 15, 16)
        pl.semaphore_wait(barrier, near + 15)

    @pl.when((y >= 2) & (ty == 0))
    def _():
        greet(small, 8, 8)
        pl.semaphore_wait(barrier, near + 8)


def turned_row(y, turned):
    return y + turned * (3 - 2 * y)


def sibling_facts():
    ty, tx, pos, y, zh, x = coordinates()
    takes = ((ty == 0) & (y == 0)) | ((ty == 1) & (y == 3))
    gives = ((ty == 1) & (y == 0)) | ((ty == 0) & (y == 3))
    return takes, gives


def close_copy(index, role, piece, src, held, send_sem, recv_sem):
    ty, tx, pos, y, zh, x = coordinates()
    k = role[2]
    layers = pl.ds(2 * piece, 2)
    other_ty, other_tx, _, other_pos = close_peer(role, True)
    if k == 0:
        source, target = src.at[layers], held.at[ty, 0, layers, zh]
    else:
        lanes = pl.ds(128 * (k - 1), 128)
        source, target = src.at[layers, :, lanes], held.at[ty, 1, layers, zh, :, lanes]
    return pltpu.make_async_remote_copy(
        src_ref=source,
        dst_ref=target,
        send_sem=send_sem.at[piece, index],
        recv_sem=recv_sem.at[piece, index],
        device_id=peer(other_ty, other_tx, other_pos),
        device_id_type=MESH,
    )


def close_start(piece, src, held, send_sem, recv_sem):
    ty, tx, pos, y, zh, x = coordinates()
    takes, gives = sibling_facts()
    for half in (1, 0):
        for index, role in enumerate(ROLES):
            if role[1] == half:
                copy = close_copy(index, role, piece, src, held, send_sem, recv_sem)
                when(has_role(role, gives, tx > 0, tx < 3), copy.start)
    for layer in (2 * piece, 2 * piece + 1):
        held[ty, 0, layer, zh] = src[layer]


def close_wait(piece, half, src, held, send_sem, recv_sem):
    ty, tx, pos, y, zh, x = coordinates()
    takes, gives = sibling_facts()
    for index, role in enumerate(ROLES):
        if role[1] != half:
            continue
        copy = close_copy(index, role, piece, src, held, send_sem, recv_sem)
        when(has_role(role, takes, tx < 3, tx > 0), copy.wait_recv)


def close_drain(piece, src, held, send_sem, recv_sem):
    ty, tx, pos, y, zh, x = coordinates()
    takes, gives = sibling_facts()
    for index, role in enumerate(ROLES):
        copy = close_copy(index, role, piece, src, held, send_sem, recv_sem)
        when(has_role(role, gives, tx > 0, tx < 3), copy.wait_send)


def clear_missing(held):
    ty, tx, pos, y, zh, x = coordinates()
    takes, gives = sibling_facts()
    nothing = jnp.zeros((4, 2, 8, 128), f32)

    @pl.when(jnp.logical_not(takes))
    def _():
        for kind in range(2):
            held[1 - ty, kind] = jnp.zeros((4, 2, 8, W), f32)

    @pl.when(tx == 3)
    def _():
        for core in range(2):
            held[core, 1, :, :, :, 0:128] = nothing

    @pl.when(tx == 0)
    def _():
        for core in range(2):
            held[core, 1, :, :, :, 128:256] = nothing


def row_swap(row_start, zh):
    ty, tx, pos, y, _, x = coordinates()
    row = y * 64 + zh * 32 + x * 8 + lax.broadcasted_iota(jnp.int32, (8, W), 0)
    return ((row < MARGIN) & (row_start > row + MARGIN)) | ((row >= 192) & (row > row_start + 191))


def column_swap(column_start):
    column = lax.broadcasted_iota(jnp.int32, (8, W), 1)
    return ((column < MARGIN) & (column_start > column + MARGIN)) | (
        (column >= 192) & (column > column_start + 191)
    )


def far_copy(j, piece, rows, turned, blocks, window, send_sem, recv_sem):
    ty, tx, pos, y, zh, x = coordinates()
    t = ((turned_row(y, turned) % 2) * 4 + x + j) % 8
    layers = pl.ds(2 * piece, 2)
    if rows is None:
        source, target = blocks.at[piece, j], window.at[layers, pl.ds(2 * y, 2), x]
    else:
        source, target = blocks.at[piece, j, :, rows], window.at[layers, 2 * y + rows, x]
    return pltpu.make_async_remote_copy(
        src_ref=source,
        dst_ref=target,
        send_sem=send_sem.at[piece, j],
        recv_sem=recv_sem.at[piece, y * 4 + x],
        device_id=peer(ty, tx, position(turned_row(t // 4, turned), zh, t % 4)),
        device_id_type=MESH,
    )


def far_start(piece, half, turned, offsets, held, *far):
    ty, tx, pos, y, zh, x = coordinates()
    blocks, window = far[:2]
    rows = 1 - zh if half else zh
    slot_row = turned_row(y, turned)
    for j in range(8):
        t = ((slot_row % 2) * 4 + x + j) % 8
        target = position(t // 4, zh, t % 4)
        swap_rows = row_swap(offsets[0, target], rows)
        swap_columns = column_swap(offsets[1, target])
        for part in range(2):
            layer = 2 * piece + part
            own = jnp.where(swap_columns, held[ty, 1, layer, rows], held[ty, 0, layer, rows])
            sibling = jnp.where(swap_columns, held[1 - ty, 1, layer, rows], held[1 - ty, 0, layer, rows])
            blocks[piece, j, part, rows] = jnp.where(swap_rows, sibling, own)
        if j == 0:

            @pl.when(slot_row >= 2)
            def _():
                far_copy(0, piece, rows, turned, *far).start()

            @pl.when(slot_row < 2)
            def _():
                for part in range(2):
                    window[2 * piece + part, 2 * y + rows, x] = blocks[piece, 0, part, rows]

        else:
            far_copy(j, piece, rows, turned, *far).start()


def far_wait(piece, blocks, window, send_sem, recv_sem):
    ty, tx, pos, y, zh, x = coordinates()

    def arrive(j, carry):
        s = (y * 4 + x + j) % 16
        pltpu.make_async_remote_copy(
            src_ref=blocks.at[piece, 0],
            dst_ref=window.at[pl.ds(2 * piece, 2), pl.ds(2 * (s // 4), 2), s % 4],
            send_sem=send_sem.at[piece, 0],
            recv_sem=recv_sem.at[piece, s],
            device_id=peer(ty, tx, position(s // 4, zh, s % 4)),
            device_id_type=MESH,
        ).wait_recv()
        return carry

    lax.fori_loop(1, 16, arrive, 0)


def far_drain(piece, turned, *far):
    ty, tx, pos, y, zh, x = coordinates()

    @pl.when(turned_row(y, turned) >= 2)
    def _():
        far_copy(0, piece, None, turned, *far).wait_send()

    for j in range(1, 8):
        far_copy(j, piece, None, turned, *far).wait_send()


def return_copy(j, piece, gradient, arrived, send_sem, recv_sem):
    ty, tx, pos, y, zh, x = coordinates()
    t = (y * 4 + x + j) % 16
    slot = (turned_row(y, ty) % 2) * 4 + x
    return pltpu.make_async_remote_copy(
        src_ref=gradient.at[pl.ds(2 * piece, 2), pl.ds(2 * (t // 4), 2), t % 4],
        dst_ref=arrived.at[piece, slot],
        send_sem=send_sem.at[piece, j],
        recv_sem=recv_sem.at[piece, slot],
        device_id=peer(ty, tx, position(t // 4, zh, t % 4)),
        device_id_type=MESH,
    )


def return_start(piece, gradient, arrived, send_sem, recv_sem):
    ty, tx, pos, y, zh, x = coordinates()
    slot = (turned_row(y, ty) % 2) * 4 + x

    def leave(j, carry):
        return_copy(j, piece, gradient, arrived, send_sem, recv_sem).start()
        return carry

    lax.fori_loop(1, 16, leave, 0)
    for part in range(2):
        arrived[piece, slot, part] = gradient[2 * piece + part, pl.ds(2 * y, 2), x]


def return_wait(piece, gradient, arrived, send_sem, recv_sem):
    ty, tx, pos, y, zh, x = coordinates()
    slot_row = turned_row(y, ty)
    base = (slot_row % 2) * 4 + x

    def wait_for(s):
        pltpu.make_async_remote_copy(
            src_ref=gradient.at[pl.ds(2 * piece, 2), pl.ds(0, 2), 0],
            dst_ref=arrived.at[piece, s],
            send_sem=send_sem.at[piece, 0],
            recv_sem=recv_sem.at[piece, s],
            device_id=peer(ty, tx, position(turned_row(s // 4, ty), zh, s % 4)),
            device_id_type=MESH,
        ).wait_recv()

    @pl.when(slot_row >= 2)
    def _():
        wait_for(base)

    for j in range(1, 8):
        wait_for((base + j) % 8)


def return_drain(piece, gradient, arrived, send_sem, recv_sem):
    def left(j, carry):
        return_copy(j, piece, gradient, arrived, send_sem, recv_sem).wait_send()
        return carry

    lax.fori_loop(1, 16, left, 0)


def add_returned(piece, offsets, arrived, sums):
    ty, tx, pos, y, zh, x = coordinates()
    for rows in range(2):
        totals = [[jnp.zeros((8, W), f32)] * 4 for _ in range(2)]
        for j in range(8):
            target = position(j // 4, zh, j % 4)
            swap_rows = row_swap(offsets[0, target], rows)
            swap_columns = column_swap(offsets[1, target])
            for part in range(2):
                block = arrived[piece, j, part, rows]
                mine = jnp.where(swap_rows, 0.0, block)
                theirs = jnp.where(swap_rows, block, 0.0)
                own, own_side, sibling, sibling_side = totals[part]
                totals[part] = [
                    own + jnp.where(swap_columns, 0.0, mine),
                    own_side + jnp.where(swap_columns, mine, 0.0),
                    sibling + jnp.where(swap_columns, 0.0, theirs),
                    sibling_side + jnp.where(swap_columns, theirs, 0.0),
                ]
        for part in range(2):
            layer = 2 * piece + part
            sums[ty, 0, layer, rows] = totals[part][0]
            sums[ty, 1, layer, rows] = totals[part][1]
            sums[1 - ty, 0, layer, rows] = totals[part][2]
            sums[1 - ty, 1, layer, rows] = totals[part][3]


def sum_copy(index, role, piece, sums, parts_own, parts_side, send_sem, recv_sem):
    s, h, k = role
    layers = pl.ds(2 * piece, 2)
    other_ty, other_tx, other_zh, other_pos = close_peer(role, False)
    if k == 0:
        source, target = sums.at[other_ty, 0, layers, other_zh], parts_own.at[2 * s + h, layers]
    else:
        lanes = pl.ds(128 * (k - 1), 128)
        source = sums.at[other_ty, 1, layers, other_zh, :, lanes]
        target = parts_side.at[2 * s + h, layers, :, lanes]
    return pltpu.make_async_remote_copy(
        src_ref=source,
        dst_ref=target,
        send_sem=send_sem.at[piece, index],
        recv_sem=recv_sem.at[piece, index],
        device_id=peer(other_ty, other_tx, other_pos),
        device_id_type=MESH,
    )


def sum_each(piece, action, *refs):
    ty, tx, pos, y, zh, x = coordinates()
    takes, gives = sibling_facts()
    for index, role in enumerate(ROLES):
        copy = sum_copy(index, role, piece, *refs)
        if action == "recv":
            when(has_role(role, gives, tx > 0, tx < 3), copy.wait_recv)
        else:
            act = copy.start if action == "start" else copy.wait_send
            when(has_role(role, takes, tx < 3, tx > 0), act)


def clear_parts(parts_own, parts_side):
    ty, tx, pos, y, zh, x = coordinates()
    takes, gives = sibling_facts()
    nothing = jnp.zeros((4, 8, 128), f32)

    @pl.when(jnp.logical_not(gives))
    def _():
        for part in (2, 3):
            parts_own[part] = jnp.zeros((4, 8, W), f32)
            parts_side[part] = jnp.zeros((4, 8, W), f32)

    @pl.when(tx == 0)
    def _():
        for part in range(4):
            parts_side[part, :, :, 0:128] = nothing

    @pl.when(tx == 3)
    def _():
        for part in range(4):
            parts_side[part, :, :, 128:256] = nothing


def split(value):
    high = value.astype(bf16)
    return high, (value - high.astype(f32)).astype(bf16)


def product(left, right):
    return jnp.dot(left, right, preferred_element_type=f32)


def from_right(value, table):
    high, low = split(value)
    return product(high, table[0]) + product(low, table[0]) + product(high, table[1])


def from_left(table, value):
    high, low = split(value)
    return product(table[0], high) + product(table[0], low) + product(table[1], high)


def transform(real_part, imag_part, right, left):
    join = jnp.concatenate
    h = W // 2
    a, b, c, d = real_part[:, :h], real_part[:, h:], imag_part[:, :h], imag_part[:, h:]
    even = from_right(join([a + b, c + d], 1), right[0, 0])
    odd = from_right(join([a - b, c - d], 1), right[0, 1])
    real_part, imag_part = join([even[:, :h], odd[:, :h]], 1), join([even[:, h:], odd[:, h:]], 1)
    a, b, c, d = real_part[:h], real_part[h:], imag_part[:h], imag_part[h:]
    even = from_left(left[0, 0], join([a + b, c + d], 0))
    odd = from_left(left[0, 1], join([a - b, c - d], 0))
    return join([even[:h], odd[:h]], 0), join([even[h:], odd[h:]], 0)


def inverse(real_part, imag_part, right, left):
    join = jnp.concatenate
    h = W // 2
    even = from_right(join([real_part[:, :h], imag_part[:, :h]], 1), right[1, 0])
    odd = from_right(join([real_part[:, h:], imag_part[:, h:]], 1), right[1, 1])
    total, rest = even + odd, even - odd
    real_part, imag_part = join([total[:, :h], rest[:, :h]], 1), join([total[:, h:], rest[:, h:]], 1)
    even = from_left(left[1, 0], join([real_part[:h], imag_part[:h]], 0))
    odd = from_left(left[1, 1], join([real_part[h:], imag_part[h:]], 0))
    total, rest = even + odd, even - odd
    return join([total[:h], rest[:h]], 0), join([total[h:], rest[h:]], 0)


def parts_of(value, count):
    parts = []
    for _ in range(count):
        parts.append(value.astype(bf16))
        value = value - parts[-1].astype(f32)
    return parts


def reordered(value, first, second, count):
    value = sum(product(first, part) for part in parts_of(value, count))
    return sum(product(part, second) for part in parts_of(value, count))


def complex_product(first_real, first_imag, second_real, second_imag):
    return (
        first_real * second_real - first_imag * second_imag,
        first_real * second_imag + first_imag * second_real,
    )


def shifted_probe(offsets, slot, illumination):
    down = (offsets[0, slot] + 192) % 256
    across = (offsets[1, slot] + 192) % 256
    return [pltpu.roll(pltpu.roll(illumination[part], down, 0), across, 1) for part in range(2)]


def layer_of(window, layer):
    return window[layer].reshape(W, W)


def between_field(window, probe, slab, right, left):
    entering = complex_product(probe[0], probe[1], layer_of(window, 0), layer_of(window, 1))
    spectrum = transform(entering[0], entering[1], right, left)
    spectrum = complex_product(spectrum[0], spectrum[1], slab[0], slab[1])
    return inverse(spectrum[0], spectrum[1], right, left)


def farfield_of(between, window, right, left):
    leaving = complex_product(between[0], between[1], layer_of(window, 2), layer_of(window, 3))
    return transform(leaving[0], leaving[1], right, left)


def kernel(
    offsets,
    counts,
    rows,
    momentum,
    measured_hbm,
    illumination_hbm,
    phase_hbm,
    right_hbm,
    left_hbm,
    order_hbm,
    new_rows,
    new_momentum,
    amplitude,
    measured,
    illumination,
    phase,
    right,
    left,
    order,
    ordered_measured,
    probe,
    slab,
    between_kept,
    held_first,
    held_second,
    blocks_first,
    blocks_second,
    window_first,
    window_second,
    gradient,
    arrived,
    sums,
    parts_own,
    parts_side,
    local_sem,
    measured_sem,
    close_send_first,
    close_recv_first,
    close_send_second,
    close_recv_second,
    far_send_first,
    far_recv_first,
    far_send_second,
    far_recv_second,
    return_send,
    return_recv,
    sum_send,
    sum_recv,
):
    ty, tx, pos, y, zh, x = coordinates()
    loads = [
        pltpu.make_async_copy(source, target, local_sem.at[n])
        for n, (source, target) in enumerate(
            (
                (phase_hbm, phase),
                (illumination_hbm, illumination),
                (right_hbm, right),
                (order_hbm, order),
                (left_hbm, left),
                (measured_hbm, measured),
            )
        )
    ]

    works = (y < 2) | (ty == 1)
    slot_row = jnp.where(y < 2, y, 3 - y)
    slot = position(slot_row, zh, x)

    @pl.when(works)
    def _():
        for load in loads:
            load.start()

    clear_missing(held_first)
    clear_missing(held_second)
    clear_parts(parts_own, parts_side)
    enter()
    close_first = (rows, held_first, close_send_first, close_recv_first)
    close_second = (new_rows, held_second, close_send_second, close_recv_second)
    far_first = (blocks_first, window_first, far_send_first, far_recv_first)
    far_second = (blocks_second, window_second, far_send_second, far_recv_second)
    returned = (gradient, arrived, return_send, return_recv)
    summed = (sums, parts_own, parts_side, sum_send, sum_recv)
    for piece in (0, 1):
        close_start(piece, *close_first)
    for half in (0, 1):
        for piece in (0, 1):
            close_wait(piece, half, *close_first)
            far_start(piece, half, ty, offsets, held_first, *far_first)
    live = jnp.where(slot < counts[0, 0], 1.0, 0.0)
    move_measured = pltpu.make_async_remote_copy(
        src_ref=ordered_measured,
        dst_ref=ordered_measured,
        send_sem=measured_sem.at[0],
        recv_sem=measured_sem.at[1],
        device_id=peer(ty, tx, position(3 - y, zh, x)),
        device_id_type=MESH,
    )

    @pl.when(works)
    def _():
        for load in loads:
            load.wait()

    @pl.when(y < 2)
    def _():
        ordered_measured[...] = reordered(measured[...], order[0], order[1], 3)

    @pl.when((y < 2) & (ty == 1))
    def _():
        move_measured.start()

    @pl.when(works)
    def _():
        angles = reordered(phase[...], order[0], order[1], 3)
        slab[0] = jnp.cos(angles)
        slab[1] = jnp.sin(angles)
        shifted = shifted_probe(offsets, slot, illumination)
        probe[0] = shifted[0]
        probe[1] = shifted[1]

    @pl.when(turned_row(y, ty) < 2)
    def _():
        far_wait(0, *far_first)
        between = between_field(window_first, probe, slab, right, left)
        between_kept[0] = between[0]
        between_kept[1] = between[1]
        far_wait(1, *far_first)
        farfield = farfield_of(between, window_first, right, left)
        magnitude = jnp.sqrt(farfield[0] * farfield[0] + farfield[1] * farfield[1])

        @pl.when(ty == 1)
        def _():
            move_measured.wait_recv()

        keeping = (1.0 - ordered_measured[...] / jnp.maximum(magnitude, magnitude_floor)) * live
        backward = inverse(farfield[0] * keeping, farfield[1] * keeping, right, left)
        grad_second = complex_product(between_kept[0], -between_kept[1], backward[0], backward[1])
        gradient[2] = grad_second[0].reshape(8, 4, 8, W)
        gradient[3] = grad_second[1].reshape(8, 4, 8, W)
        return_start(1, *returned)
        toward = complex_product(layer_of(window_first, 2), -layer_of(window_first, 3), backward[0], backward[1])
        spectrum = transform(toward[0], toward[1], right, left)
        spectrum = complex_product(spectrum[0], spectrum[1], slab[0], -slab[1])
        incoming = inverse(spectrum[0], spectrum[1], right, left)
        grad_first = complex_product(probe[0], -probe[1], incoming[0], incoming[1])
        gradient[0] = grad_first[0].reshape(8, 4, 8, W)
        gradient[1] = grad_first[1].reshape(8, 4, 8, W)
        return_start(0, *returned)

    for piece in (1, 0):
        return_wait(piece, *returned)
        add_returned(piece, offsets, arrived, sums)
        sum_each(piece, "start", *summed)
        sum_each(piece, "recv", *summed)
        for layer in (2 * piece, 2 * piece + 1):
            total = sums[ty, 0, layer, zh]
            for part in range(4):
                if part:
                    total = total + parts_own[part, layer]
                total = total + parts_side[part, layer]
            velocity = momentum_rate * momentum[layer] + total
            new_momentum[layer] = velocity
            new_rows[layer] = rows[layer] - step_length * velocity
        close_start(piece, *close_second)
        for half in (0, 1):
            close_wait(piece, half, *close_second)
            far_start(piece, half, 0, offsets, held_second, *far_second)

    @pl.when(y < 2)
    def _():
        far_wait(0, *far_second)
        between = between_field(window_second, probe, slab, right, left)
        far_wait(1, *far_second)
        farfield = farfield_of(between, window_second, right, left)
        magnitude = jnp.sqrt(farfield[0] * farfield[0] + farfield[1] * farfield[1]) * live
        amplitude[...] = reordered(magnitude, order[1], order[0], 2)

    @pl.when(y >= 2)
    def _():
        amplitude[...] = jnp.zeros_like(amplitude)

    for piece in (0, 1):
        close_drain(piece, *close_first)
        close_drain(piece, *close_second)
        far_drain(piece, ty, *far_first)
        far_drain(piece, 0, *far_second)
        sum_each(piece, "sent", *summed)

    @pl.when(turned_row(y, ty) < 2)
    def _():
        for piece in (0, 1):
            return_drain(piece, *returned)

    @pl.when((y < 2) & (ty == 1))
    def _():
        move_measured.wait_send()


def shards(object_field, momentum, measured, illumination, slab_phase, offsets, entry_counts):
    rows = object_field.reshape(4, 8, W)
    right, left, order = (jnp.asarray(t) for t in tables(W))
    dma = pltpu.SemaphoreType.DMA
    close = len(ROLES)
    window_shape = (4, 8, 4, 8, W)
    held_shape = (2, 2, 4, 2, 8, W)
    blocks_shape = (2, 8, 2, 2, 8, W)
    field = (2, W, W)
    vmem = pl.BlockSpec(memory_space=pltpu.VMEM)
    smem = pl.BlockSpec(memory_space=pltpu.SMEM)
    remain = pl.BlockSpec(memory_space=pl.ANY)
    new_rows, new_momentum, amplitude = pl.pallas_call(
        kernel,
        out_shape=(
            jax.ShapeDtypeStruct((4, 8, W), f32),
            jax.ShapeDtypeStruct((4, 8, W), f32),
            jax.ShapeDtypeStruct((W, W), f32),
        ),
        in_specs=[smem, smem, vmem, vmem, remain, remain, remain, remain, remain, remain],
        out_specs=[vmem, vmem, vmem],
        scratch_shapes=[
            pltpu.VMEM((W, W), f32),
            pltpu.VMEM(field, f32),
            pltpu.VMEM((W, W), f32),
            pltpu.VMEM(right.shape, bf16),
            pltpu.VMEM(left.shape, bf16),
            pltpu.VMEM(order.shape, bf16),
            pltpu.VMEM((W, W), f32),
            pltpu.VMEM(field, f32),
            pltpu.VMEM(field, f32),
            pltpu.VMEM(field, f32),
            pltpu.VMEM(held_shape, f32),
            pltpu.VMEM(held_shape, f32),
            pltpu.VMEM(blocks_shape, f32),
            pltpu.VMEM(blocks_shape, f32),
            pltpu.VMEM(window_shape, f32),
            pltpu.VMEM(window_shape, f32),
            pltpu.VMEM(window_shape, f32),
            pltpu.VMEM(blocks_shape, f32),
            pltpu.VMEM(held_shape, f32),
            pltpu.VMEM((4, 4, 8, W), f32),
            pltpu.VMEM((4, 4, 8, W), f32),
            dma((6,)),
            dma((2,)),
            dma((2, close)),
            dma((2, close)),
            dma((2, close)),
            dma((2, close)),
            dma((2, 8)),
            dma((2, 16)),
            dma((2, 8)),
            dma((2, 16)),
            dma((2, 16)),
            dma((2, 8)),
            dma((2, close)),
            dma((2, close)),
        ],
        compiler_params=pltpu.CompilerParams(
            has_side_effects=True, vmem_limit_bytes=VMEM_LIMIT, collective_id=0
        ),
        name="iterate",
    )(
        offsets[0, 0].T,
        entry_counts,
        rows,
        momentum.reshape(4, 8, W),
        measured[0, 0, 0],
        illumination,
        slab_phase,
        right,
        left,
        order,
    )
    return (
        new_rows.reshape(2, 2, 8, W),
        new_momentum.reshape(2, 2, 8, W),
        amplitude[None, None, None],
    )


def solution(mesh):
    rows = P(None, None, ("ty", "pos"), "tx")
    slots = P("ty", "tx", "pos", None, None)
    return jax.shard_map(
        shards,
        mesh=mesh,
        in_specs=(rows, rows, slots, P(), P(), P("ty", "tx", None, None), P("ty", "tx")),
        out_specs=(rows, rows, slots),
        check_vma=False,
    )
```

```python
import functools
import math

import jax
import jax.numpy as jnp
import numpy as np
from jax import lax
from jax.experimental import pallas as pl
from jax.experimental.pallas import tpu as pltpu
from jax.sharding import PartitionSpec as P

f32 = jnp.float32
bf16 = jnp.bfloat16
MESH = pl.DeviceIdType.MESH
magnitude_floor = 0.5
momentum_rate = 0.9
step_length = 0.05
W = 256
MARGIN = 64
ROLES = [(s, h, k) for s in range(2) for h in range(2) for k in range(3) if (s, h, k) != (0, 0, 0)]
VMEM_LIMIT = 60 * 1024 * 1024


def tables(length):
    half = length // 2
    place = np.arange(half)

    def halves(value):
        value = value.astype(np.float32)
        high = value.astype(jnp.bfloat16)
        low = (value - high.astype(np.float32)).astype(jnp.bfloat16)
        return np.stack([high, low])

    right = []
    for direction in (-1.0, 1.0):
        for odd in (0, 1):
            turns = (place[:, None] * (2 * place[None, :] + odd)) % length
            if direction > 0:
                turns = turns.T
            angles = turns * (direction * 2.0 * math.pi / length)
            c = np.cos(angles) / math.sqrt(length)
            s = np.sin(angles) / math.sqrt(length)
            right.append(halves(np.block([[c, s], [-s, c]])))
    right = np.stack(right).reshape(2, 2, 2, length, length)
    left = right.swapaxes(3, 4)
    order = np.zeros((length, length))
    order[np.arange(length), np.concatenate([2 * place, 2 * place + 1])] = 1.0
    return right, np.ascontiguousarray(left), np.stack([order, order.T]).astype(jnp.bfloat16)


def coordinates():
    ty = lax.axis_index("ty")
    tx = lax.axis_index("tx")
    pos = lax.axis_index("pos")
    return ty, tx, pos, pos // 8, (pos // 4) % 2, pos % 4


def peer(ty, tx, pos):
    return {"ty": ty, "tx": tx, "pos": pos}


def position(y, zh, x):
    return y * 8 + zh * 4 + x


def close_peer(role, outward):
    s, h, k = role
    ty, tx, pos, y, zh, x = coordinates()
    step = (0, 3, 1)[k] if outward else (0, 1, 3)[k]
    other_ty = 1 - ty if s else ty
    other_zh = 1 - zh if h else zh
    return other_ty, (tx + step) % 4, other_zh, position(y, other_zh, x)


def has_role(role, y_pair, tx_lower, tx_upper):
    s, h, k = role
    terms = ([y_pair] if s else []) + [[], [tx_lower], [tx_upper]][k]
    return functools.reduce(jnp.logical_and, terms) if terms else None


def when(condition, body):
    if condition is None:
        body()
    else:
        pl.when(condition)(body)


def enter():
    ty, tx, pos, y, zh, x = coordinates()
    barrier = pltpu.get_barrier_semaphore()
    outer = (y == 0) | (y == 3)
    for role in ROLES:
        other_ty, other_tx, _, other_pos = close_peer(role, True)

        def signal(other_ty=other_ty, other_tx=other_tx, other_pos=other_pos):
            pl.semaphore_signal(barrier, inc=1, device_id=peer(other_ty, other_tx, other_pos), device_id_type=MESH)

        when(has_role(role, outer, tx > 0, tx < 3), signal)
    near = jnp.where((tx == 0) | (tx == 3), 4, 6) * jnp.where(outer, 2, 1) - 1
    me = y * 4 + x
    small = (y % 2) * 4 + x

    def greet(start, count, modulus):
        def body(j, carry):
            t = (start + j) % modulus
            pl.semaphore_signal(
                barrier, inc=1, device_id=peer(ty, tx, position(t // 4, zh, t % 4)), device_id_type=MESH
            )
            return carry

        lax.fori_loop(0, count, body, 0)

    @pl.when((y < 2) | (ty == 1))
    def _():
        greet(me + 1, 15, 16)
        pl.semaphore_wait(barrier, near + 15)

    @pl.when((y >= 2) & (ty == 0))
    def _():
        greet(small, 8, 8)
        pl.semaphore_wait(barrier, near + 8)


def turned_row(y, turned):
    return y + turned * (3 - 2 * y)


def sibling_facts():
    ty, tx, pos, y, zh, x = coordinates()
    takes = ((ty == 0) & (y == 0)) | ((ty == 1) & (y == 3))
    gives = ((ty == 1) & (y == 0)) | ((ty == 0) & (y == 3))
    return takes, gives


def close_copy(index, role, piece, src, held, send_sem, recv_sem):
    ty, tx, pos, y, zh, x = coordinates()
    k = role[2]
    layers = pl.ds(2 * piece, 2)
    other_ty, other_tx, _, other_pos = close_peer(role, True)
    if k == 0:
        source, target = src.at[layers], held.at[ty, 0, layers, zh]
    else:
        lanes = pl.ds(128 * (k - 1), 128)
        source, target = src.at[layers, :, lanes], held.at[ty, 1, layers, zh, :, lanes]
    return pltpu.make_async_remote_copy(
        src_ref=source,
        dst_ref=target,
        send_sem=send_sem.at[piece, index],
        recv_sem=recv_sem.at[piece, index],
        device_id=peer(other_ty, other_tx, other_pos),
        device_id_type=MESH,
    )


def close_start(piece, src, held, send_sem, recv_sem):
    ty, tx, pos, y, zh, x = coordinates()
    takes, gives = sibling_facts()
    for half in (1, 0):
        for index, role in enumerate(ROLES):
            if role[1] == half:
                copy = close_copy(index, role, piece, src, held, send_sem, recv_sem)
                when(has_role(role, gives, tx > 0, tx < 3), copy.start)
    for layer in (2 * piece, 2 * piece + 1):
        held[ty, 0, layer, zh] = src[layer]


def close_wait(piece, half, src, held, send_sem, recv_sem):
    ty, tx, pos, y, zh, x = coordinates()
    takes, gives = sibling_facts()
    for index, role in enumerate(ROLES):
        if role[1] != half:
            continue
        copy = close_copy(index, role, piece, src, held, send_sem, recv_sem)
        when(has_role(role, takes, tx < 3, tx > 0), copy.wait_recv)


def close_drain(piece, src, held, send_sem, recv_sem):
    ty, tx, pos, y, zh, x = coordinates()
    takes, gives = sibling_facts()
    for index, role in enumerate(ROLES):
        copy = close_copy(index, role, piece, src, held, send_sem, recv_sem)
        when(has_role(role, gives, tx > 0, tx < 3), copy.wait_send)


def clear_missing(held):
    ty, tx, pos, y, zh, x = coordinates()
    takes, gives = sibling_facts()
    nothing = jnp.zeros((4, 2, 8, 128), f32)

    @pl.when(jnp.logical_not(takes))
    def _():
        for kind in range(2):
            held[1 - ty, kind] = jnp.zeros((4, 2, 8, W), f32)

    @pl.when(tx == 3)
    def _():
        for core in range(2):
            held[core, 1, :, :, :, 0:128] = nothing

    @pl.when(tx == 0)
    def _():
        for core in range(2):
            held[core, 1, :, :, :, 128:256] = nothing


def row_swap(row_start, zh):
    ty, tx, pos, y, _, x = coordinates()
    row = y * 64 + zh * 32 + x * 8 + lax.broadcasted_iota(jnp.int32, (8, W), 0)
    return ((row < MARGIN) & (row_start > row + MARGIN)) | ((row >= 192) & (row > row_start + 191))


def column_swap(column_start):
    column = lax.broadcasted_iota(jnp.int32, (8, W), 1)
    return ((column < MARGIN) & (column_start > column + MARGIN)) | (
        (column >= 192) & (column > column_start + 191)
    )


def far_copy(j, piece, rows, turned, blocks, window, send_sem, recv_sem):
    ty, tx, pos, y, zh, x = coordinates()
    t = ((turned_row(y, turned) % 2) * 4 + x + j) % 8
    layers = pl.ds(2 * piece, 2)
    if rows is None:
        source, target = blocks.at[piece, j], window.at[layers, pl.ds(2 * y, 2), x]
    else:
        source, target = blocks.at[piece, j, :, rows], window.at[layers, 2 * y + rows, x]
    return pltpu.make_async_remote_copy(
        src_ref=source,
        dst_ref=target,
        send_sem=send_sem.at[piece, j],
        recv_sem=recv_sem.at[piece, y * 4 + x],
        device_id=peer(ty, tx, position(turned_row(t // 4, turned), zh, t % 4)),
        device_id_type=MESH,
    )


def far_start(piece, half, turned, offsets, held, *far):
    ty, tx, pos, y, zh, x = coordinates()
    blocks, window = far[:2]
    rows = 1 - zh if half else zh
    slot_row = turned_row(y, turned)
    for j in range(8):
        t = ((slot_row % 2) * 4 + x + j) % 8
        target = position(t // 4, zh, t % 4)
        swap_rows = row_swap(offsets[0, target], rows)
        swap_columns = column_swap(offsets[1, target])
        for part in range(2):
            layer = 2 * piece + part
            own = jnp.where(swap_columns, held[ty, 1, layer, rows], held[ty, 0, layer, rows])
            sibling = jnp.where(swap_columns, held[1 - ty, 1, layer, rows], held[1 - ty, 0, layer, rows])
            blocks[piece, j, part, rows] = jnp.where(swap_rows, sibling, own)
        if j == 0:

            @pl.when(slot_row >= 2)
            def _():
                far_copy(0, piece, rows, turned, *far).start()

            @pl.when(slot_row < 2)
            def _():
                for part in range(2):
                    window[2 * piece + part, 2 * y + rows, x] = blocks[piece, 0, part, rows]

        else:
            far_copy(j, piece, rows, turned, *far).start()


def far_wait(piece, blocks, window, send_sem, recv_sem):
    ty, tx, pos, y, zh, x = coordinates()

    def arrive(j, carry):
        s = (y * 4 + x + j) % 16
        pltpu.make_async_remote_copy(
            src_ref=blocks.at[piece, 0],
            dst_ref=window.at[pl.ds(2 * piece, 2), pl.ds(2 * (s // 4), 2), s % 4],
            send_sem=send_sem.at[piece, 0],
            recv_sem=recv_sem.at[piece, s],
            device_id=peer(ty, tx, position(s // 4, zh, s % 4)),
            device_id_type=MESH,
        ).wait_recv()
        return carry

    lax.fori_loop(1, 16, arrive, 0)


def far_drain(piece, turned, *far):
    ty, tx, pos, y, zh, x = coordinates()

    @pl.when(turned_row(y, turned) >= 2)
    def _():
        far_copy(0, piece, None, turned, *far).wait_send()

    for j in range(1, 8):
        far_copy(j, piece, None, turned, *far).wait_send()


def return_copy(j, piece, gradient, arrived, send_sem, recv_sem):
    ty, tx, pos, y, zh, x = coordinates()
    t = (y * 4 + x + j) % 16
    slot = (turned_row(y, ty) % 2) * 4 + x
    return pltpu.make_async_remote_copy(
        src_ref=gradient.at[pl.ds(2 * piece, 2), pl.ds(2 * (t // 4), 2), t % 4],
        dst_ref=arrived.at[piece, slot],
        send_sem=send_sem.at[piece, j],
        recv_sem=recv_sem.at[piece, slot],
        device_id=peer(ty, tx, position(t // 4, zh, t % 4)),
        device_id_type=MESH,
    )


def return_start(piece, gradient, arrived, send_sem, recv_sem):
    ty, tx, pos, y, zh, x = coordinates()
    slot = (turned_row(y, ty) % 2) * 4 + x

    def leave(j, carry):
        return_copy(j, piece, gradient, arrived, send_sem, recv_sem).start()
        return carry

    lax.fori_loop(1, 16, leave, 0)
    for part in range(2):
        arrived[piece, slot, part] = gradient[2 * piece + part, pl.ds(2 * y, 2), x]


def return_wait(piece, gradient, arrived, send_sem, recv_sem):
    ty, tx, pos, y, zh, x = coordinates()
    slot_row = turned_row(y, ty)
    base = (slot_row % 2) * 4 + x

    def wait_for(s):
        pltpu.make_async_remote_copy(
            src_ref=gradient.at[pl.ds(2 * piece, 2), pl.ds(0, 2), 0],
            dst_ref=arrived.at[piece, s],
            send_sem=send_sem.at[piece, 0],
            recv_sem=recv_sem.at[piece, s],
            device_id=peer(ty, tx, position(turned_row(s // 4, ty), zh, s % 4)),
            device_id_type=MESH,
        ).wait_recv()

    @pl.when(slot_row >= 2)
    def _():
        wait_for(base)

    for j in range(1, 8):
        wait_for((base + j) % 8)


def return_drain(piece, gradient, arrived, send_sem, recv_sem):
    def left(j, carry):
        return_copy(j, piece, gradient, arrived, send_sem, recv_sem).wait_send()
        return carry

    lax.fori_loop(1, 16, left, 0)


def add_returned(piece, offsets, arrived, sums):
    ty, tx, pos, y, zh, x = coordinates()
    for rows in range(2):
        totals = [[jnp.zeros((8, W), f32)] * 4 for _ in range(2)]
        for j in range(8):
            target = position(j // 4, zh, j % 4)
            swap_rows = row_swap(offsets[0, target], rows)
            swap_columns = column_swap(offsets[1, target])
            for part in range(2):
                block = arrived[piece, j, part, rows]
                mine = jnp.where(swap_rows, 0.0, block)
                theirs = jnp.where(swap_rows, block, 0.0)
                own, own_side, sibling, sibling_side = totals[part]
                totals[part] = [
                    own + jnp.where(swap_columns, 0.0, mine),
                    own_side + jnp.where(swap_columns, mine, 0.0),
                    sibling + jnp.where(swap_columns, 0.0, theirs),
                    sibling_side + jnp.where(swap_columns, theirs, 0.0),
                ]
        for part in range(2):
            layer = 2 * piece + part
            sums[ty, 0, layer, rows] = totals[part][0]
            sums[ty, 1, layer, rows] = totals[part][1]
            sums[1 - ty, 0, layer, rows] = totals[part][2]
            sums[1 - ty, 1, layer, rows] = totals[part][3]


def sum_copy(index, role, piece, sums, parts_own, parts_side, send_sem, recv_sem):
    s, h, k = role
    layers = pl.ds(2 * piece, 2)
    other_ty, other_tx, other_zh, other_pos = close_peer(role, False)
    if k == 0:
        source, target = sums.at[other_ty, 0, layers, other_zh], parts_own.at[2 * s + h, layers]
    else:
        lanes = pl.ds(128 * (k - 1), 128)
        source = sums.at[other_ty, 1, layers, other_zh, :, lanes]
        target = parts_side.at[2 * s + h, layers, :, lanes]
    return pltpu.make_async_remote_copy(
        src_ref=source,
        dst_ref=target,
        send_sem=send_sem.at[piece, index],
        recv_sem=recv_sem.at[piece, index],
        device_id=peer(other_ty, other_tx, other_pos),
        device_id_type=MESH,
    )


def sum_each(piece, action, *refs):
    ty, tx, pos, y, zh, x = coordinates()
    takes, gives = sibling_facts()
    for index, role in enumerate(ROLES):
        copy = sum_copy(index, role, piece, *refs)
        if action == "recv":
            when(has_role(role, gives, tx > 0, tx < 3), copy.wait_recv)
        else:
            act = copy.start if action == "start" else copy.wait_send
            when(has_role(role, takes, tx < 3, tx > 0), act)


def clear_parts(parts_own, parts_side):
    ty, tx, pos, y, zh, x = coordinates()
    takes, gives = sibling_facts()
    nothing = jnp.zeros((4, 8, 128), f32)

    @pl.when(jnp.logical_not(gives))
    def _():
        for part in (2, 3):
            parts_own[part] = jnp.zeros((4, 8, W), f32)
            parts_side[part] = jnp.zeros((4, 8, W), f32)

    @pl.when(tx == 0)
    def _():
        for part in range(4):
            parts_side[part, :, :, 0:128] = nothing

    @pl.when(tx == 3)
    def _():
        for part in range(4):
            parts_side[part, :, :, 128:256] = nothing


def split(value):
    high = value.astype(bf16)
    return high, (value - high.astype(f32)).astype(bf16)


def product(left, right):
    return jnp.dot(left, right, preferred_element_type=f32)


def from_right(value, table):
    high, low = split(value)
    return product(high, table[0]) + product(low, table[0]) + product(high, table[1])


def from_left(table, value):
    high, low = split(value)
    return product(table[0], high) + product(table[0], low) + product(table[1], high)


def transform(real_part, imag_part, right, left):
    join = jnp.concatenate
    h = W // 2
    a, b, c, d = real_part[:, :h], real_part[:, h:], imag_part[:, :h], imag_part[:, h:]
    even = from_right(join([a + b, c + d], 1), right[0, 0])
    odd = from_right(join([a - b, c - d], 1), right[0, 1])
    real_part, imag_part = join([even[:, :h], odd[:, :h]], 1), join([even[:, h:], odd[:, h:]], 1)
    a, b, c, d = real_part[:h], real_part[h:], imag_part[:h], imag_part[h:]
    even = from_left(left[0, 0], join([a + b, c + d], 0))
    odd = from_left(left[0, 1], join([a - b, c - d], 0))
    return join([even[:h], odd[:h]], 0), join([even[h:], odd[h:]], 0)


def inverse(real_part, imag_part, right, left):
    join = jnp.concatenate
    h = W // 2
    even = from_right(join([real_part[:, :h], imag_part[:, :h]], 1), right[1, 0])
    odd = from_right(join([real_part[:, h:], imag_part[:, h:]], 1), right[1, 1])
    total, rest = even + odd, even - odd
    real_part, imag_part = join([total[:, :h], rest[:, :h]], 1), join([total[:, h:], rest[:, h:]], 1)
    even = from_left(left[1, 0], join([real_part[:h], imag_part[:h]], 0))
    odd = from_left(left[1, 1], join([real_part[h:], imag_part[h:]], 0))
    total, rest = even + odd, even - odd
    return join([total[:h], rest[:h]], 0), join([total[h:], rest[h:]], 0)


def parts_of(value, count):
    parts = []
    for _ in range(count):
        parts.append(value.astype(bf16))
        value = value - parts[-1].astype(f32)
    return parts


def reordered(value, first, second, count):
    value = sum(product(first, part) for part in parts_of(value, count))
    return sum(product(part, second) for part in parts_of(value, count))


def complex_product(first_real, first_imag, second_real, second_imag):
    return (
        first_real * second_real - first_imag * second_imag,
        first_real * second_imag + first_imag * second_real,
    )


def shifted_probe(offsets, slot, illumination):
    down = (offsets[0, slot] + 192) % 256
    across = (offsets[1, slot] + 192) % 256
    return [pltpu.roll(pltpu.roll(illumination[part], down, 0), across, 1) for part in range(2)]


def layer_of(window, layer):
    return window[layer].reshape(W, W)


def between_field(window, probe, slab, right, left):
    entering = complex_product(probe[0], probe[1], layer_of(window, 0), layer_of(window, 1))
    spectrum = transform(entering[0], entering[1], right, left)
    spectrum = complex_product(spectrum[0], spectrum[1], slab[0], slab[1])
    return inverse(spectrum[0], spectrum[1], right, left)


def farfield_of(between, window, right, left):
    leaving = complex_product(between[0], between[1], layer_of(window, 2), layer_of(window, 3))
    return transform(leaving[0], leaving[1], right, left)


def kernel(
    offsets,
    counts,
    rows,
    momentum,
    measured_hbm,
    illumination_hbm,
    phase_hbm,
    right_hbm,
    left_hbm,
    order_hbm,
    new_rows,
    new_momentum,
    amplitude,
    measured,
    illumination,
    phase,
    right,
    left,
    order,
    ordered_measured,
    probe,
    slab,
    between_kept,
    held_first,
    held_second,
    blocks_first,
    blocks_second,
    window_first,
    window_second,
    gradient,
    arrived,
    sums,
    parts_own,
    parts_side,
    local_sem,
    measured_sem,
    close_send_first,
    close_recv_first,
    close_send_second,
    close_recv_second,
    far_send_first,
    far_recv_first,
    far_send_second,
    far_recv_second,
    return_send,
    return_recv,
    sum_send,
    sum_recv,
):
    ty, tx, pos, y, zh, x = coordinates()
    loads = [
        pltpu.make_async_copy(source, target, local_sem.at[n])
        for n, (source, target) in enumerate(
            (
                (phase_hbm, phase),
                (illumination_hbm, illumination),
                (right_hbm, right),
                (order_hbm, order),
                (left_hbm, left),
                (measured_hbm, measured),
            )
        )
    ]

    works = (y < 2) | (ty == 1)
    slot_row = jnp.where(y < 2, y, 3 - y)
    slot = position(slot_row, zh, x)

    @pl.when(works)
    def _():
        for load in loads:
            load.start()

    clear_missing(held_first)
    clear_missing(held_second)
    clear_parts(parts_own, parts_side)
    enter()
    close_first = (rows, held_first, close_send_first, close_recv_first)
    close_second = (new_rows, held_second, close_send_second, close_recv_second)
    far_first = (blocks_first, window_first, far_send_first, far_recv_first)
    far_second = (blocks_second, window_second, far_send_second, far_recv_second)
    returned = (gradient, arrived, return_send, return_recv)
    summed = (sums, parts_own, parts_side, sum_send, sum_recv)
    for piece in (0, 1):
        close_start(piece, *close_first)
    for half in (0, 1):
        for piece in (0, 1):
            close_wait(piece, half, *close_first)
            far_start(piece, half, ty, offsets, held_first, *far_first)
    live = jnp.where(slot < counts[0, 0], 1.0, 0.0)
    move_measured = pltpu.make_async_remote_copy(
        src_ref=ordered_measured,
        dst_ref=ordered_measured,
        send_sem=measured_sem.at[0],
        recv_sem=measured_sem.at[1],
        device_id=peer(ty, tx, position(3 - y, zh, x)),
        device_id_type=MESH,
    )

    @pl.when(works)
    def _():
        for load in loads:
            load.wait()

    @pl.when(y < 2)
    def _():
        ordered_measured[...] = reordered(measured[...], order[0], order[1], 3)

    @pl.when((y < 2) & (ty == 1))
    def _():
        move_measured.start()

    @pl.when(works)
    def _():
        angles = reordered(phase[...], order[0], order[1], 3)
        slab[0] = jnp.cos(angles)
        slab[1] = jnp.sin(angles)
        shifted = shifted_probe(offsets, slot, illumination)
        probe[0] = shifted[0]
        probe[1] = shifted[1]

    @pl.when(turned_row(y, ty) < 2)
    def _():
        far_wait(0, *far_first)
        between = between_field(window_first, probe, slab, right, left)
        between_kept[0] = between[0]
        between_kept[1] = between[1]
        far_wait(1, *far_first)
        farfield = farfield_of(between, window_first, right, left)
        magnitude = jnp.sqrt(farfield[0] * farfield[0] + farfield[1] * farfield[1])

        @pl.when(ty == 1)
        def _():
            move_measured.wait_recv()

        keeping = (1.0 - ordered_measured[...] / jnp.maximum(magnitude, magnitude_floor)) * live
        backward = inverse(farfield[0] * keeping, farfield[1] * keeping, right, left)
        grad_second = complex_product(between_kept[0], -between_kept[1], backward[0], backward[1])
        gradient[2] = grad_second[0].reshape(8, 4, 8, W)
        gradient[3] = grad_second[1].reshape(8, 4, 8, W)
        return_start(1, *returned)
        toward = complex_product(layer_of(window_first, 2), -layer_of(window_first, 3), backward[0], backward[1])
        spectrum = transform(toward[0], toward[1], right, left)
        spectrum = complex_product(spectrum[0], spectrum[1], slab[0], -slab[1])
        incoming = inverse(spectrum[0], spectrum[1], right, left)
        grad_first = complex_product(probe[0], -probe[1], incoming[0], incoming[1])
        gradient[0] = grad_first[0].reshape(8, 4, 8, W)
        gradient[1] = grad_first[1].reshape(8, 4, 8, W)
        return_start(0, *returned)

    for piece in (1, 0):
        return_wait(piece, *returned)
        add_returned(piece, offsets, arrived, sums)
        sum_each(piece, "start", *summed)
    for piece in (1, 0):
        sum_each(piece, "recv", *summed)
        for layer in (2 * piece, 2 * piece + 1):
            total = sums[ty, 0, layer, zh]
            for part in range(4):
                if part:
                    total = total + parts_own[part, layer]
                total = total + parts_side[part, layer]
            velocity = momentum_rate * momentum[layer] + total
            new_momentum[layer] = velocity
            new_rows[layer] = rows[layer] - step_length * velocity
        close_start(piece, *close_second)
    for piece, half in ((1, 0), (0, 0), (0, 1), (1, 1)):
        close_wait(piece, half, *close_second)
        far_start(piece, half, 0, offsets, held_second, *far_second)

    @pl.when(y < 2)
    def _():
        far_wait(0, *far_second)
        between = between_field(window_second, probe, slab, right, left)
        far_wait(1, *far_second)
        farfield = farfield_of(between, window_second, right, left)
        magnitude = jnp.sqrt(farfield[0] * farfield[0] + farfield[1] * farfield[1]) * live
        amplitude[...] = reordered(magnitude, order[1], order[0], 2)

    @pl.when(y >= 2)
    def _():
        amplitude[...] = jnp.zeros_like(amplitude)

    for piece in (0, 1):
        close_drain(piece, *close_first)
        close_drain(piece, *close_second)
        far_drain(piece, ty, *far_first)
        far_drain(piece, 0, *far_second)
        sum_each(piece, "sent", *summed)

    @pl.when(turned_row(y, ty) < 2)
    def _():
        for piece in (0, 1):
            return_drain(piece, *returned)

    @pl.when((y < 2) & (ty == 1))
    def _():
        move_measured.wait_send()


def hand_over(*refs):
    for source, target in zip(refs[:3], refs[3:]):
        target[...] = source[...]


def shards(object_field, momentum, measured, illumination, slab_phase, offsets, entry_counts):
    rows = object_field.reshape(4, 8, W)
    right, left, order = (jnp.asarray(t) for t in tables(W))
    dma = pltpu.SemaphoreType.DMA
    close = len(ROLES)
    window_shape = (4, 8, 4, 8, W)
    held_shape = (2, 2, 4, 2, 8, W)
    blocks_shape = (2, 8, 2, 2, 8, W)
    field = (2, W, W)
    vmem = pl.BlockSpec(memory_space=pltpu.VMEM)
    smem = pl.BlockSpec(memory_space=pltpu.SMEM)
    remain = pl.BlockSpec(memory_space=pl.ANY)
    shapes = (
        jax.ShapeDtypeStruct((4, 8, W), f32),
        jax.ShapeDtypeStruct((4, 8, W), f32),
        jax.ShapeDtypeStruct((W, W), f32),
    )
    results = pl.pallas_call(
        kernel,
        out_shape=shapes,
        in_specs=[smem, smem, vmem, vmem, remain, remain, remain, remain, remain, remain],
        out_specs=[vmem, vmem, vmem],
        scratch_shapes=[
            pltpu.VMEM((W, W), f32),
            pltpu.VMEM(field, f32),
            pltpu.VMEM((W, W), f32),
            pltpu.VMEM(right.shape, bf16),
            pltpu.VMEM(left.shape, bf16),
            pltpu.VMEM(order.shape, bf16),
            pltpu.VMEM((W, W), f32),
            pltpu.VMEM(field, f32),
            pltpu.VMEM(field, f32),
            pltpu.VMEM(field, f32),
            pltpu.VMEM(held_shape, f32),
            pltpu.VMEM(held_shape, f32),
            pltpu.VMEM(blocks_shape, f32),
            pltpu.VMEM(blocks_shape, f32),
            pltpu.VMEM(window_shape, f32),
            pltpu.VMEM(window_shape, f32),
            pltpu.VMEM(window_shape, f32),
            pltpu.VMEM(blocks_shape, f32),
            pltpu.VMEM(held_shape, f32),
            pltpu.VMEM((4, 4, 8, W), f32),
            pltpu.VMEM((4, 4, 8, W), f32),
            dma((6,)),
            dma((2,)),
            dma((2, close)),
            dma((2, close)),
            dma((2, close)),
            dma((2, close)),
            dma((2, 8)),
            dma((2, 16)),
            dma((2, 8)),
            dma((2, 16)),
            dma((2, 16)),
            dma((2, 8)),
            dma((2, close)),
            dma((2, close)),
        ],
        compiler_params=pltpu.CompilerParams(
            has_side_effects=True, vmem_limit_bytes=VMEM_LIMIT, collective_id=0
        ),
        name="iterate",
    )(
        offsets[0, 0].T,
        entry_counts,
        rows,
        momentum.reshape(4, 8, W),
        measured[0, 0, 0],
        illumination,
        slab_phase,
        right,
        left,
        order,
    )
    new_rows, new_momentum, amplitude = pl.pallas_call(
        hand_over,
        out_shape=shapes,
        in_specs=[vmem] * 3,
        out_specs=[vmem] * 3,
        compiler_params=pltpu.CompilerParams(vmem_limit_bytes=VMEM_LIMIT),
        name="hand_over",
    )(*results)
    return (
        new_rows.reshape(2, 2, 8, W),
        new_momentum.reshape(2, 2, 8, W),
        amplitude[None, None, None],
    )


def solution(mesh):
    rows = P(None, None, ("ty", "pos"), "tx")
    slots = P("ty", "tx", "pos", None, None)
    return jax.shard_map(
        shards,
        mesh=mesh,
        in_specs=(rows, rows, slots, P(), P(), P("ty", "tx", None, None), P("ty", "tx")),
        out_specs=(rows, rows, slots),
        check_vma=False,
    )
```

```python
import functools
import math

import jax
import jax.numpy as jnp
import numpy as np
from jax import lax
from jax.experimental import pallas as pl
from jax.experimental.pallas import tpu as pltpu
from jax.sharding import PartitionSpec as P

f32 = jnp.float32
bf16 = jnp.bfloat16
MESH = pl.DeviceIdType.MESH
magnitude_floor = 0.5
momentum_rate = 0.9
step_length = 0.05
W = 256
MARGIN = 64
ROLES = [(s, h, k) for s in range(2) for h in range(2) for k in range(3) if (s, h, k) != (0, 0, 0)]
VMEM_LIMIT = 60 * 1024 * 1024


def tables(length):
    half = length // 2
    place = np.arange(half)

    def halves(value):
        value = value.astype(np.float32)
        high = value.astype(jnp.bfloat16)
        low = (value - high.astype(np.float32)).astype(jnp.bfloat16)
        return np.stack([high, low])

    right = []
    for direction in (-1.0, 1.0):
        for odd in (0, 1):
            turns = (place[:, None] * (2 * place[None, :] + odd)) % length
            if direction > 0:
                turns = turns.T
            angles = turns * (direction * 2.0 * math.pi / length)
            c = np.cos(angles) / math.sqrt(length)
            s = np.sin(angles) / math.sqrt(length)
            right.append(halves(np.block([[c, s], [-s, c]])))
    right = np.stack(right).reshape(2, 2, 2, length, length)
    left = right.swapaxes(3, 4)
    order = np.zeros((length, length))
    order[np.arange(length), np.concatenate([2 * place, 2 * place + 1])] = 1.0
    return right, np.ascontiguousarray(left), np.stack([order, order.T]).astype(jnp.bfloat16)


def coordinates():
    ty = lax.axis_index("ty")
    tx = lax.axis_index("tx")
    pos = lax.axis_index("pos")
    return ty, tx, pos, pos // 8, (pos // 4) % 2, pos % 4


def peer(ty, tx, pos):
    return {"ty": ty, "tx": tx, "pos": pos}


def position(y, zh, x):
    return y * 8 + zh * 4 + x


def close_peer(role, outward):
    s, h, k = role
    ty, tx, pos, y, zh, x = coordinates()
    step = (0, 3, 1)[k] if outward else (0, 1, 3)[k]
    other_ty = 1 - ty if s else ty
    other_zh = 1 - zh if h else zh
    return other_ty, (tx + step) % 4, other_zh, position(y, other_zh, x)


def has_role(role, y_pair, tx_lower, tx_upper):
    s, h, k = role
    terms = ([y_pair] if s else []) + [[], [tx_lower], [tx_upper]][k]
    return functools.reduce(jnp.logical_and, terms) if terms else None


def when(condition, body):
    if condition is None:
        body()
    else:
        pl.when(condition)(body)


def enter(clear):
    ty, tx, pos, y, zh, x = coordinates()
    barrier = pltpu.get_barrier_semaphore()
    outer = (y == 0) | (y == 3)
    for role in ROLES:
        other_ty, other_tx, _, other_pos = close_peer(role, True)

        def signal(other_ty=other_ty, other_tx=other_tx, other_pos=other_pos):
            pl.semaphore_signal(barrier, inc=1, device_id=peer(other_ty, other_tx, other_pos), device_id_type=MESH)

        when(has_role(role, outer, tx > 0, tx < 3), signal)
    near = jnp.where((tx == 0) | (tx == 3), 4, 6) * jnp.where(outer, 2, 1) - 1
    me = y * 4 + x
    small = (y % 2) * 4 + x

    def greet(start, count, modulus):
        def body(j, carry):
            t = (start + j) % modulus
            pl.semaphore_signal(
                barrier, inc=1, device_id=peer(ty, tx, position(t // 4, zh, t % 4)), device_id_type=MESH
            )
            return carry

        lax.fori_loop(0, count, body, 0)

    everyone = (y < 2) | (ty == 1)

    @pl.when(everyone)
    def _():
        greet(me + 1, 15, 16)

    @pl.when(jnp.logical_not(everyone))
    def _():
        greet(small, 8, 8)

    clear()
    pl.semaphore_wait(barrier, near + jnp.where(everyone, 15, 8))


def turned_row(y, turned):
    return y + turned * (3 - 2 * y)


def sibling_facts():
    ty, tx, pos, y, zh, x = coordinates()
    takes = ((ty == 0) & (y == 0)) | ((ty == 1) & (y == 3))
    gives = ((ty == 1) & (y == 0)) | ((ty == 0) & (y == 3))
    return takes, gives


def close_copy(index, role, piece, src, held, send_sem, recv_sem):
    ty, tx, pos, y, zh, x = coordinates()
    k = role[2]
    layers = pl.ds(2 * piece, 2)
    other_ty, other_tx, _, other_pos = close_peer(role, True)
    if k == 0:
        source, target = src.at[layers], held.at[ty, 0, layers, zh]
    else:
        lanes = pl.ds(128 * (k - 1), 128)
        source, target = src.at[layers, :, lanes], held.at[ty, 1, layers, zh, :, lanes]
    return pltpu.make_async_remote_copy(
        src_ref=source,
        dst_ref=target,
        send_sem=send_sem.at[piece, index],
        recv_sem=recv_sem.at[piece, index],
        device_id=peer(other_ty, other_tx, other_pos),
        device_id_type=MESH,
    )


def close_start(piece, src, held, send_sem, recv_sem):
    ty, tx, pos, y, zh, x = coordinates()
    takes, gives = sibling_facts()
    for half in (1, 0):
        for index, role in enumerate(ROLES):
            if role[1] == half:
                copy = close_copy(index, role, piece, src, held, send_sem, recv_sem)
                when(has_role(role, gives, tx > 0, tx < 3), copy.start)
    for layer in (2 * piece, 2 * piece + 1):
        held[ty, 0, layer, zh] = src[layer]


def close_wait(piece, half, src, held, send_sem, recv_sem):
    ty, tx, pos, y, zh, x = coordinates()
    takes, gives = sibling_facts()
    for index, role in enumerate(ROLES):
        if role[1] != half:
            continue
        copy = close_copy(index, role, piece, src, held, send_sem, recv_sem)
        when(has_role(role, takes, tx < 3, tx > 0), copy.wait_recv)


def close_drain(piece, src, held, send_sem, recv_sem):
    ty, tx, pos, y, zh, x = coordinates()
    takes, gives = sibling_facts()
    for index, role in enumerate(ROLES):
        copy = close_copy(index, role, piece, src, held, send_sem, recv_sem)
        when(has_role(role, gives, tx > 0, tx < 3), copy.wait_send)


def clear_missing(held):
    ty, tx, pos, y, zh, x = coordinates()
    takes, gives = sibling_facts()
    nothing = jnp.zeros((4, 2, 8, 128), f32)

    @pl.when(jnp.logical_not(takes))
    def _():
        for kind in range(2):
            held[1 - ty, kind] = jnp.zeros((4, 2, 8, W), f32)

    @pl.when(tx == 3)
    def _():
        for core in range(2):
            held[core, 1, :, :, :, 0:128] = nothing

    @pl.when(tx == 0)
    def _():
        for core in range(2):
            held[core, 1, :, :, :, 128:256] = nothing


def row_swap(row_start, zh):
    ty, tx, pos, y, _, x = coordinates()
    row = y * 64 + zh * 32 + x * 8 + lax.broadcasted_iota(jnp.int32, (8, W), 0)
    return ((row < MARGIN) & (row_start > row + MARGIN)) | ((row >= 192) & (row > row_start + 191))


def column_swap(column_start):
    column = lax.broadcasted_iota(jnp.int32, (8, W), 1)
    return ((column < MARGIN) & (column_start > column + MARGIN)) | (
        (column >= 192) & (column > column_start + 191)
    )


def far_copy(j, piece, rows, turned, blocks, window, send_sem, recv_sem):
    ty, tx, pos, y, zh, x = coordinates()
    t = ((turned_row(y, turned) % 2) * 4 + x + j) % 8
    layers = pl.ds(2 * piece, 2)
    if rows is None:
        source, target = blocks.at[piece, j], window.at[layers, pl.ds(2 * y, 2), x]
    else:
        source, target = blocks.at[piece, j, :, rows], window.at[layers, 2 * y + rows, x]
    return pltpu.make_async_remote_copy(
        src_ref=source,
        dst_ref=target,
        send_sem=send_sem.at[piece, j],
        recv_sem=recv_sem.at[piece, y * 4 + x],
        device_id=peer(ty, tx, position(turned_row(t // 4, turned), zh, t % 4)),
        device_id_type=MESH,
    )


def far_start(piece, half, turned, offsets, held, *far):
    ty, tx, pos, y, zh, x = coordinates()
    blocks, window = far[:2]
    rows = 1 - zh if half else zh
    slot_row = turned_row(y, turned)
    for j in range(8):
        t = ((slot_row % 2) * 4 + x + j) % 8
        target = position(t // 4, zh, t % 4)
        swap_rows = row_swap(offsets[0, target], rows)
        swap_columns = column_swap(offsets[1, target])
        for part in range(2):
            layer = 2 * piece + part
            own = jnp.where(swap_columns, held[ty, 1, layer, rows], held[ty, 0, layer, rows])
            sibling = jnp.where(swap_columns, held[1 - ty, 1, layer, rows], held[1 - ty, 0, layer, rows])
            blocks[piece, j, part, rows] = jnp.where(swap_rows, sibling, own)
        if j == 0:

            @pl.when(slot_row >= 2)
            def _():
                far_copy(0, piece, rows, turned, *far).start()

            @pl.when(slot_row < 2)
            def _():
                for part in range(2):
                    window[2 * piece + part, 2 * y + rows, x] = blocks[piece, 0, part, rows]

        else:
            far_copy(j, piece, rows, turned, *far).start()


def far_wait(piece, blocks, window, send_sem, recv_sem):
    ty, tx, pos, y, zh, x = coordinates()

    def arrive(j, carry):
        s = (y * 4 + x + j) % 16
        pltpu.make_async_remote_copy(
            src_ref=blocks.at[piece, 0],
            dst_ref=window.at[pl.ds(2 * piece, 2), pl.ds(2 * (s // 4), 2), s % 4],
            send_sem=send_sem.at[piece, 0],
            recv_sem=recv_sem.at[piece, s],
            device_id=peer(ty, tx, position(s // 4, zh, s % 4)),
            device_id_type=MESH,
        ).wait_recv()
        return carry

    lax.fori_loop(1, 16, arrive, 0)


def far_drain(piece, turned, *far):
    ty, tx, pos, y, zh, x = coordinates()

    @pl.when(turned_row(y, turned) >= 2)
    def _():
        far_copy(0, piece, None, turned, *far).wait_send()

    for j in range(1, 8):
        far_copy(j, piece, None, turned, *far).wait_send()


def chosen_rows(half):
    zh = coordinates()[4]
    return 1 - zh if half else zh


def return_copy(j, piece, half, gradient, arrived, send_sem, recv_sem):
    ty, tx, pos, y, zh, x = coordinates()
    t = (y * 4 + x + j) % 16
    slot = (turned_row(y, ty) % 2) * 4 + x
    layers = pl.ds(2 * piece, 2)
    if half is None:
        source, target = gradient.at[layers, pl.ds(2 * (t // 4), 2), t % 4], arrived.at[piece, slot]
    else:
        rows = chosen_rows(half)
        source, target = gradient.at[layers, 2 * (t // 4) + rows, t % 4], arrived.at[piece, slot, :, rows]
    return pltpu.make_async_remote_copy(
        src_ref=source,
        dst_ref=target,
        send_sem=send_sem.at[piece, j],
        recv_sem=recv_sem.at[piece, half or 0, slot],
        device_id=peer(ty, tx, position(t // 4, zh, t % 4)),
        device_id_type=MESH,
    )


def return_start(piece, half, gradient, arrived, send_sem, recv_sem):
    ty, tx, pos, y, zh, x = coordinates()
    slot = (turned_row(y, ty) % 2) * 4 + x

    def leave(j, carry):
        return_copy(j, piece, half, gradient, arrived, send_sem, recv_sem).start()
        return carry

    lax.fori_loop(1, 16, leave, 0)
    for part in range(2):
        if half is None:
            arrived[piece, slot, part] = gradient[2 * piece + part, pl.ds(2 * y, 2), x]
        else:
            rows = chosen_rows(half)
            arrived[piece, slot, part, rows] = gradient[2 * piece + part, 2 * y + rows, x]


def return_wait(piece, half, gradient, arrived, send_sem, recv_sem):
    ty, tx, pos, y, zh, x = coordinates()
    slot_row = turned_row(y, ty)
    base = (slot_row % 2) * 4 + x
    layers = pl.ds(2 * piece, 2)

    def wait_for(s):
        if half is None:
            source, target = gradient.at[layers, pl.ds(0, 2), 0], arrived.at[piece, s]
        else:
            source, target = gradient.at[layers, 0, 0], arrived.at[piece, s, :, chosen_rows(half)]
        pltpu.make_async_remote_copy(
            src_ref=source,
            dst_ref=target,
            send_sem=send_sem.at[piece, 0],
            recv_sem=recv_sem.at[piece, half or 0, s],
            device_id=peer(ty, tx, position(turned_row(s // 4, ty), zh, s % 4)),
            device_id_type=MESH,
        ).wait_recv()

    @pl.when(slot_row >= 2)
    def _():
        wait_for(base)

    for j in range(1, 8):
        wait_for((base + j) % 8)


def return_drain(piece, gradient, arrived, send_sem, recv_sem):
    def left(j, carry):
        return_copy(j, piece, None, gradient, arrived, send_sem, recv_sem).wait_send()
        return carry

    lax.fori_loop(1, 16, left, 0)


def add_returned(piece, half, offsets, arrived, sums):
    ty, tx, pos, y, zh, x = coordinates()
    rows = chosen_rows(half)
    totals = [[jnp.zeros((8, W), f32)] * 4 for _ in range(2)]
    for j in range(8):
        target = position(j // 4, zh, j % 4)
        swap_rows = row_swap(offsets[0, target], rows)
        swap_columns = column_swap(offsets[1, target])
        for part in range(2):
            block = arrived[piece, j, part, rows]
            mine = jnp.where(swap_rows, 0.0, block)
            theirs = jnp.where(swap_rows, block, 0.0)
            own, own_side, sibling, sibling_side = totals[part]
            totals[part] = [
                own + jnp.where(swap_columns, 0.0, mine),
                own_side + jnp.where(swap_columns, mine, 0.0),
                sibling + jnp.where(swap_columns, 0.0, theirs),
                sibling_side + jnp.where(swap_columns, theirs, 0.0),
            ]
    for part in range(2):
        layer = 2 * piece + part
        sums[ty, 0, layer, rows] = totals[part][0]
        sums[ty, 1, layer, rows] = totals[part][1]
        sums[1 - ty, 0, layer, rows] = totals[part][2]
        sums[1 - ty, 1, layer, rows] = totals[part][3]


def sum_copy(index, role, piece, sums, parts_own, parts_side, send_sem, recv_sem):
    s, h, k = role
    layers = pl.ds(2 * piece, 2)
    other_ty, other_tx, other_zh, other_pos = close_peer(role, False)
    if k == 0:
        source, target = sums.at[other_ty, 0, layers, other_zh], parts_own.at[2 * s + h, layers]
    else:
        lanes = pl.ds(128 * (k - 1), 128)
        source = sums.at[other_ty, 1, layers, other_zh, :, lanes]
        target = parts_side.at[2 * s + h, layers, :, lanes]
    return pltpu.make_async_remote_copy(
        src_ref=source,
        dst_ref=target,
        send_sem=send_sem.at[piece, index],
        recv_sem=recv_sem.at[piece, index],
        device_id=peer(other_ty, other_tx, other_pos),
        device_id_type=MESH,
    )


def sum_each(piece, action, half, *refs):
    ty, tx, pos, y, zh, x = coordinates()
    takes, gives = sibling_facts()
    for index, role in enumerate(ROLES):
        if half not in (None, role[1]):
            continue
        copy = sum_copy(index, role, piece, *refs)
        if action == "recv":
            when(has_role(role, gives, tx > 0, tx < 3), copy.wait_recv)
        else:
            act = copy.start if action == "start" else copy.wait_send
            when(has_role(role, takes, tx < 3, tx > 0), act)


def clear_parts(parts_own, parts_side):
    ty, tx, pos, y, zh, x = coordinates()
    takes, gives = sibling_facts()
    nothing = jnp.zeros((4, 8, 128), f32)

    @pl.when(jnp.logical_not(gives))
    def _():
        for part in (2, 3):
            parts_own[part] = jnp.zeros((4, 8, W), f32)
            parts_side[part] = jnp.zeros((4, 8, W), f32)

    @pl.when(tx == 0)
    def _():
        for part in range(4):
            parts_side[part, :, :, 0:128] = nothing

    @pl.when(tx == 3)
    def _():
        for part in range(4):
            parts_side[part, :, :, 128:256] = nothing


def split(value):
    high = value.astype(bf16)
    return high, (value - high.astype(f32)).astype(bf16)


def product(left, right):
    return jnp.dot(left, right, preferred_element_type=f32)


def from_right(value, table):
    high, low = split(value)
    return product(high, table[0]) + product(low, table[0]) + product(high, table[1])


def from_left(table, value):
    high, low = split(value)
    return product(table[0], high) + product(table[0], low) + product(table[1], high)


def transform(real_part, imag_part, right, left):
    join = jnp.concatenate
    h = W // 2
    a, b, c, d = real_part[:, :h], real_part[:, h:], imag_part[:, :h], imag_part[:, h:]
    even = from_right(join([a + b, c + d], 1), right[0, 0])
    odd = from_right(join([a - b, c - d], 1), right[0, 1])
    real_part, imag_part = join([even[:, :h], odd[:, :h]], 1), join([even[:, h:], odd[:, h:]], 1)
    a, b, c, d = real_part[:h], real_part[h:], imag_part[:h], imag_part[h:]
    even = from_left(left[0, 0], join([a + b, c + d], 0))
    odd = from_left(left[0, 1], join([a - b, c - d], 0))
    return join([even[:h], odd[:h]], 0), join([even[h:], odd[h:]], 0)


def inverse(real_part, imag_part, right, left):
    join = jnp.concatenate
    h = W // 2
    even = from_right(join([real_part[:, :h], imag_part[:, :h]], 1), right[1, 0])
    odd = from_right(join([real_part[:, h:], imag_part[:, h:]], 1), right[1, 1])
    total, rest = even + odd, even - odd
    real_part, imag_part = join([total[:, :h], rest[:, :h]], 1), join([total[:, h:], rest[:, h:]], 1)
    even = from_left(left[1, 0], join([real_part[:h], imag_part[:h]], 0))
    odd = from_left(left[1, 1], join([real_part[h:], imag_part[h:]], 0))
    total, rest = even + odd, even - odd
    return join([total[:h], rest[:h]], 0), join([total[h:], rest[h:]], 0)


def parts_of(value, count):
    parts = []
    for _ in range(count):
        parts.append(value.astype(bf16))
        value = value - parts[-1].astype(f32)
    return parts


def reordered(value, first, second, count):
    value = sum(product(first, part) for part in parts_of(value, count))
    return sum(product(part, second) for part in parts_of(value, count))


def complex_product(first_real, first_imag, second_real, second_imag):
    return (
        first_real * second_real - first_imag * second_imag,
        first_real * second_imag + first_imag * second_real,
    )


def shifted_probe(offsets, slot, illumination):
    down = (offsets[0, slot] + 192) % 256
    across = (offsets[1, slot] + 192) % 256
    return [pltpu.roll(pltpu.roll(illumination[part], down, 0), across, 1) for part in range(2)]


def layer_of(window, layer):
    return window[layer].reshape(W, W)


def between_field(window, probe, slab, right, left):
    entering = complex_product(probe[0], probe[1], layer_of(window, 0), layer_of(window, 1))
    spectrum = transform(entering[0], entering[1], right, left)
    spectrum = complex_product(spectrum[0], spectrum[1], slab[0], slab[1])
    return inverse(spectrum[0], spectrum[1], right, left)


def farfield_of(between, window, right, left):
    leaving = complex_product(between[0], between[1], layer_of(window, 2), layer_of(window, 3))
    return transform(leaving[0], leaving[1], right, left)


def kernel(
    offsets_hbm,
    counts_hbm,
    rows_hbm,
    momentum_hbm,
    measured_hbm,
    illumination_hbm,
    phase_hbm,
    right_hbm,
    left_hbm,
    order_hbm,
    new_rows,
    new_momentum,
    amplitude,
    offsets,
    counts,
    rows,
    momentum,
    measured,
    illumination,
    phase,
    right,
    left,
    order,
    ordered_measured,
    probe,
    slab,
    between_kept,
    held_first,
    held_second,
    blocks_first,
    blocks_second,
    window_first,
    window_second,
    gradient,
    arrived,
    sums,
    parts_own,
    parts_side,
    local_sem,
    measured_sem,
    close_send_first,
    close_recv_first,
    close_send_second,
    close_recv_second,
    far_send_first,
    far_recv_first,
    far_send_second,
    far_recv_second,
    return_send,
    return_recv,
    sum_send,
    sum_recv,
):
    ty, tx, pos, y, zh, x = coordinates()
    loads = [
        pltpu.make_async_copy(source, target, local_sem.at[n])
        for n, (source, target) in enumerate(
            (
                (phase_hbm, phase),
                (illumination_hbm, illumination),
                (right_hbm, right),
                (order_hbm, order),
                (left_hbm, left),
                (measured_hbm, measured),
                (counts_hbm, counts),
                (rows_hbm, rows),
                (offsets_hbm, offsets),
                (momentum_hbm, momentum),
            )
        )
    ]
    loads, (counts_load, rows_load, offsets_load, momentum_load) = loads[:-4], loads[-4:]

    works = (y < 2) | (ty == 1)
    slot_row = jnp.where(y < 2, y, 3 - y)
    slot = position(slot_row, zh, x)

    def begin():
        rows_load.start()
        offsets_load.start()
        counts_load.start()
        momentum_load.start()

        @pl.when(works)
        def _():
            for load in loads:
                load.start()

        clear_missing(held_first)
        clear_missing(held_second)
        clear_parts(parts_own, parts_side)
        rows_load.wait()

    enter(begin)
    close_first = (rows, held_first, close_send_first, close_recv_first)
    close_second = (new_rows, held_second, close_send_second, close_recv_second)
    far_first = (blocks_first, window_first, far_send_first, far_recv_first)
    far_second = (blocks_second, window_second, far_send_second, far_recv_second)
    returned = (gradient, arrived, return_send, return_recv)
    summed = (sums, parts_own, parts_side, sum_send, sum_recv)
    for piece in (0, 1):
        close_start(piece, *close_first)
    offsets_load.wait()
    counts_load.wait()
    for half in (0, 1):
        for piece in (0, 1):
            close_wait(piece, half, *close_first)
            far_start(piece, half, ty, offsets, held_first, *far_first)
    live = jnp.where(slot < counts[0, 0], 1.0, 0.0)
    move_measured = pltpu.make_async_remote_copy(
        src_ref=ordered_measured,
        dst_ref=ordered_measured,
        send_sem=measured_sem.at[0],
        recv_sem=measured_sem.at[1],
        device_id=peer(ty, tx, position(3 - y, zh, x)),
        device_id_type=MESH,
    )

    @pl.when(works)
    def _():
        for load in loads:
            load.wait()

    @pl.when(y < 2)
    def _():
        ordered_measured[...] = reordered(measured[...], order[0], order[1], 3)

    @pl.when((y < 2) & (ty == 1))
    def _():
        move_measured.start()

    @pl.when(works)
    def _():
        angles = reordered(phase[...], order[0], order[1], 3)
        slab[0] = jnp.cos(angles)
        slab[1] = jnp.sin(angles)
        shifted = shifted_probe(offsets, slot, illumination)
        probe[0] = shifted[0]
        probe[1] = shifted[1]

    @pl.when(turned_row(y, ty) < 2)
    def _():
        far_wait(0, *far_first)
        between = between_field(window_first, probe, slab, right, left)
        between_kept[0] = between[0]
        between_kept[1] = between[1]
        far_wait(1, *far_first)
        farfield = farfield_of(between, window_first, right, left)
        magnitude = jnp.sqrt(farfield[0] * farfield[0] + farfield[1] * farfield[1])

        @pl.when(ty == 1)
        def _():
            move_measured.wait_recv()

        keeping = (1.0 - ordered_measured[...] / jnp.maximum(magnitude, magnitude_floor)) * live
        backward = inverse(farfield[0] * keeping, farfield[1] * keeping, right, left)
        grad_second = complex_product(between_kept[0], -between_kept[1], backward[0], backward[1])
        gradient[2] = grad_second[0].reshape(8, 4, 8, W)
        gradient[3] = grad_second[1].reshape(8, 4, 8, W)
        return_start(1, None, *returned)
        toward = complex_product(layer_of(window_first, 2), -layer_of(window_first, 3), backward[0], backward[1])
        spectrum = transform(toward[0], toward[1], right, left)
        spectrum = complex_product(spectrum[0], spectrum[1], slab[0], -slab[1])
        incoming = inverse(spectrum[0], spectrum[1], right, left)
        grad_first = complex_product(probe[0], -probe[1], incoming[0], incoming[1])
        gradient[0] = grad_first[0].reshape(8, 4, 8, W)
        gradient[1] = grad_first[1].reshape(8, 4, 8, W)
        for half in (1, 0):
            return_start(0, half, *returned)

    return_wait(1, None, *returned)
    for half in (1, 0):
        add_returned(1, half, offsets, arrived, sums)
        sum_each(1, "start", half, *summed)
    for half in (1, 0):
        return_wait(0, half, *returned)
        add_returned(0, half, offsets, arrived, sums)
        sum_each(0, "start", half, *summed)
    momentum_load.wait()
    for piece in (1, 0):
        sum_each(piece, "recv", None, *summed)
        for layer in (2 * piece, 2 * piece + 1):
            total = sums[ty, 0, layer, zh]
            for part in range(4):
                if part:
                    total = total + parts_own[part, layer]
                total = total + parts_side[part, layer]
            velocity = momentum_rate * momentum[layer] + total
            new_momentum[layer] = velocity
            new_rows[layer] = rows[layer] - step_length * velocity
        close_start(piece, *close_second)
    for piece, half in ((1, 0), (0, 0), (0, 1), (1, 1)):
        close_wait(piece, half, *close_second)
        far_start(piece, half, 0, offsets, held_second, *far_second)

    @pl.when(y < 2)
    def _():
        far_wait(0, *far_second)
        between = between_field(window_second, probe, slab, right, left)
        far_wait(1, *far_second)
        farfield = farfield_of(between, window_second, right, left)
        magnitude = jnp.sqrt(farfield[0] * farfield[0] + farfield[1] * farfield[1]) * live
        amplitude[...] = reordered(magnitude, order[1], order[0], 2)

    @pl.when(y >= 2)
    def _():
        amplitude[...] = jnp.zeros_like(amplitude)

    for piece in (0, 1):
        close_drain(piece, *close_first)
        close_drain(piece, *close_second)
        far_drain(piece, ty, *far_first)
        far_drain(piece, 0, *far_second)
        sum_each(piece, "sent", None, *summed)

    @pl.when(turned_row(y, ty) < 2)
    def _():
        for piece in (0, 1):
            return_drain(piece, *returned)

    @pl.when((y < 2) & (ty == 1))
    def _():
        move_measured.wait_send()


def hand_over(*refs):
    for source, target in zip(refs[:3], refs[3:]):
        target[...] = source[...]


def shards(object_field, momentum, measured, illumination, slab_phase, offsets, entry_counts):
    rows = object_field.reshape(4, 8, W)
    right, left, order = (jnp.asarray(t) for t in tables(W))
    dma = pltpu.SemaphoreType.DMA
    close = len(ROLES)
    window_shape = (4, 8, 4, 8, W)
    held_shape = (2, 2, 4, 2, 8, W)
    blocks_shape = (2, 8, 2, 2, 8, W)
    field = (2, W, W)
    vmem = pl.BlockSpec(memory_space=pltpu.VMEM)
    remain = pl.BlockSpec(memory_space=pl.ANY)
    shapes = (
        jax.ShapeDtypeStruct((4, 8, W), f32),
        jax.ShapeDtypeStruct((4, 8, W), f32),
        jax.ShapeDtypeStruct((W, W), f32),
    )
    results = pl.pallas_call(
        kernel,
        out_shape=shapes,
        in_specs=[remain] * 10,
        out_specs=[vmem, vmem, vmem],
        scratch_shapes=[
            pltpu.SMEM((2, offsets.shape[2]), jnp.int32),
            pltpu.SMEM((1, 1), jnp.int32),
            pltpu.VMEM((4, 8, W), f32),
            pltpu.VMEM((4, 8, W), f32),
            pltpu.VMEM((W, W), f32),
            pltpu.VMEM(field, f32),
            pltpu.VMEM((W, W), f32),
            pltpu.VMEM(right.shape, bf16),
            pltpu.VMEM(left.shape, bf16),
            pltpu.VMEM(order.shape, bf16),
            pltpu.VMEM((W, W), f32),
            pltpu.VMEM(field, f32),
            pltpu.VMEM(field, f32),
            pltpu.VMEM(field, f32),
            pltpu.VMEM(held_shape, f32),
            pltpu.VMEM(held_shape, f32),
            pltpu.VMEM(blocks_shape, f32),
            pltpu.VMEM(blocks_shape, f32),
            pltpu.VMEM(window_shape, f32),
            pltpu.VMEM(window_shape, f32),
            pltpu.VMEM(window_shape, f32),
            pltpu.VMEM(blocks_shape, f32),
            pltpu.VMEM(held_shape, f32),
            pltpu.VMEM((4, 4, 8, W), f32),
            pltpu.VMEM((4, 4, 8, W), f32),
            dma((10,)),
            dma((2,)),
            dma((2, close)),
            dma((2, close)),
            dma((2, close)),
            dma((2, close)),
            dma((2, 8)),
            dma((2, 16)),
            dma((2, 8)),
            dma((2, 16)),
            dma((2, 16)),
            dma((2, 2, 8)),
            dma((2, close)),
            dma((2, close)),
        ],
        compiler_params=pltpu.CompilerParams(
            has_side_effects=True, vmem_limit_bytes=VMEM_LIMIT, collective_id=0
        ),
        name="iterate",
    )(
        offsets[0, 0].T,
        entry_counts,
        rows,
        momentum.reshape(4, 8, W),
        measured[0, 0, 0],
        illumination,
        slab_phase,
        right,
        left,
        order,
    )
    new_rows, new_momentum, amplitude = pl.pallas_call(
        hand_over,
        out_shape=shapes,
        in_specs=[vmem] * 3,
        out_specs=[vmem] * 3,
        compiler_params=pltpu.CompilerParams(vmem_limit_bytes=VMEM_LIMIT),
        name="hand_over",
    )(*results)
    return (
        new_rows.reshape(2, 2, 8, W),
        new_momentum.reshape(2, 2, 8, W),
        amplitude[None, None, None],
    )


def solution(mesh):
    rows = P(None, None, ("ty", "pos"), "tx")
    slots = P("ty", "tx", "pos", None, None)
    return jax.shard_map(
        shards,
        mesh=mesh,
        in_specs=(rows, rows, slots, P(), P(), P("ty", "tx", None, None), P("ty", "tx")),
        out_specs=(rows, rows, slots),
        check_vma=False,
    )
```

```python
import functools
import math

import jax
import jax.numpy as jnp
import numpy as np
from jax import lax
from jax.experimental import pallas as pl
from jax.experimental.pallas import tpu as pltpu
from jax.sharding import PartitionSpec as P

f32 = jnp.float32
bf16 = jnp.bfloat16
MESH = pl.DeviceIdType.MESH
magnitude_floor = 0.5
momentum_rate = 0.9
step_length = 0.05
W = 256
MARGIN = 64
ROLES = [(s, h, k) for s in range(2) for h in range(2) for k in range(3) if (s, h, k) != (0, 0, 0)]
VMEM_LIMIT = 60 * 1024 * 1024


def tables(length):
    half = length // 2
    place = np.arange(half)

    def halves(value):
        value = value.astype(np.float32)
        high = value.astype(jnp.bfloat16)
        low = (value - high.astype(np.float32)).astype(jnp.bfloat16)
        return np.stack([high, low])

    right = []
    for direction in (-1.0, 1.0):
        for odd in (0, 1):
            turns = (place[:, None] * (2 * place[None, :] + odd)) % length
            if direction > 0:
                turns = turns.T
            angles = turns * (direction * 2.0 * math.pi / length)
            c = np.cos(angles) / math.sqrt(length)
            s = np.sin(angles) / math.sqrt(length)
            right.append(halves(np.block([[c, s], [-s, c]])))
    right = np.stack(right).reshape(2, 2, 2, length, length)
    left = right.swapaxes(3, 4)
    order = np.zeros((length, length))
    order[np.arange(length), np.concatenate([2 * place, 2 * place + 1])] = 1.0
    return right, np.ascontiguousarray(left), np.stack([order, order.T]).astype(jnp.bfloat16)


def coordinates():
    ty = lax.axis_index("ty")
    tx = lax.axis_index("tx")
    pos = lax.axis_index("pos")
    return ty, tx, pos, pos // 8, (pos // 4) % 2, pos % 4


def peer(ty, tx, pos):
    return {"ty": ty, "tx": tx, "pos": pos}


def position(y, zh, x):
    return y * 8 + zh * 4 + x


def close_peer(role, outward):
    s, h, k = role
    ty, tx, pos, y, zh, x = coordinates()
    step = (0, 3, 1)[k] if outward else (0, 1, 3)[k]
    other_ty = 1 - ty if s else ty
    other_zh = 1 - zh if h else zh
    return other_ty, (tx + step) % 4, other_zh, position(y, other_zh, x)


def has_role(role, y_pair, tx_lower, tx_upper):
    s, h, k = role
    terms = ([y_pair] if s else []) + [[], [tx_lower], [tx_upper]][k]
    return functools.reduce(jnp.logical_and, terms) if terms else None


def when(condition, body):
    if condition is None:
        body()
    else:
        pl.when(condition)(body)


def enter(clear):
    ty, tx, pos, y, zh, x = coordinates()
    barrier = pltpu.get_barrier_semaphore()
    outer = (y == 0) | (y == 3)
    for role in ROLES:
        other_ty, other_tx, _, other_pos = close_peer(role, True)

        def signal(other_ty=other_ty, other_tx=other_tx, other_pos=other_pos):
            pl.semaphore_signal(barrier, inc=1, device_id=peer(other_ty, other_tx, other_pos), device_id_type=MESH)

        when(has_role(role, outer, tx > 0, tx < 3), signal)
    near = jnp.where((tx == 0) | (tx == 3), 4, 6) * jnp.where(outer, 2, 1) - 1
    me = y * 4 + x
    small = (y % 2) * 4 + x

    def greet(start, count, modulus):
        def body(j, carry):
            t = (start + j) % modulus
            pl.semaphore_signal(
                barrier, inc=1, device_id=peer(ty, tx, position(t // 4, zh, t % 4)), device_id_type=MESH
            )
            return carry

        lax.fori_loop(0, count, body, 0)

    everyone = (y < 2) | (ty == 1)

    @pl.when(everyone)
    def _():
        greet(me + 1, 15, 16)

    @pl.when(jnp.logical_not(everyone))
    def _():
        greet(small, 8, 8)

    clear()
    pl.semaphore_wait(barrier, near + jnp.where(everyone, 15, 8))


def turned_row(y, turned):
    return y + turned * (3 - 2 * y)


def sibling_facts():
    ty, tx, pos, y, zh, x = coordinates()
    takes = ((ty == 0) & (y == 0)) | ((ty == 1) & (y == 3))
    gives = ((ty == 1) & (y == 0)) | ((ty == 0) & (y == 3))
    return takes, gives


def close_copy(index, role, piece, src, held, send_sem, recv_sem):
    ty, tx, pos, y, zh, x = coordinates()
    k = role[2]
    layers = pl.ds(2 * piece, 2)
    other_ty, other_tx, _, other_pos = close_peer(role, True)
    if k == 0:
        source, target = src.at[layers], held.at[ty, 0, layers, zh]
    else:
        lanes = pl.ds(128 * (k - 1), 128)
        source, target = src.at[layers, :, lanes], held.at[ty, 1, layers, zh, :, lanes]
    return pltpu.make_async_remote_copy(
        src_ref=source,
        dst_ref=target,
        send_sem=send_sem.at[piece, index],
        recv_sem=recv_sem.at[piece, index],
        device_id=peer(other_ty, other_tx, other_pos),
        device_id_type=MESH,
    )


def close_start(piece, src, held, send_sem, recv_sem):
    ty, tx, pos, y, zh, x = coordinates()
    takes, gives = sibling_facts()
    for half in (1, 0):
        for index, role in enumerate(ROLES):
            if role[1] == half:
                copy = close_copy(index, role, piece, src, held, send_sem, recv_sem)
                when(has_role(role, gives, tx > 0, tx < 3), copy.start)
    for layer in (2 * piece, 2 * piece + 1):
        held[ty, 0, layer, zh] = src[layer]


def close_wait(piece, half, src, held, send_sem, recv_sem):
    ty, tx, pos, y, zh, x = coordinates()
    takes, gives = sibling_facts()
    for index, role in enumerate(ROLES):
        if role[1] != half:
            continue
        copy = close_copy(index, role, piece, src, held, send_sem, recv_sem)
        when(has_role(role, takes, tx < 3, tx > 0), copy.wait_recv)


def close_drain(piece, src, held, send_sem, recv_sem):
    ty, tx, pos, y, zh, x = coordinates()
    takes, gives = sibling_facts()
    for index, role in enumerate(ROLES):
        copy = close_copy(index, role, piece, src, held, send_sem, recv_sem)
        when(has_role(role, gives, tx > 0, tx < 3), copy.wait_send)


def clear_missing(held):
    ty, tx, pos, y, zh, x = coordinates()
    takes, gives = sibling_facts()
    nothing = jnp.zeros((4, 2, 8, 128), f32)

    @pl.when(jnp.logical_not(takes))
    def _():
        for kind in range(2):
            held[1 - ty, kind] = jnp.zeros((4, 2, 8, W), f32)

    @pl.when(tx == 3)
    def _():
        for core in range(2):
            held[core, 1, :, :, :, 0:128] = nothing

    @pl.when(tx == 0)
    def _():
        for core in range(2):
            held[core, 1, :, :, :, 128:256] = nothing


def row_swap(row_start, zh):
    ty, tx, pos, y, _, x = coordinates()
    row = y * 64 + zh * 32 + x * 8 + lax.broadcasted_iota(jnp.int32, (8, W), 0)
    return ((row < MARGIN) & (row_start > row + MARGIN)) | ((row >= 192) & (row > row_start + 191))


def column_swap(column_start):
    column = lax.broadcasted_iota(jnp.int32, (8, W), 1)
    return ((column < MARGIN) & (column_start > column + MARGIN)) | (
        (column >= 192) & (column > column_start + 191)
    )


def far_copy(j, piece, rows, turned, blocks, window, send_sem, recv_sem):
    ty, tx, pos, y, zh, x = coordinates()
    t = ((turned_row(y, turned) % 2) * 4 + x + j) % 8
    layers = pl.ds(2 * piece, 2)
    if rows is None:
        source, target = blocks.at[piece, j], window.at[layers, pl.ds(2 * y, 2), x]
    else:
        source, target = blocks.at[piece, j, :, rows], window.at[layers, 2 * y + rows, x]
    return pltpu.make_async_remote_copy(
        src_ref=source,
        dst_ref=target,
        send_sem=send_sem.at[piece, j],
        recv_sem=recv_sem.at[piece, y * 4 + x],
        device_id=peer(ty, tx, position(turned_row(t // 4, turned), zh, t % 4)),
        device_id_type=MESH,
    )


def far_start(piece, half, turned, offsets, held, *far):
    ty, tx, pos, y, zh, x = coordinates()
    blocks, window = far[:2]
    rows = 1 - zh if half else zh
    slot_row = turned_row(y, turned)
    for j in range(8):
        t = ((slot_row % 2) * 4 + x + j) % 8
        target = position(t // 4, zh, t % 4)
        swap_rows = row_swap(offsets[0, target], rows)
        swap_columns = column_swap(offsets[1, target])
        for part in range(2):
            layer = 2 * piece + part
            own = jnp.where(swap_columns, held[ty, 1, layer, rows], held[ty, 0, layer, rows])
            sibling = jnp.where(swap_columns, held[1 - ty, 1, layer, rows], held[1 - ty, 0, layer, rows])
            blocks[piece, j, part, rows] = jnp.where(swap_rows, sibling, own)
        if j == 0:

            @pl.when(slot_row >= 2)
            def _():
                far_copy(0, piece, rows, turned, *far).start()

            @pl.when(slot_row < 2)
            def _():
                for part in range(2):
                    window[2 * piece + part, 2 * y + rows, x] = blocks[piece, 0, part, rows]

        else:
            far_copy(j, piece, rows, turned, *far).start()


def far_wait(piece, blocks, window, send_sem, recv_sem):
    ty, tx, pos, y, zh, x = coordinates()

    def arrive(j, carry):
        s = (y * 4 + x + j) % 16
        pltpu.make_async_remote_copy(
            src_ref=blocks.at[piece, 0],
            dst_ref=window.at[pl.ds(2 * piece, 2), pl.ds(2 * (s // 4), 2), s % 4],
            send_sem=send_sem.at[piece, 0],
            recv_sem=recv_sem.at[piece, s],
            device_id=peer(ty, tx, position(s // 4, zh, s % 4)),
            device_id_type=MESH,
        ).wait_recv()
        return carry

    lax.fori_loop(1, 16, arrive, 0)


def far_drain(piece, turned, *far):
    ty, tx, pos, y, zh, x = coordinates()

    @pl.when(turned_row(y, turned) >= 2)
    def _():
        far_copy(0, piece, None, turned, *far).wait_send()

    for j in range(1, 8):
        far_copy(j, piece, None, turned, *far).wait_send()


def chosen_rows(half):
    zh = coordinates()[4]
    return 1 - zh if half else zh


def return_copy(j, piece, half, gradient, arrived, send_sem, recv_sem):
    ty, tx, pos, y, zh, x = coordinates()
    t = (y * 4 + x + j) % 16
    slot = (turned_row(y, ty) % 2) * 4 + x
    layers = pl.ds(2 * piece, 2)
    if half is None:
        source, target = gradient.at[layers, pl.ds(2 * (t // 4), 2), t % 4], arrived.at[piece, slot]
    else:
        rows = chosen_rows(half)
        source, target = gradient.at[layers, 2 * (t // 4) + rows, t % 4], arrived.at[piece, slot, :, rows]
    return pltpu.make_async_remote_copy(
        src_ref=source,
        dst_ref=target,
        send_sem=send_sem.at[piece, j],
        recv_sem=recv_sem.at[piece, half or 0, slot],
        device_id=peer(ty, tx, position(t // 4, zh, t % 4)),
        device_id_type=MESH,
    )


def return_start(piece, half, gradient, arrived, send_sem, recv_sem):
    ty, tx, pos, y, zh, x = coordinates()
    slot = (turned_row(y, ty) % 2) * 4 + x

    def leave(j, carry):
        return_copy(j, piece, half, gradient, arrived, send_sem, recv_sem).start()
        return carry

    lax.fori_loop(1, 16, leave, 0)
    for part in range(2):
        if half is None:
            arrived[piece, slot, part] = gradient[2 * piece + part, pl.ds(2 * y, 2), x]
        else:
            rows = chosen_rows(half)
            arrived[piece, slot, part, rows] = gradient[2 * piece + part, 2 * y + rows, x]


def return_wait(piece, half, gradient, arrived, send_sem, recv_sem):
    ty, tx, pos, y, zh, x = coordinates()
    slot_row = turned_row(y, ty)
    base = (slot_row % 2) * 4 + x
    layers = pl.ds(2 * piece, 2)

    def wait_for(s):
        if half is None:
            source, target = gradient.at[layers, pl.ds(0, 2), 0], arrived.at[piece, s]
        else:
            source, target = gradient.at[layers, 0, 0], arrived.at[piece, s, :, chosen_rows(half)]
        pltpu.make_async_remote_copy(
            src_ref=source,
            dst_ref=target,
            send_sem=send_sem.at[piece, 0],
            recv_sem=recv_sem.at[piece, half or 0, s],
            device_id=peer(ty, tx, position(turned_row(s // 4, ty), zh, s % 4)),
            device_id_type=MESH,
        ).wait_recv()

    @pl.when(slot_row >= 2)
    def _():
        wait_for(base)

    for j in range(1, 8):
        wait_for((base + j) % 8)


def return_drain(piece, gradient, arrived, send_sem, recv_sem):
    def left(j, carry):
        return_copy(j, piece, None, gradient, arrived, send_sem, recv_sem).wait_send()
        return carry

    lax.fori_loop(1, 16, left, 0)


def add_returned(piece, half, offsets, arrived, sums):
    ty, tx, pos, y, zh, x = coordinates()
    rows = chosen_rows(half)
    totals = [[jnp.zeros((8, W), f32)] * 4 for _ in range(2)]
    for j in range(8):
        target = position(j // 4, zh, j % 4)
        swap_rows = row_swap(offsets[0, target], rows)
        swap_columns = column_swap(offsets[1, target])
        for part in range(2):
            block = arrived[piece, j, part, rows]
            mine = jnp.where(swap_rows, 0.0, block)
            theirs = jnp.where(swap_rows, block, 0.0)
            own, own_side, sibling, sibling_side = totals[part]
            totals[part] = [
                own + jnp.where(swap_columns, 0.0, mine),
                own_side + jnp.where(swap_columns, mine, 0.0),
                sibling + jnp.where(swap_columns, 0.0, theirs),
                sibling_side + jnp.where(swap_columns, theirs, 0.0),
            ]
    for part in range(2):
        layer = 2 * piece + part
        sums[ty, 0, layer, rows] = totals[part][0]
        sums[ty, 1, layer, rows] = totals[part][1]
        sums[1 - ty, 0, layer, rows] = totals[part][2]
        sums[1 - ty, 1, layer, rows] = totals[part][3]


def sum_copy(index, role, piece, sums, parts_own, parts_side, send_sem, recv_sem):
    s, h, k = role
    layers = pl.ds(2 * piece, 2)
    other_ty, other_tx, other_zh, other_pos = close_peer(role, False)
    if k == 0:
        source, target = sums.at[other_ty, 0, layers, other_zh], parts_own.at[2 * s + h, layers]
    else:
        lanes = pl.ds(128 * (k - 1), 128)
        source = sums.at[other_ty, 1, layers, other_zh, :, lanes]
        target = parts_side.at[2 * s + h, layers, :, lanes]
    return pltpu.make_async_remote_copy(
        src_ref=source,
        dst_ref=target,
        send_sem=send_sem.at[piece, index],
        recv_sem=recv_sem.at[piece, index],
        device_id=peer(other_ty, other_tx, other_pos),
        device_id_type=MESH,
    )


def sum_each(piece, action, half, *refs):
    ty, tx, pos, y, zh, x = coordinates()
    takes, gives = sibling_facts()
    for index, role in enumerate(ROLES):
        if half not in (None, role[1]):
            continue
        copy = sum_copy(index, role, piece, *refs)
        if action == "recv":
            when(has_role(role, gives, tx > 0, tx < 3), copy.wait_recv)
        else:
            act = copy.start if action == "start" else copy.wait_send
            when(has_role(role, takes, tx < 3, tx > 0), act)


def clear_parts(parts_own, parts_side):
    ty, tx, pos, y, zh, x = coordinates()
    takes, gives = sibling_facts()
    nothing = jnp.zeros((4, 8, 128), f32)

    @pl.when(jnp.logical_not(gives))
    def _():
        for part in (2, 3):
            parts_own[part] = jnp.zeros((4, 8, W), f32)
            parts_side[part] = jnp.zeros((4, 8, W), f32)

    @pl.when(tx == 0)
    def _():
        for part in range(4):
            parts_side[part, :, :, 0:128] = nothing

    @pl.when(tx == 3)
    def _():
        for part in range(4):
            parts_side[part, :, :, 128:256] = nothing


def split(value):
    high = value.astype(bf16)
    return high, (value - high.astype(f32)).astype(bf16)


def product(left, right):
    return jnp.dot(left, right, preferred_element_type=f32)


def from_right(value, table):
    high, low = split(value)
    return product(high, table[0]) + product(low, table[0]) + product(high, table[1])


def from_left(table, value):
    high, low = split(value)
    return product(table[0], high) + product(table[0], low) + product(table[1], high)


def transform(real_part, imag_part, right, left):
    join = jnp.concatenate
    h = W // 2
    a, b, c, d = real_part[:, :h], real_part[:, h:], imag_part[:, :h], imag_part[:, h:]
    even = from_right(join([a + b, c + d], 1), right[0, 0])
    odd = from_right(join([a - b, c - d], 1), right[0, 1])
    real_part, imag_part = join([even[:, :h], odd[:, :h]], 1), join([even[:, h:], odd[:, h:]], 1)
    a, b, c, d = real_part[:h], real_part[h:], imag_part[:h], imag_part[h:]
    even = from_left(left[0, 0], join([a + b, c + d], 0))
    odd = from_left(left[0, 1], join([a - b, c - d], 0))
    return join([even[:h], odd[:h]], 0), join([even[h:], odd[h:]], 0)


def inverse(real_part, imag_part, right, left):
    join = jnp.concatenate
    h = W // 2
    even = from_right(join([real_part[:, :h], imag_part[:, :h]], 1), right[1, 0])
    odd = from_right(join([real_part[:, h:], imag_part[:, h:]], 1), right[1, 1])
    total, rest = even + odd, even - odd
    real_part, imag_part = join([total[:, :h], rest[:, :h]], 1), join([total[:, h:], rest[:, h:]], 1)
    even = from_left(left[1, 0], join([real_part[:h], imag_part[:h]], 0))
    odd = from_left(left[1, 1], join([real_part[h:], imag_part[h:]], 0))
    total, rest = even + odd, even - odd
    return join([total[:h], rest[:h]], 0), join([total[h:], rest[h:]], 0)


def parts_of(value, count):
    parts = []
    for _ in range(count):
        parts.append(value.astype(bf16))
        value = value - parts[-1].astype(f32)
    return parts


def reordered(value, first, second, count):
    value = sum(product(first, part) for part in parts_of(value, count))
    return sum(product(part, second) for part in parts_of(value, count))


def complex_product(first_real, first_imag, second_real, second_imag):
    return (
        first_real * second_real - first_imag * second_imag,
        first_real * second_imag + first_imag * second_real,
    )


def shifted_probe(offsets, slot, illumination):
    down = (offsets[0, slot] + 192) % 256
    across = (offsets[1, slot] + 192) % 256
    return [pltpu.roll(pltpu.roll(illumination[part], down, 0), across, 1) for part in range(2)]


def layer_of(window, layer):
    return window[layer].reshape(W, W)


def between_field(window, probe, slab, right, left):
    entering = complex_product(probe[0], probe[1], layer_of(window, 0), layer_of(window, 1))
    spectrum = transform(entering[0], entering[1], right, left)
    spectrum = complex_product(spectrum[0], spectrum[1], slab[0], slab[1])
    return inverse(spectrum[0], spectrum[1], right, left)


def farfield_of(between, window, right, left):
    leaving = complex_product(between[0], between[1], layer_of(window, 2), layer_of(window, 3))
    return transform(leaving[0], leaving[1], right, left)


def kernel(
    offsets_hbm,
    counts_hbm,
    rows_hbm,
    momentum_hbm,
    measured_hbm,
    illumination_hbm,
    phase_hbm,
    right_hbm,
    left_hbm,
    order_hbm,
    new_rows_out,
    new_momentum_out,
    amplitude,
    new_rows,
    new_momentum,
    offsets,
    counts,
    rows,
    momentum,
    measured,
    illumination,
    phase,
    right,
    left,
    order,
    ordered_measured,
    probe,
    slab,
    between_kept,
    held_first,
    held_second,
    blocks_first,
    blocks_second,
    window_first,
    window_second,
    gradient,
    arrived,
    sums,
    parts_own,
    parts_side,
    local_sem,
    measured_sem,
    store_sem,
    close_send_first,
    close_recv_first,
    close_send_second,
    close_recv_second,
    far_send_first,
    far_recv_first,
    far_send_second,
    far_recv_second,
    return_send,
    return_recv,
    sum_send,
    sum_recv,
):
    ty, tx, pos, y, zh, x = coordinates()
    loads = [
        pltpu.make_async_copy(source, target, local_sem.at[n])
        for n, (source, target) in enumerate(
            (
                (phase_hbm, phase),
                (illumination_hbm, illumination),
                (right_hbm, right),
                (order_hbm, order),
                (left_hbm, left),
                (measured_hbm, measured),
                (counts_hbm, counts),
                (rows_hbm, rows),
                (offsets_hbm, offsets),
                (momentum_hbm, momentum),
            )
        )
    ]
    loads, (counts_load, rows_load, offsets_load, momentum_load) = loads[:-4], loads[-4:]

    works = (y < 2) | (ty == 1)
    slot_row = jnp.where(y < 2, y, 3 - y)
    slot = position(slot_row, zh, x)

    def begin():
        rows_load.start()
        offsets_load.start()
        counts_load.start()
        momentum_load.start()

        @pl.when(works)
        def _():
            for load in loads:
                load.start()

        clear_missing(held_first)
        clear_missing(held_second)
        clear_parts(parts_own, parts_side)
        rows_load.wait()

    enter(begin)
    close_first = (rows, held_first, close_send_first, close_recv_first)
    close_second = (new_rows, held_second, close_send_second, close_recv_second)
    far_first = (blocks_first, window_first, far_send_first, far_recv_first)
    far_second = (blocks_second, window_second, far_send_second, far_recv_second)
    returned = (gradient, arrived, return_send, return_recv)
    summed = (sums, parts_own, parts_side, sum_send, sum_recv)
    for piece in (0, 1):
        close_start(piece, *close_first)
    offsets_load.wait()
    counts_load.wait()
    for piece in (0, 1):
        for half in (0, 1):
            close_wait(piece, half, *close_first)
            far_start(piece, half, ty, offsets, held_first, *far_first)
    live = jnp.where(slot < counts[0, 0], 1.0, 0.0)
    move_measured = pltpu.make_async_remote_copy(
        src_ref=ordered_measured,
        dst_ref=ordered_measured,
        send_sem=measured_sem.at[0],
        recv_sem=measured_sem.at[1],
        device_id=peer(ty, tx, position(3 - y, zh, x)),
        device_id_type=MESH,
    )

    @pl.when(works)
    def _():
        for load in loads:
            load.wait()

    @pl.when(y < 2)
    def _():
        ordered_measured[...] = reordered(measured[...], order[0], order[1], 3)

    @pl.when((y < 2) & (ty == 1))
    def _():
        move_measured.start()

    @pl.when(works)
    def _():
        angles = reordered(phase[...], order[0], order[1], 3)
        slab[0] = jnp.cos(angles)
        slab[1] = jnp.sin(angles)
        shifted = shifted_probe(offsets, slot, illumination)
        probe[0] = shifted[0]
        probe[1] = shifted[1]

    @pl.when(turned_row(y, ty) < 2)
    def _():
        far_wait(0, *far_first)
        between = between_field(window_first, probe, slab, right, left)
        between_kept[0] = between[0]
        between_kept[1] = between[1]
        far_wait(1, *far_first)
        farfield = farfield_of(between, window_first, right, left)
        magnitude = jnp.sqrt(farfield[0] * farfield[0] + farfield[1] * farfield[1])

        @pl.when(ty == 1)
        def _():
            move_measured.wait_recv()

        keeping = (1.0 - ordered_measured[...] / jnp.maximum(magnitude, magnitude_floor)) * live
        backward = inverse(farfield[0] * keeping, farfield[1] * keeping, right, left)
        grad_second = complex_product(between_kept[0], -between_kept[1], backward[0], backward[1])
        gradient[2] = grad_second[0].reshape(8, 4, 8, W)
        gradient[3] = grad_second[1].reshape(8, 4, 8, W)
        for half in (1, 0):
            return_start(1, half, *returned)
        toward = complex_product(layer_of(window_first, 2), -layer_of(window_first, 3), backward[0], backward[1])
        spectrum = transform(toward[0], toward[1], right, left)
        spectrum = complex_product(spectrum[0], spectrum[1], slab[0], -slab[1])
        incoming = inverse(spectrum[0], spectrum[1], right, left)
        grad_first = complex_product(probe[0], -probe[1], incoming[0], incoming[1])
        gradient[0] = grad_first[0].reshape(8, 4, 8, W)
        gradient[1] = grad_first[1].reshape(8, 4, 8, W)
        for half in (1, 0):
            return_start(0, half, *returned)

    for half in (1, 0):
        return_wait(1, half, *returned)
        add_returned(1, half, offsets, arrived, sums)
        sum_each(1, "start", half, *summed)
    for half in (1, 0):
        return_wait(0, half, *returned)
        add_returned(0, half, offsets, arrived, sums)
        sum_each(0, "start", half, *summed)
    momentum_load.wait()
    for piece in (1, 0):
        sum_each(piece, "recv", None, *summed)
        for layer in (2 * piece, 2 * piece + 1):
            total = sums[ty, 0, layer, zh]
            for part in range(4):
                if part:
                    total = total + parts_own[part, layer]
                total = total + parts_side[part, layer]
            velocity = momentum_rate * momentum[layer] + total
            new_momentum[layer] = velocity
            new_rows[layer] = rows[layer] - step_length * velocity
        close_start(piece, *close_second)
    stores = [
        pltpu.make_async_copy(new_rows, new_rows_out, store_sem.at[0]),
        pltpu.make_async_copy(new_momentum, new_momentum_out, store_sem.at[1]),
    ]
    for store in stores:
        store.start()
    for piece, half in ((1, 0), (0, 0), (0, 1), (1, 1)):
        close_wait(piece, half, *close_second)
        far_start(piece, half, 0, offsets, held_second, *far_second)

    @pl.when(y < 2)
    def _():
        far_wait(0, *far_second)
        between = between_field(window_second, probe, slab, right, left)
        far_wait(1, *far_second)
        farfield = farfield_of(between, window_second, right, left)
        magnitude = jnp.sqrt(farfield[0] * farfield[0] + farfield[1] * farfield[1]) * live
        amplitude[...] = reordered(magnitude, order[1], order[0], 2)

    @pl.when(y >= 2)
    def _():
        amplitude[...] = jnp.zeros_like(amplitude)

    for store in stores:
        store.wait()
    for piece in (0, 1):
        close_drain(piece, *close_first)
        close_drain(piece, *close_second)
        far_drain(piece, ty, *far_first)
        far_drain(piece, 0, *far_second)
        sum_each(piece, "sent", None, *summed)

    @pl.when(turned_row(y, ty) < 2)
    def _():
        for piece in (0, 1):
            return_drain(piece, *returned)

    @pl.when((y < 2) & (ty == 1))
    def _():
        move_measured.wait_send()


def hand_over(*refs):
    for source, target in zip(refs[:3], refs[3:]):
        target[...] = source[...]


def shards(object_field, momentum, measured, illumination, slab_phase, offsets, entry_counts):
    rows = object_field.reshape(4, 8, W)
    right, left, order = (jnp.asarray(t) for t in tables(W))
    dma = pltpu.SemaphoreType.DMA
    close = len(ROLES)
    window_shape = (4, 8, 4, 8, W)
    held_shape = (2, 2, 4, 2, 8, W)
    blocks_shape = (2, 8, 2, 2, 8, W)
    field = (2, W, W)
    vmem = pl.BlockSpec(memory_space=pltpu.VMEM)
    remain = pl.BlockSpec(memory_space=pl.ANY)
    shapes = (
        jax.ShapeDtypeStruct((4, 8, W), f32),
        jax.ShapeDtypeStruct((4, 8, W), f32),
        jax.ShapeDtypeStruct((W, W), f32),
    )
    results = pl.pallas_call(
        kernel,
        out_shape=shapes,
        in_specs=[remain] * 10,
        out_specs=[remain, remain, vmem],
        scratch_shapes=[
            pltpu.VMEM((4, 8, W), f32),
            pltpu.VMEM((4, 8, W), f32),
            pltpu.SMEM((2, offsets.shape[2]), jnp.int32),
            pltpu.SMEM((1, 1), jnp.int32),
            pltpu.VMEM((4, 8, W), f32),
            pltpu.VMEM((4, 8, W), f32),
            pltpu.VMEM((W, W), f32),
            pltpu.VMEM(field, f32),
            pltpu.VMEM((W, W), f32),
            pltpu.VMEM(right.shape, bf16),
            pltpu.VMEM(left.shape, bf16),
            pltpu.VMEM(order.shape, bf16),
            pltpu.VMEM((W, W), f32),
            pltpu.VMEM(field, f32),
            pltpu.VMEM(field, f32),
            pltpu.VMEM(field, f32),
            pltpu.VMEM(held_shape, f32),
            pltpu.VMEM(held_shape, f32),
            pltpu.VMEM(blocks_shape, f32),
            pltpu.VMEM(blocks_shape, f32),
            pltpu.VMEM(window_shape, f32),
            pltpu.VMEM(window_shape, f32),
            pltpu.VMEM(window_shape, f32),
            pltpu.VMEM(blocks_shape, f32),
            pltpu.VMEM(held_shape, f32),
            pltpu.VMEM((4, 4, 8, W), f32),
            pltpu.VMEM((4, 4, 8, W), f32),
            dma((10,)),
            dma((2,)),
            dma((2,)),
            dma((2, close)),
            dma((2, close)),
            dma((2, close)),
            dma((2, close)),
            dma((2, 8)),
            dma((2, 16)),
            dma((2, 8)),
            dma((2, 16)),
            dma((2, 16)),
            dma((2, 2, 8)),
            dma((2, close)),
            dma((2, close)),
        ],
        compiler_params=pltpu.CompilerParams(
            has_side_effects=True, vmem_limit_bytes=VMEM_LIMIT, collective_id=0
        ),
        name="iterate",
    )(
        offsets[0, 0].T,
        entry_counts,
        rows,
        momentum.reshape(4, 8, W),
        measured[0, 0, 0],
        illumination,
        slab_phase,
        right,
        left,
        order,
    )
    new_rows, new_momentum, amplitude = pl.pallas_call(
        hand_over,
        out_shape=shapes,
        in_specs=[vmem] * 3,
        out_specs=[vmem] * 3,
        compiler_params=pltpu.CompilerParams(vmem_limit_bytes=VMEM_LIMIT),
        name="hand_over",
    )(*results)
    return (
        new_rows.reshape(2, 2, 8, W),
        new_momentum.reshape(2, 2, 8, W),
        amplitude[None, None, None],
    )


def solution(mesh):
    rows = P(None, None, ("ty", "pos"), "tx")
    slots = P("ty", "tx", "pos", None, None)
    return jax.shard_map(
        shards,
        mesh=mesh,
        in_specs=(rows, rows, slots, P(), P(), P("ty", "tx", None, None), P("ty", "tx")),
        out_specs=(rows, rows, slots),
        check_vma=False,
    )
```

```python
import functools
import math

import jax
import jax.numpy as jnp
import numpy as np
from jax import lax
from jax.experimental import pallas as pl
from jax.experimental.pallas import tpu as pltpu
from jax.sharding import PartitionSpec as P

f32 = jnp.float32
bf16 = jnp.bfloat16
MESH = pl.DeviceIdType.MESH
magnitude_floor = 0.5
momentum_rate = 0.9
step_length = 0.05
W = 256
MARGIN = 64
ROLES = [(s, h, k) for s in range(2) for h in range(2) for k in range(3) if (s, h, k) != (0, 0, 0)]
VMEM_LIMIT = 60 * 1024 * 1024


def tables(length):
    half = length // 2
    place = np.arange(half)

    def halves(value):
        value = value.astype(np.float32)
        high = value.astype(jnp.bfloat16)
        low = (value - high.astype(np.float32)).astype(jnp.bfloat16)
        return np.stack([high, low])

    right = []
    for direction in (-1.0, 1.0):
        for odd in (0, 1):
            turns = (place[:, None] * (2 * place[None, :] + odd)) % length
            if direction > 0:
                turns = turns.T
            angles = turns * (direction * 2.0 * math.pi / length)
            c = np.cos(angles) / math.sqrt(length)
            s = np.sin(angles) / math.sqrt(length)
            right.append(halves(np.block([[c, s], [-s, c]])))
    right = np.stack(right).reshape(2, 2, 2, length, length)
    left = right.swapaxes(3, 4)
    order = np.zeros((length, length))
    order[np.arange(length), np.concatenate([2 * place, 2 * place + 1])] = 1.0
    return right, np.ascontiguousarray(left), np.stack([order, order.T]).astype(jnp.bfloat16)


def coordinates():
    ty = lax.axis_index("ty")
    tx = lax.axis_index("tx")
    pos = lax.axis_index("pos")
    return ty, tx, pos, pos // 8, (pos // 4) % 2, pos % 4


def peer(ty, tx, pos):
    return {"ty": ty, "tx": tx, "pos": pos}


def position(y, zh, x):
    return y * 8 + zh * 4 + x


def close_peer(role, outward):
    s, h, k = role
    ty, tx, pos, y, zh, x = coordinates()
    step = (0, 3, 1)[k] if outward else (0, 1, 3)[k]
    other_ty = 1 - ty if s else ty
    other_zh = 1 - zh if h else zh
    return other_ty, (tx + step) % 4, other_zh, position(y, other_zh, x)


def has_role(role, y_pair, tx_lower, tx_upper):
    s, h, k = role
    terms = ([y_pair] if s else []) + [[], [tx_lower], [tx_upper]][k]
    return functools.reduce(jnp.logical_and, terms) if terms else None


def when(condition, body):
    if condition is None:
        body()
    else:
        pl.when(condition)(body)


def enter(clear):
    ty, tx, pos, y, zh, x = coordinates()
    barrier = pltpu.get_barrier_semaphore()
    outer = (y == 0) | (y == 3)
    for role in ROLES:
        other_ty, other_tx, _, other_pos = close_peer(role, True)

        def signal(other_ty=other_ty, other_tx=other_tx, other_pos=other_pos):
            pl.semaphore_signal(barrier, inc=1, device_id=peer(other_ty, other_tx, other_pos), device_id_type=MESH)

        when(has_role(role, outer, tx > 0, tx < 3), signal)
    near = jnp.where((tx == 0) | (tx == 3), 4, 6) * jnp.where(outer, 2, 1) - 1
    me = y * 4 + x
    small = (y % 2) * 4 + x

    def greet(start, count, modulus):
        def body(j, carry):
            t = (start + j) % modulus
            pl.semaphore_signal(
                barrier, inc=1, device_id=peer(ty, tx, position(t // 4, zh, t % 4)), device_id_type=MESH
            )
            return carry

        lax.fori_loop(0, count, body, 0)

    everyone = (y < 2) | (ty == 1)

    @pl.when(everyone)
    def _():
        greet(me + 1, 15, 16)

    @pl.when(jnp.logical_not(everyone))
    def _():
        greet(small, 8, 8)

    clear()
    pl.semaphore_wait(barrier, near + jnp.where(everyone, 15, 8))


def turned_row(y, turned):
    return y + turned * (3 - 2 * y)


def sibling_facts():
    ty, tx, pos, y, zh, x = coordinates()
    takes = ((ty == 0) & (y == 0)) | ((ty == 1) & (y == 3))
    gives = ((ty == 1) & (y == 0)) | ((ty == 0) & (y == 3))
    return takes, gives


def close_copy(index, role, piece, src, held, send_sem, recv_sem):
    ty, tx, pos, y, zh, x = coordinates()
    k = role[2]
    layers = pl.ds(2 * piece, 2)
    other_ty, other_tx, _, other_pos = close_peer(role, True)
    if k == 0:
        source, target = src.at[layers], held.at[ty, 0, layers, zh]
    else:
        lanes = pl.ds(128 * (k - 1), 128)
        source, target = src.at[layers, :, lanes], held.at[ty, 1, layers, zh, :, lanes]
    return pltpu.make_async_remote_copy(
        src_ref=source,
        dst_ref=target,
        send_sem=send_sem.at[piece, index],
        recv_sem=recv_sem.at[piece, index],
        device_id=peer(other_ty, other_tx, other_pos),
        device_id_type=MESH,
    )


def close_start(piece, src, held, send_sem, recv_sem):
    ty, tx, pos, y, zh, x = coordinates()
    takes, gives = sibling_facts()
    for half in (1, 0):
        for index, role in enumerate(ROLES):
            if role[1] == half:
                copy = close_copy(index, role, piece, src, held, send_sem, recv_sem)
                when(has_role(role, gives, tx > 0, tx < 3), copy.start)
    for layer in (2 * piece, 2 * piece + 1):
        held[ty, 0, layer, zh] = src[layer]


def close_wait(piece, half, src, held, send_sem, recv_sem):
    ty, tx, pos, y, zh, x = coordinates()
    takes, gives = sibling_facts()
    for index, role in enumerate(ROLES):
        if role[1] != half:
            continue
        copy = close_copy(index, role, piece, src, held, send_sem, recv_sem)
        when(has_role(role, takes, tx < 3, tx > 0), copy.wait_recv)


def close_drain(piece, src, held, send_sem, recv_sem):
    ty, tx, pos, y, zh, x = coordinates()
    takes, gives = sibling_facts()
    for index, role in enumerate(ROLES):
        copy = close_copy(index, role, piece, src, held, send_sem, recv_sem)
        when(has_role(role, gives, tx > 0, tx < 3), copy.wait_send)


def clear_missing(held):
    ty, tx, pos, y, zh, x = coordinates()
    takes, gives = sibling_facts()
    nothing = jnp.zeros((4, 2, 8, 128), f32)

    @pl.when(jnp.logical_not(takes))
    def _():
        for kind in range(2):
            held[1 - ty, kind] = jnp.zeros((4, 2, 8, W), f32)

    @pl.when(tx == 3)
    def _():
        for core in range(2):
            held[core, 1, :, :, :, 0:128] = nothing

    @pl.when(tx == 0)
    def _():
        for core in range(2):
            held[core, 1, :, :, :, 128:256] = nothing


def row_swap(row_start, zh):
    ty, tx, pos, y, _, x = coordinates()
    row = y * 64 + zh * 32 + x * 8 + lax.broadcasted_iota(jnp.int32, (8, W), 0)
    return ((row < MARGIN) & (row_start > row + MARGIN)) | ((row >= 192) & (row > row_start + 191))


def column_swap(column_start):
    column = lax.broadcasted_iota(jnp.int32, (8, W), 1)
    return ((column < MARGIN) & (column_start > column + MARGIN)) | (
        (column >= 192) & (column > column_start + 191)
    )


def far_copy(j, piece, rows, turned, blocks, window, send_sem, recv_sem):
    ty, tx, pos, y, zh, x = coordinates()
    t = ((turned_row(y, turned) % 2) * 4 + x + j) % 8
    layers = pl.ds(2 * piece, 2)
    if rows is None:
        source, target = blocks.at[piece, j], window.at[layers, pl.ds(2 * y, 2), x]
    else:
        source, target = blocks.at[piece, j, :, rows], window.at[layers, 2 * y + rows, x]
    return pltpu.make_async_remote_copy(
        src_ref=source,
        dst_ref=target,
        send_sem=send_sem.at[piece, j],
        recv_sem=recv_sem.at[piece, y * 4 + x],
        device_id=peer(ty, tx, position(turned_row(t // 4, turned), zh, t % 4)),
        device_id_type=MESH,
    )


def far_start(piece, half, turned, offsets, held, *far):
    ty, tx, pos, y, zh, x = coordinates()
    blocks, window = far[:2]
    rows = 1 - zh if half else zh
    slot_row = turned_row(y, turned)
    for j in range(8):
        t = ((slot_row % 2) * 4 + x + j) % 8
        target = position(t // 4, zh, t % 4)
        swap_rows = row_swap(offsets[0, target], rows)
        swap_columns = column_swap(offsets[1, target])
        for part in range(2):
            layer = 2 * piece + part
            own = jnp.where(swap_columns, held[ty, 1, layer, rows], held[ty, 0, layer, rows])
            sibling = jnp.where(swap_columns, held[1 - ty, 1, layer, rows], held[1 - ty, 0, layer, rows])
            blocks[piece, j, part, rows] = jnp.where(swap_rows, sibling, own)
        if j == 0:

            @pl.when(slot_row >= 2)
            def _():
                far_copy(0, piece, rows, turned, *far).start()

            @pl.when(slot_row < 2)
            def _():
                for part in range(2):
                    window[2 * piece + part, 2 * y + rows, x] = blocks[piece, 0, part, rows]

        else:
            far_copy(j, piece, rows, turned, *far).start()


def far_wait(piece, blocks, window, send_sem, recv_sem):
    ty, tx, pos, y, zh, x = coordinates()

    def arrive(j, carry):
        s = (y * 4 + x + j) % 16
        pltpu.make_async_remote_copy(
            src_ref=blocks.at[piece, 0],
            dst_ref=window.at[pl.ds(2 * piece, 2), pl.ds(2 * (s // 4), 2), s % 4],
            send_sem=send_sem.at[piece, 0],
            recv_sem=recv_sem.at[piece, s],
            device_id=peer(ty, tx, position(s // 4, zh, s % 4)),
            device_id_type=MESH,
        ).wait_recv()
        return carry

    lax.fori_loop(1, 16, arrive, 0)


def far_drain(piece, turned, *far):
    ty, tx, pos, y, zh, x = coordinates()

    @pl.when(turned_row(y, turned) >= 2)
    def _():
        far_copy(0, piece, None, turned, *far).wait_send()

    for j in range(1, 8):
        far_copy(j, piece, None, turned, *far).wait_send()


def chosen_rows(half):
    zh = coordinates()[4]
    return 1 - zh if half else zh


def return_copy(j, piece, half, gradient, arrived, send_sem, recv_sem):
    ty, tx, pos, y, zh, x = coordinates()
    t = (y * 4 + x + j) % 16
    slot = (turned_row(y, ty) % 2) * 4 + x
    layers = pl.ds(2 * piece, 2)
    if half is None:
        source, target = gradient.at[layers, pl.ds(2 * (t // 4), 2), t % 4], arrived.at[piece, slot]
    else:
        rows = chosen_rows(half)
        source, target = gradient.at[layers, 2 * (t // 4) + rows, t % 4], arrived.at[piece, slot, :, rows]
    return pltpu.make_async_remote_copy(
        src_ref=source,
        dst_ref=target,
        send_sem=send_sem.at[piece, j],
        recv_sem=recv_sem.at[piece, half or 0, slot],
        device_id=peer(ty, tx, position(t // 4, zh, t % 4)),
        device_id_type=MESH,
    )


def return_start(piece, half, gradient, arrived, send_sem, recv_sem):
    ty, tx, pos, y, zh, x = coordinates()
    slot = (turned_row(y, ty) % 2) * 4 + x

    def leave(j, carry):
        return_copy(j, piece, half, gradient, arrived, send_sem, recv_sem).start()
        return carry

    lax.fori_loop(1, 16, leave, 0)
    for part in range(2):
        if half is None:
            arrived[piece, slot, part] = gradient[2 * piece + part, pl.ds(2 * y, 2), x]
        else:
            rows = chosen_rows(half)
            arrived[piece, slot, part, rows] = gradient[2 * piece + part, 2 * y + rows, x]


def return_wait(piece, half, gradient, arrived, send_sem, recv_sem):
    ty, tx, pos, y, zh, x = coordinates()
    slot_row = turned_row(y, ty)
    base = (slot_row % 2) * 4 + x
    layers = pl.ds(2 * piece, 2)

    def wait_for(s):
        if half is None:
            source, target = gradient.at[layers, pl.ds(0, 2), 0], arrived.at[piece, s]
        else:
            source, target = gradient.at[layers, 0, 0], arrived.at[piece, s, :, chosen_rows(half)]
        pltpu.make_async_remote_copy(
            src_ref=source,
            dst_ref=target,
            send_sem=send_sem.at[piece, 0],
            recv_sem=recv_sem.at[piece, half or 0, s],
            device_id=peer(ty, tx, position(turned_row(s // 4, ty), zh, s % 4)),
            device_id_type=MESH,
        ).wait_recv()

    @pl.when(slot_row >= 2)
    def _():
        wait_for(base)

    for j in range(1, 8):
        wait_for((base + j) % 8)


def return_drain(piece, gradient, arrived, send_sem, recv_sem):
    def left(j, carry):
        return_copy(j, piece, None, gradient, arrived, send_sem, recv_sem).wait_send()
        return carry

    lax.fori_loop(1, 16, left, 0)


def add_returned(piece, half, offsets, arrived, sums):
    ty, tx, pos, y, zh, x = coordinates()
    rows = chosen_rows(half)
    totals = [[jnp.zeros((8, W), f32)] * 4 for _ in range(2)]
    for j in range(8):
        target = position(j // 4, zh, j % 4)
        swap_rows = row_swap(offsets[0, target], rows)
        swap_columns = column_swap(offsets[1, target])
        for part in range(2):
            block = arrived[piece, j, part, rows]
            mine = jnp.where(swap_rows, 0.0, block)
            theirs = jnp.where(swap_rows, block, 0.0)
            own, own_side, sibling, sibling_side = totals[part]
            totals[part] = [
                own + jnp.where(swap_columns, 0.0, mine),
                own_side + jnp.where(swap_columns, mine, 0.0),
                sibling + jnp.where(swap_columns, 0.0, theirs),
                sibling_side + jnp.where(swap_columns, theirs, 0.0),
            ]
    for part in range(2):
        layer = 2 * piece + part
        sums[ty, 0, layer, rows] = totals[part][0]
        sums[ty, 1, layer, rows] = totals[part][1]
        sums[1 - ty, 0, layer, rows] = totals[part][2]
        sums[1 - ty, 1, layer, rows] = totals[part][3]


def sum_copy(index, role, piece, sums, parts_own, parts_side, send_sem, recv_sem):
    s, h, k = role
    layers = pl.ds(2 * piece, 2)
    other_ty, other_tx, other_zh, other_pos = close_peer(role, False)
    if k == 0:
        source, target = sums.at[other_ty, 0, layers, other_zh], parts_own.at[2 * s + h, layers]
    else:
        lanes = pl.ds(128 * (k - 1), 128)
        source = sums.at[other_ty, 1, layers, other_zh, :, lanes]
        target = parts_side.at[2 * s + h, layers, :, lanes]
    return pltpu.make_async_remote_copy(
        src_ref=source,
        dst_ref=target,
        send_sem=send_sem.at[piece, index],
        recv_sem=recv_sem.at[piece, index],
        device_id=peer(other_ty, other_tx, other_pos),
        device_id_type=MESH,
    )


def sum_each(piece, action, half, *refs):
    ty, tx, pos, y, zh, x = coordinates()
    takes, gives = sibling_facts()
    for index, role in enumerate(ROLES):
        if half not in (None, role[1]):
            continue
        copy = sum_copy(index, role, piece, *refs)
        if action == "recv":
            when(has_role(role, gives, tx > 0, tx < 3), copy.wait_recv)
        else:
            act = copy.start if action == "start" else copy.wait_send
            when(has_role(role, takes, tx < 3, tx > 0), act)


def clear_parts(parts_own, parts_side):
    ty, tx, pos, y, zh, x = coordinates()
    takes, gives = sibling_facts()
    nothing = jnp.zeros((4, 8, 128), f32)

    @pl.when(jnp.logical_not(gives))
    def _():
        for part in (2, 3):
            parts_own[part] = jnp.zeros((4, 8, W), f32)
            parts_side[part] = jnp.zeros((4, 8, W), f32)

    @pl.when(tx == 0)
    def _():
        for part in range(4):
            parts_side[part, :, :, 0:128] = nothing

    @pl.when(tx == 3)
    def _():
        for part in range(4):
            parts_side[part, :, :, 128:256] = nothing


def split(value):
    high = value.astype(bf16)
    return high, (value - high.astype(f32)).astype(bf16)


def product(left, right):
    return jnp.dot(left, right, preferred_element_type=f32)


def from_right(value, table):
    high, low = split(value)
    return product(high, table[0]) + product(low, table[0]) + product(high, table[1])


def from_left(table, value):
    high, low = split(value)
    return product(table[0], high) + product(table[0], low) + product(table[1], high)


def transform(real_part, imag_part, right, left):
    join = jnp.concatenate
    h = W // 2
    a, b, c, d = real_part[:, :h], real_part[:, h:], imag_part[:, :h], imag_part[:, h:]
    even = from_right(join([a + b, c + d], 1), right[0, 0])
    odd = from_right(join([a - b, c - d], 1), right[0, 1])
    real_part, imag_part = join([even[:, :h], odd[:, :h]], 1), join([even[:, h:], odd[:, h:]], 1)
    a, b, c, d = real_part[:h], real_part[h:], imag_part[:h], imag_part[h:]
    even = from_left(left[0, 0], join([a + b, c + d], 0))
    odd = from_left(left[0, 1], join([a - b, c - d], 0))
    return join([even[:h], odd[:h]], 0), join([even[h:], odd[h:]], 0)


def inverse(real_part, imag_part, right, left):
    join = jnp.concatenate
    h = W // 2
    even = from_right(join([real_part[:, :h], imag_part[:, :h]], 1), right[1, 0])
    odd = from_right(join([real_part[:, h:], imag_part[:, h:]], 1), right[1, 1])
    total, rest = even + odd, even - odd
    real_part, imag_part = join([total[:, :h], rest[:, :h]], 1), join([total[:, h:], rest[:, h:]], 1)
    even = from_left(left[1, 0], join([real_part[:h], imag_part[:h]], 0))
    odd = from_left(left[1, 1], join([real_part[h:], imag_part[h:]], 0))
    total, rest = even + odd, even - odd
    return join([total[:h], rest[:h]], 0), join([total[h:], rest[h:]], 0)


def parts_of(value, count):
    parts = []
    for _ in range(count):
        parts.append(value.astype(bf16))
        value = value - parts[-1].astype(f32)
    return parts


def reordered(value, first, second, count):
    value = sum(product(first, part) for part in parts_of(value, count))
    return sum(product(part, second) for part in parts_of(value, count))


def complex_product(first_real, first_imag, second_real, second_imag):
    return (
        first_real * second_real - first_imag * second_imag,
        first_real * second_imag + first_imag * second_real,
    )


def shifted_probe(offsets, slot, illumination):
    down = (offsets[0, slot] + 192) % 256
    across = (offsets[1, slot] + 192) % 256
    return [pltpu.roll(pltpu.roll(illumination[part], down, 0), across, 1) for part in range(2)]


def layer_of(window, layer):
    return window[layer].reshape(W, W)


def between_field(window, probe, slab, right, left):
    entering = complex_product(probe[0], probe[1], layer_of(window, 0), layer_of(window, 1))
    spectrum = transform(entering[0], entering[1], right, left)
    spectrum = complex_product(spectrum[0], spectrum[1], slab[0], slab[1])
    return inverse(spectrum[0], spectrum[1], right, left)


def farfield_of(between, window, right, left):
    leaving = complex_product(between[0], between[1], layer_of(window, 2), layer_of(window, 3))
    return transform(leaving[0], leaving[1], right, left)


def kernel(
    offsets_hbm,
    counts_hbm,
    rows_hbm,
    momentum_hbm,
    measured_hbm,
    illumination_hbm,
    phase_hbm,
    right_hbm,
    left_hbm,
    order_hbm,
    new_rows_out,
    new_momentum_out,
    amplitude,
    new_rows,
    new_momentum,
    offsets,
    counts,
    rows,
    momentum,
    measured,
    illumination,
    phase,
    right,
    left,
    order,
    ordered_measured,
    probe,
    slab,
    between_kept,
    held_first,
    held_second,
    blocks_first,
    blocks_second,
    window_first,
    window_second,
    gradient,
    arrived,
    sums,
    parts_own,
    parts_side,
    local_sem,
    measured_sem,
    store_sem,
    close_send_first,
    close_recv_first,
    close_send_second,
    close_recv_second,
    far_send_first,
    far_recv_first,
    far_send_second,
    far_recv_second,
    return_send,
    return_recv,
    sum_send,
    sum_recv,
):
    ty, tx, pos, y, zh, x = coordinates()
    loads = [
        pltpu.make_async_copy(source, target, local_sem.at[n])
        for n, (source, target) in enumerate(
            (
                (phase_hbm, phase),
                (illumination_hbm, illumination),
                (right_hbm, right),
                (order_hbm, order),
                (left_hbm, left),
                (measured_hbm, measured),
                (counts_hbm, counts),
                (rows_hbm, rows),
                (offsets_hbm, offsets),
                (momentum_hbm, momentum),
            )
        )
    ]
    loads, (counts_load, rows_load, offsets_load, momentum_load) = loads[:-4], loads[-4:]

    works = (y < 2) | (ty == 1)
    slot_row = jnp.where(y < 2, y, 3 - y)
    slot = position(slot_row, zh, x)

    def begin():
        rows_load.start()
        offsets_load.start()
        counts_load.start()
        momentum_load.start()

        @pl.when(works)
        def _():
            for load in loads:
                load.start()

        clear_missing(held_first)
        clear_missing(held_second)
        clear_parts(parts_own, parts_side)
        rows_load.wait()

    enter(begin)
    close_first = (rows, held_first, close_send_first, close_recv_first)
    close_second = (new_rows, held_second, close_send_second, close_recv_second)
    far_first = (blocks_first, window_first, far_send_first, far_recv_first)
    far_second = (blocks_second, window_second, far_send_second, far_recv_second)
    returned = (gradient, arrived, return_send, return_recv)
    summed = (sums, parts_own, parts_side, sum_send, sum_recv)
    for piece in (0, 1):
        close_start(piece, *close_first)
    offsets_load.wait()
    counts_load.wait()
    for piece in (0, 1):
        for half in (0, 1):
            close_wait(piece, half, *close_first)
            far_start(piece, half, ty, offsets, held_first, *far_first)
    live = jnp.where(slot < counts[0, 0], 1.0, 0.0)
    move_measured = pltpu.make_async_remote_copy(
        src_ref=ordered_measured,
        dst_ref=ordered_measured,
        send_sem=measured_sem.at[0],
        recv_sem=measured_sem.at[1],
        device_id=peer(ty, tx, position(3 - y, zh, x)),
        device_id_type=MESH,
    )

    @pl.when(works)
    def _():
        for load in loads:
            load.wait()

    @pl.when(y < 2)
    def _():
        ordered_measured[...] = reordered(measured[...], order[0], order[1], 3)

    @pl.when((y < 2) & (ty == 1))
    def _():
        move_measured.start()

    @pl.when(works)
    def _():
        angles = reordered(phase[...], order[0], order[1], 3)
        slab[0] = jnp.cos(angles)
        slab[1] = jnp.sin(angles)
        shifted = shifted_probe(offsets, slot, illumination)
        probe[0] = shifted[0]
        probe[1] = shifted[1]

    @pl.when(turned_row(y, ty) < 2)
    def _():
        far_wait(0, *far_first)
        between = between_field(window_first, probe, slab, right, left)
        between_kept[0] = between[0]
        between_kept[1] = between[1]
        far_wait(1, *far_first)
        farfield = farfield_of(between, window_first, right, left)
        magnitude = jnp.sqrt(farfield[0] * farfield[0] + farfield[1] * farfield[1])

        @pl.when(ty == 1)
        def _():
            move_measured.wait_recv()

        keeping = (1.0 - ordered_measured[...] / jnp.maximum(magnitude, magnitude_floor)) * live
        backward = inverse(farfield[0] * keeping, farfield[1] * keeping, right, left)
        grad_second = complex_product(between_kept[0], -between_kept[1], backward[0], backward[1])
        gradient[2] = grad_second[0].reshape(8, 4, 8, W)
        gradient[3] = grad_second[1].reshape(8, 4, 8, W)
        for half in (1, 0):
            return_start(1, half, *returned)
        toward = complex_product(layer_of(window_first, 2), -layer_of(window_first, 3), backward[0], backward[1])
        spectrum = transform(toward[0], toward[1], right, left)
        spectrum = complex_product(spectrum[0], spectrum[1], slab[0], -slab[1])
        incoming = inverse(spectrum[0], spectrum[1], right, left)
        grad_first = complex_product(probe[0], -probe[1], incoming[0], incoming[1])
        gradient[0] = grad_first[0].reshape(8, 4, 8, W)
        gradient[1] = grad_first[1].reshape(8, 4, 8, W)
        for half in (1, 0):
            return_start(0, half, *returned)

    for half in (1, 0):
        return_wait(1, half, *returned)
        add_returned(1, half, offsets, arrived, sums)
        sum_each(1, "start", half, *summed)
    for half in (1, 0):
        return_wait(0, half, *returned)
        add_returned(0, half, offsets, arrived, sums)
        sum_each(0, "start", half, *summed)
    momentum_load.wait()
    for piece in (1, 0):
        sum_each(piece, "recv", None, *summed)
        for layer in (2 * piece, 2 * piece + 1):
            total = sums[ty, 0, layer, zh]
            for part in range(4):
                if part:
                    total = total + parts_own[part, layer]
                total = total + parts_side[part, layer]
            velocity = momentum_rate * momentum[layer] + total
            new_momentum[layer] = velocity
            new_rows[layer] = rows[layer] - step_length * velocity
        close_start(piece, *close_second)
    stores = [
        pltpu.make_async_copy(new_rows, new_rows_out, store_sem.at[0]),
        pltpu.make_async_copy(new_momentum, new_momentum_out, store_sem.at[1]),
    ]
    for store in stores:
        store.start()
    for piece, half in ((1, 0), (0, 0), (0, 1), (1, 1)):
        close_wait(piece, half, *close_second)
        far_start(piece, half, 0, offsets, held_second, *far_second)

    for store in stores:
        store.wait()
    for piece in (0, 1):
        close_drain(piece, *close_first)
        close_drain(piece, *close_second)
        far_drain(piece, ty, *far_first)
        sum_each(piece, "sent", None, *summed)

    @pl.when(turned_row(y, ty) < 2)
    def _():
        for piece in (0, 1):
            return_drain(piece, *returned)

    @pl.when((y < 2) & (ty == 1))
    def _():
        move_measured.wait_send()

    @pl.when(y < 2)
    def _():
        far_wait(0, *far_second)
        between = between_field(window_second, probe, slab, right, left)
        far_wait(1, *far_second)
        farfield = farfield_of(between, window_second, right, left)
        magnitude = jnp.sqrt(farfield[0] * farfield[0] + farfield[1] * farfield[1]) * live
        amplitude[...] = reordered(magnitude, order[1], order[0], 2)

    @pl.when(y >= 2)
    def _():
        amplitude[...] = jnp.zeros_like(amplitude)

    for piece in (0, 1):
        far_drain(piece, 0, *far_second)


def hand_over(*refs):
    for source, target in zip(refs[:3], refs[3:]):
        target[...] = source[...]


def shards(object_field, momentum, measured, illumination, slab_phase, offsets, entry_counts):
    rows = object_field.reshape(4, 8, W)
    right, left, order = (jnp.asarray(t) for t in tables(W))
    dma = pltpu.SemaphoreType.DMA
    close = len(ROLES)
    window_shape = (4, 8, 4, 8, W)
    held_shape = (2, 2, 4, 2, 8, W)
    blocks_shape = (2, 8, 2, 2, 8, W)
    field = (2, W, W)
    vmem = pl.BlockSpec(memory_space=pltpu.VMEM)
    remain = pl.BlockSpec(memory_space=pl.ANY)
    shapes = (
        jax.ShapeDtypeStruct((4, 8, W), f32),
        jax.ShapeDtypeStruct((4, 8, W), f32),
        jax.ShapeDtypeStruct((W, W), f32),
    )
    results = pl.pallas_call(
        kernel,
        out_shape=shapes,
        in_specs=[remain] * 10,
        out_specs=[remain, remain, vmem],
        scratch_shapes=[
            pltpu.VMEM((4, 8, W), f32),
            pltpu.VMEM((4, 8, W), f32),
            pltpu.SMEM((2, offsets.shape[2]), jnp.int32),
            pltpu.SMEM((1, 1), jnp.int32),
            pltpu.VMEM((4, 8, W), f32),
            pltpu.VMEM((4, 8, W), f32),
            pltpu.VMEM((W, W), f32),
            pltpu.VMEM(field, f32),
            pltpu.VMEM((W, W), f32),
            pltpu.VMEM(right.shape, bf16),
            pltpu.VMEM(left.shape, bf16),
            pltpu.VMEM(order.shape, bf16),
            pltpu.VMEM((W, W), f32),
            pltpu.VMEM(field, f32),
            pltpu.VMEM(field, f32),
            pltpu.VMEM(field, f32),
            pltpu.VMEM(held_shape, f32),
            pltpu.VMEM(held_shape, f32),
            pltpu.VMEM(blocks_shape, f32),
            pltpu.VMEM(blocks_shape, f32),
            pltpu.VMEM(window_shape, f32),
            pltpu.VMEM(window_shape, f32),
            pltpu.VMEM(window_shape, f32),
            pltpu.VMEM(blocks_shape, f32),
            pltpu.VMEM(held_shape, f32),
            pltpu.VMEM((4, 4, 8, W), f32),
            pltpu.VMEM((4, 4, 8, W), f32),
            dma((10,)),
            dma((2,)),
            dma((2,)),
            dma((2, close)),
            dma((2, close)),
            dma((2, close)),
            dma((2, close)),
            dma((2, 8)),
            dma((2, 16)),
            dma((2, 8)),
            dma((2, 16)),
            dma((2, 16)),
            dma((2, 2, 8)),
            dma((2, close)),
            dma((2, close)),
        ],
        compiler_params=pltpu.CompilerParams(
            has_side_effects=True, vmem_limit_bytes=VMEM_LIMIT, collective_id=0
        ),
        name="iterate",
    )(
        offsets[0, 0].T,
        entry_counts,
        rows,
        momentum.reshape(4, 8, W),
        measured[0, 0, 0],
        illumination,
        slab_phase,
        right,
        left,
        order,
    )
    new_rows, new_momentum, amplitude = pl.pallas_call(
        hand_over,
        out_shape=shapes,
        in_specs=[vmem] * 3,
        out_specs=[vmem] * 3,
        compiler_params=pltpu.CompilerParams(vmem_limit_bytes=VMEM_LIMIT),
        name="hand_over",
    )(*results)
    return (
        new_rows.reshape(2, 2, 8, W),
        new_momentum.reshape(2, 2, 8, W),
        amplitude[None, None, None],
    )


def solution(mesh):
    rows = P(None, None, ("ty", "pos"), "tx")
    slots = P("ty", "tx", "pos", None, None)
    return jax.shard_map(
        shards,
        mesh=mesh,
        in_specs=(rows, rows, slots, P(), P(), P("ty", "tx", None, None), P("ty", "tx")),
        out_specs=(rows, rows, slots),
        check_vma=False,
    )
```
